32 devices in a mesh: gx: 4 (over z), gy: 8 (over y, x, core).
Axes of the slice: x: 2, y: 2, z: 4, core: 2. Of those that a mesh axis runs over, the one named last changes fastest.
Arguments:
- state: float32 [8, 2, 16, 4064], P(None, None, 'gx', 'gy'), may hold values from -1 to 5, as said below
- shear_offset: int32 [1], replicated, may hold values from 0 to 4063
- remap_shift: int32 [16], P('gx'), may hold values from 0 to 4063
- frac_index: int32 [16], P('gx'), may hold values from 0 to 15
Outputs:
- new_state: float32 [8, 2, 16, 4064], P(None, None, 'gx', 'gy')
The draws below stay inside these ranges and needn't reach their ends.
Inputs may be any that keep to these rules, and one draw needn't show every extreme that they name: `state`: field 0 lies in 0.5 to 2, fields 1 to 3 and 5 to 7 within 1 in magnitude, field 4 in 1 to 5.
All inputs are finite; a program needn't handle non-finite values.
Results may differ from the reference program's by a relative error of at most 0.00002.
Values sent between devices are 32-bit elements; how exact they have to be, the bound alone decides.
No kernel may reach another device: no remote copies, remote signals or barrier semaphores. Data moves between devices by JAX's collectives and lax.ppermute only.
A program may use at most 64 MiB of HBM per device.

```python
import jax
import jax.numpy as jnp
from jax import lax

FRAC = 16
NZ = 2
NX = 16
NY = 4064


def signed_values(key, shape, low, high):
    keys = jax.random.split(key, 2)
    magnitude = jax.random.uniform(keys[0], shape, jnp.float32, low, high)
    sign_bit = jax.random.bernoulli(keys[1], 0.5, shape)
    return jnp.where(sign_bit, magnitude, -magnitude)


def draw_state(key, part):
    keys = jax.random.split(jax.random.fold_in(key, 11), 4)
    shape = (NZ, NX, NY)
    density = jax.random.uniform(keys[0], shape, jnp.float32, 0.5, 0.6)
    momenta = signed_values(keys[1], (3,) + shape, 0.7, 1.0)
    fields = signed_values(keys[3], (3,) + shape, 0.7, 1.0)
    thermal = jax.random.uniform(keys[2], shape, jnp.float32, 0.2, 0.4)
    kinetic = 0.5 * jnp.sum(momenta * momenta, axis=0) / density
    energy = thermal + kinetic + 1.5
    return jnp.concatenate([density[None], momenta, energy[None], fields], axis=0)


def set_ends(result, stream_key, low, top_value):
    spot = [jax.random.randint(jax.random.fold_in(stream_key, axis), (), 0, length) for axis, length in enumerate(result.shape)]
    longest = result.shape.index(max(result.shape))
    next_to = spot[:longest] + [(spot[longest] + 1) % result.shape[longest]] + spot[longest + 1:]
    return result.at[tuple(spot)].set(low).at[tuple(next_to)].set(top_value)


def setup_inputs(seed: int = 0) -> dict:
    seeds = jax.random.split(jax.random.key(seed), 5)
    return {
        "state": draw_state(jax.random.fold_in(seeds[4], 71), 0),
        "shear_offset": jax.random.randint(seeds[1], (1,), 0, NY).astype(jnp.int32),
        "remap_shift": set_ends(jax.random.randint(seeds[2], (NX,), 0, NY), jax.random.fold_in(seeds[2], 1), 0, NY - 1).astype(jnp.int32),
        "frac_index": set_ends(jax.random.randint(seeds[3], (NX,), 0, FRAC), jax.random.fold_in(seeds[3], 1), 0, FRAC - 1).astype(jnp.int32),
    }


ADIABATIC = 5.0 / 3.0
ROTATION = 1.0
SHEAR_RATE = 1.5
MAX_SPEED = 5.0
TIME_STEP = 0.05


def next_cell(value, grid_axis):
    return jnp.roll(value, -1, grid_axis)


def prev_cell(value, grid_axis):
    return jnp.roll(value, 1, grid_axis)


def tendency(state):
    density, mom_x, mom_y, mom_z, energy, face_x, face_y, face_z = state
    cen_x = 0.5 * (face_x + next_cell(face_x, 1))
    cen_y = 0.5 * (face_y + next_cell(face_y, 2))
    cen_z = 0.5 * (face_z + next_cell(face_z, 0))
    vel_x = mom_x / density
    vel_y = mom_y / density
    vel_z = mom_z / density
    magnetic = 0.5 * (cen_x * cen_x + cen_y * cen_y + cen_z * cen_z)
    pressure = (ADIABATIC - 1.0) * (energy - 0.5 * (mom_x * vel_x + mom_y * vel_y + mom_z * vel_z) - magnetic) + magnetic
    vel_dot = vel_x * cen_x + vel_y * cen_y + vel_z * cen_z
    conserved = (density, mom_x, mom_y, mom_z, energy)
    momenta = (mom_x, mom_y, mom_z)
    centred = (cen_x, cen_y, cen_z)
    velocity = (vel_x, vel_y, vel_z)
    change = [jnp.zeros_like(density) for member in range(5)]
    for normal, grid_axis in ((0, 1), (1, 2), (2, 0)):
        normal_speed = velocity[normal]
        across = centred[normal]
        fluxes = [momenta[normal]]
        for second in range(3):
            flux_term = momenta[second] * normal_speed - across * centred[second]
            if second == normal:
                flux_term = flux_term + pressure
            fluxes.append(flux_term)
        fluxes.append((energy + pressure) * normal_speed - across * vel_dot)
        for member in range(5):
            upwind = 0.5 * (prev_cell(fluxes[member], grid_axis) + fluxes[member]) - 0.5 * MAX_SPEED * (conserved[member] - prev_cell(conserved[member], grid_axis))
            change[member] = change[member] - (next_cell(upwind, grid_axis) - upwind)
    change[1] = change[1] + 2.0 * ROTATION * mom_y
    change[2] = change[2] - (2.0 - SHEAR_RATE) * ROTATION * mom_x
    change[4] = change[4] + SHEAR_RATE * ROTATION * (mom_x * vel_y - cen_x * cen_y)
    elec_x = -(vel_y * cen_z - vel_z * cen_y)
    elec_y = -(vel_z * cen_x - vel_x * cen_z)
    elec_z = -(vel_x * cen_y - vel_y * cen_x)
    edge_x = 0.25 * (elec_x + prev_cell(elec_x, 2) + prev_cell(elec_x, 0) + prev_cell(prev_cell(elec_x, 2), 0))
    edge_y = 0.25 * (elec_y + prev_cell(elec_y, 1) + prev_cell(elec_y, 0) + prev_cell(prev_cell(elec_y, 1), 0))
    edge_z = 0.25 * (elec_z + prev_cell(elec_z, 1) + prev_cell(elec_z, 2) + prev_cell(prev_cell(elec_z, 1), 2))
    delta_x = -((next_cell(edge_z, 2) - edge_z) - (next_cell(edge_y, 0) - edge_y))
    delta_y = -((next_cell(edge_x, 0) - edge_x) - (next_cell(edge_z, 1) - edge_z))
    delta_z = -((next_cell(edge_y, 1) - edge_y) - (next_cell(edge_x, 2) - edge_x))
    return jnp.stack(change + [delta_x, delta_y, delta_z])


def pad_shear(state, offset, width):
    left_strip = jnp.roll(state[:, :, -width:, :], offset, axis=3)
    right_strip = jnp.roll(state[:, :, :width, :], -offset, axis=3)
    radial = jnp.concatenate([left_strip, state, right_strip], axis=2)
    return jnp.concatenate([radial[..., -width:], radial, radial[..., :width]], axis=3)


def reference(state, shear_offset, remap_shift, frac_index):
    offset = shear_offset[0]
    first = state + TIME_STEP * tendency(pad_shear(state, offset, 2))[:, :, 2:-2, 2:-2]
    advanced = 0.5 * (state + (first + TIME_STEP * tendency(pad_shear(first, offset, 2))[:, :, 2:-2, 2:-2]))
    fraction = (frac_index.astype(jnp.float32) + 0.5) / FRAC
    column = jnp.arange(NY, dtype=jnp.int32)
    source = (column[None, :] - remap_shift.astype(jnp.int32)[:, None]) % NY
    before = (source - 1) % NY

    def remap_field(field):
        here = jnp.take_along_axis(field, jnp.broadcast_to(source[None], field.shape), axis=2)
        there = jnp.take_along_axis(field, jnp.broadcast_to(before[None], field.shape), axis=2)
        return (1.0 - fraction)[None, :, None] * here + fraction[None, :, None] * there

    return lax.map(remap_field, advanced)
```

```python
import jax
import jax.numpy as jnp
from jax import lax
from jax.experimental import pallas as pl
from jax.experimental.pallas import tpu as pltpu
from jax.sharding import PartitionSpec as P

FRAC = 16

ADIABATIC = 5.0 / 3.0
ROTATION = 1.0
SHEAR_RATE = 1.5
MAX_SPEED = 5.0
TIME_STEP = 0.05

LANES = 128
FIELDS = 8
PLANES = 2
BELOW = 3
ABOVE = 3
SENT = 2
SLOT = FIELDS * PLANES * SENT
HALF_STEP = 0.5 * TIME_STEP
DIFFUSE = 0.5 * MAX_SPEED * TIME_STEP
EDGE = 0.25 * TIME_STEP


def lane_index(shape):
    return lax.broadcasted_iota(jnp.int32, shape, 1)


def row_index(shape):
    return lax.broadcasted_iota(jnp.int32, shape, 0)


def after(value):
    return pltpu.roll(value, LANES - 1, 1)


def before(value):
    return pltpu.roll(value, 1, 1)


def roll_tiles(tiles, amount):
    count = len(tiles)
    part = amount % LANES
    whole = amount // LANES
    turned = [pltpu.roll(tile, part, 1) for tile in tiles]
    low = lane_index(tiles[0].shape) < part
    tiles = [jnp.where(low, turned[i - 1], turned[i]) for i in range(count)]
    bit = 1
    while bit < count:
        tiles = [
            jnp.where((whole // bit) % 2 == 1, tiles[(i - bit) % count], tiles[i])
            for i in range(count)
        ]
        bit *= 2
    return tiles


def shift_cells(tiles, amount, cells):
    total = len(tiles) * LANES
    high = roll_tiles(tiles, amount)
    low = roll_tiles(tiles, (amount + total - cells) % total)
    lane = lane_index(tiles[0].shape)
    return [
        jnp.where(lane + i * LANES >= amount, high[i], low[i]) for i in range(len(tiles))
    ]


def shear_amounts(shear, cells, peers):
    total = cells * peers
    return shear, (total - shear) % total


def pack_kernel(cells, peers, chunk, shear_ref, state_ref, first_ref, second_ref):
    width = chunk + BELOW + ABOVE
    half = width // 2
    rows = state_ref.shape[2]
    place = lax.axis_index("gx")
    places = lax.axis_size("gx")
    lower, upper = shear_amounts(shear_ref[0], cells, peers)
    up_turn = jnp.where(place == places - 1, lower % cells, 0)
    down_turn = jnp.where(place == 0, upper % cells, 0)
    odd = place % 2
    own_first = odd * (peers * SLOT)
    own_second = (1 - odd) * (peers * SLOT)

    def stacked(pieces):
        return jnp.concatenate(pieces, axis=0)

    def tiles_of(value):
        spare = -cells % LANES
        pad = jnp.zeros((value.shape[0], spare), value.dtype)
        value = jnp.concatenate([value, pad], axis=1)
        return [value[:, i : i + LANES] for i in range(0, cells + spare, LANES)]

    def turned(value, amount):
        return jnp.concatenate(shift_cells(tiles_of(value), amount, cells), axis=1)[:, :cells]

    def windows(value):
        top = peers * chunk + ABOVE - cells
        wide = jnp.concatenate([value[:, cells - BELOW :], value, value[:, :top]], axis=1)
        return [wide[:, k * chunk : k * chunk + width] for k in range(peers)]

    per_group = 8 // SENT
    groups = FIELDS * PLANES // per_group
    for group in range(groups):
        members = range(group * per_group, (group + 1) * per_group)
        blocks = [state_ref[fz // PLANES, fz % PLANES] for fz in members]
        bottom = stacked([b[:SENT] for b in blocks])
        top = stacked([b[rows - SENT :] for b in blocks])
        to_up = windows(turned(top, up_turn))
        to_down = windows(turned(bottom, down_turn))
        if group == 0:
            faces = [state_ref[5, z][SENT : SENT + 1] for z in range(PLANES)]
            pieces = [faces[i // SENT] for i in range(PLANES * SENT)]
            faces = windows(turned(stacked(pieces * (8 // len(pieces))), down_turn))
            to_down = [
                jnp.concatenate(
                    [
                        value,
                        jnp.where(
                            row_index((8, half)) % SENT == 0, face[:, :half], face[:, half:]
                        ),
                    ],
                    axis=1,
                )
                for value, face in zip(to_down, faces)
            ]

        def put(ref, base, values):
            for k, value in enumerate(values):
                at = pl.multiple_of(base + (k * SLOT + group * 8), 8)
                ref[pl.ds(at, 8), 0 : value.shape[1]] = value

        put(first_ref, own_first, windows(bottom))
        put(second_ref, own_second, windows(top))

        @pl.when(odd == 0)
        def _():
            put(first_ref, own_second, to_up)
            put(second_ref, own_first, to_down)

        @pl.when(odd == 1)
        def _():
            put(first_ref, own_second, to_down)
            put(second_ref, own_first, to_up)


def cell_terms(state, next_face_x):
    planes = range(PLANES)
    face_z = state[7]
    out = []
    for z in planes:
        density, mom_x, mom_y, mom_z, energy, face_x, face_y = (state[f][z] for f in range(7))
        cen_x = 0.5 * (face_x + next_face_x[z])
        cen_y = 0.5 * (face_y + after(face_y))
        cen_z = 0.5 * (face_z[z] + face_z[(z + 1) % PLANES])
        inverse = 1.0 / density
        vel_x, vel_y, vel_z = (mom_x * inverse, mom_y * inverse, mom_z * inverse)
        magnetic = 0.5 * (cen_x * cen_x + cen_y * cen_y + cen_z * cen_z)
        kinetic = 0.5 * (mom_x * vel_x + mom_y * vel_y + mom_z * vel_z)
        pressure = (ADIABATIC - 1.0) * (energy - kinetic - magnetic) + magnetic
        vel_dot = vel_x * cen_x + vel_y * cen_y + vel_z * cen_z
        scaled_p = HALF_STEP * pressure
        total = energy + pressure
        sv_x, sv_y, sv_z = (HALF_STEP * vel_x, HALF_STEP * vel_y, HALF_STEP * vel_z)
        sb_x, sb_y, sb_z = (HALF_STEP * cen_x, HALF_STEP * cen_y, HALF_STEP * cen_z)
        xx = mom_x * sv_x - cen_x * sb_x + scaled_p
        yy = mom_y * sv_y - cen_y * sb_y + scaled_p
        zz = mom_z * sv_z - cen_z * sb_z + scaled_p
        xy = mom_x * sv_y - cen_x * sb_y
        xz = mom_x * sv_z - cen_x * sb_z
        yz = mom_y * sv_z - cen_y * sb_z
        diffuse = [DIFFUSE * state[f][z] for f in range(5)]
        flux_x = [HALF_STEP * mom_x, xx, xy, xz, total * sv_x - sb_x * vel_dot]
        flux_y = [HALF_STEP * mom_y, xy, yy, yz, total * sv_y - sb_y * vel_dot]
        flux_z = [HALF_STEP * mom_z, xz, yz, zz, total * sv_z - sb_z * vel_dot]
        out.append(
            dict(
                diffuse=diffuse,
                low_x=[f + d for f, d in zip(flux_x, diffuse)],
                high_x=[f - d for f, d in zip(flux_x, diffuse)],
                low_y=[f + d for f, d in zip(flux_y, diffuse)],
                high_y=[f - d for f, d in zip(flux_y, diffuse)],
                flux_z=flux_z,
                shear=xy,
                e_x=EDGE * (vel_z * cen_y - vel_y * cen_z),
                e_y=EDGE * (vel_x * cen_z - vel_z * cen_x),
                e_z=EDGE * (vel_y * cen_x - vel_x * cen_y),
            )
        )
    return out


def plane_sum(terms, name):
    total = terms[0][name]
    for z in range(1, PLANES):
        total = total + terms[z][name]
    return total


def face_x_change(here, low):
    edge_y = plane_sum(here, "e_y") + plane_sum(low, "e_y")
    edge_y = [edge_y] * PLANES
    out = []
    for z in range(PLANES):
        pair = here[z]["e_z"] + low[z]["e_z"]
        out.append((edge_y[(z + 1) % PLANES] - edge_y[z]) - (after(pair) - before(pair)))
    return out


def row_step(state, low, here, high):
    new = [[None] * PLANES for f in range(FIELDS)]
    faces = [
        [
            (here[z - 1]["flux_z"][f] + here[z]["flux_z"][f])
            - (here[z]["diffuse"][f] - here[z - 1]["diffuse"][f])
            for f in range(5)
        ]
        for z in range(PLANES)
    ]
    for z in range(PLANES):
        cell = here[z]
        for f in range(5):
            along_x = high[z]["high_x"][f] - low[z]["low_x"][f]
            along_y = after(cell["high_y"][f]) - before(cell["low_y"][f])
            along_z = faces[(z + 1) % PLANES][f] - faces[z][f]
            kept = state[f][z] - 4.0 * cell["diffuse"][f]
            new[f][z] = kept - (along_x + along_y + along_z)
        mom_x, mom_y = (state[1][z], state[2][z])
        new[1][z] = new[1][z] + (TIME_STEP * 2.0 * ROTATION) * mom_y
        new[2][z] = new[2][z] - (TIME_STEP * (2.0 - SHEAR_RATE) * ROTATION) * mom_x
        new[4][z] = new[4][z] + (2.0 * SHEAR_RATE * ROTATION) * cell["shear"]
    change_x = face_x_change(here, low)
    exz = plane_sum(here, "e_x")
    edge_x = [exz + before(exz)] * PLANES
    along_y = after(exz) - before(exz)
    along_x = plane_sum(high, "e_y") - plane_sum(low, "e_y")
    for z in range(PLANES):
        pair = here[z]["e_z"] + low[z]["e_z"]
        pair_up = high[z]["e_z"] + here[z]["e_z"]
        edge = pair + before(pair)
        edge_up = pair_up + before(pair_up)
        new[5][z] = state[5][z] + change_x[z]
        new[6][z] = state[6][z] + ((edge_up - edge) - (edge_x[(z + 1) % PLANES] - edge_x[z]))
        new[7][z] = state[7][z] + (along_y - along_x)
    return new


def step_kernel(
    cells, peers, chunk, rows,
    shear_ref, shift_ref, frac_ref, first_ref, second_ref,
    out_ref, state_ref, mid_ref,
):
    width = chunk + BELOW + ABOVE
    half = width // 2
    place = lax.axis_index("gx")
    places = lax.axis_size("gx")
    part = lax.axis_index("gy")
    odd = place % 2
    even = odd == 0
    shape = (peers, LANES)
    lane = lane_index(shape)
    lower, upper = shear_amounts(shear_ref[0], cells, peers)
    lower = jnp.where(place == 0, lower, 0)
    upper = jnp.where(place == places - 1, upper, 0)
    column = part * chunk - BELOW + lane

    def load(ref, position, row):
        return ref[pl.ds(position * (peers * SLOT) + row, peers, stride=SLOT), :]

    def turn(value, amount):
        return pltpu.roll(value, amount, 0)

    def strips(value, amount):
        hop = amount // cells
        source = column - amount % cells
        pick = turn(value, hop % peers)
        pick = jnp.where(source < 0, turn(value, (hop + 1) % peers), pick)
        pick = jnp.where(source < -cells, turn(value, (hop + 2) % peers), pick)
        return jnp.where(source >= cells, turn(value, (hop + peers - 1) % peers), pick)

    def own_strips(value):
        pick = jnp.where(column < 0, turn(value, 1), value)
        return jnp.where(column >= cells, turn(value, peers - 1), pick)

    for f in range(FIELDS):
        for z in range(PLANES):
            for g in range(SENT):
                at = (f * PLANES + z) * SENT + g
                first = [load(first_ref, p, at) for p in range(2)]
                second = [load(second_ref, p, at) for p in range(2)]
                own_low = jnp.where(even, first[0], first[1])
                own_high = jnp.where(even, second[1], second[0])
                from_first = jnp.where(even, first[1], first[0])
                from_second = jnp.where(even, second[0], second[1])
                ghost_low = jnp.where(even, from_second, from_first)
                ghost_high = jnp.where(even, from_first, from_second)
                state_ref[g, f, z] = strips(ghost_low, lower)
                state_ref[SENT + g, f, z] = own_strips(own_low)
                state_ref[rows + g, f, z] = own_strips(own_high)
                state_ref[SENT + rows + g, f, z] = strips(ghost_high, upper)
    face_high = []
    for z in range(PLANES):
        parts = []
        for g in range(SENT):
            at = z * SENT + g
            ghost = jnp.where(even, load(first_ref, 1, at), load(second_ref, 1, at))
            parts.append(pltpu.roll(ghost, LANES - width + g * half, 1))
        face_high.append(strips(jnp.where(lane < half, parts[0], parts[1]), upper))

    def row_of(ref, index):
        return [[ref[index, f, z] for z in range(PLANES)] for f in range(FIELDS)]

    def faces_of(ref, index):
        return [ref[index, 5, z] for z in range(PLANES)]

    count = rows + 2 * SENT
    low = cell_terms(row_of(state_ref, 0), faces_of(state_ref, 1))
    here = cell_terms(row_of(state_ref, 1), faces_of(state_ref, 2))
    for index in range(1, count - 1):
        beyond = face_high if index + 2 == count else faces_of(state_ref, index + 2)
        high = cell_terms(row_of(state_ref, index + 1), beyond)
        new = row_step(row_of(state_ref, index), low, here, high)
        for f in range(FIELDS):
            for z in range(PLANES):
                mid_ref[index - 1, f, z] = new[f][z]
        low, here = here, high
    change = face_x_change(here, low)
    mid_face = [state_ref[count - 1, 5, z] + change[z] for z in range(PLANES)]

    count = rows + 2
    low = cell_terms(row_of(mid_ref, 0), faces_of(mid_ref, 1))
    here = cell_terms(row_of(mid_ref, 1), faces_of(mid_ref, 2))
    for index in range(1, count - 1):
        beyond = mid_face if index + 2 == count else faces_of(mid_ref, index + 2)
        high = cell_terms(row_of(mid_ref, index + 1), beyond)
        new = row_step(row_of(mid_ref, index), low, here, high)
        row = index - 1
        shift = shift_ref[row]
        hop = shift // cells
        crossing = part * chunk + lane % chunk + shift % cells >= cells
        weight = (frac_ref[row].astype(jnp.float32) + 0.5) / FRAC
        for f in range(FIELDS):
            packed = None
            for z in range(PLANES):
                done = 0.5 * (state_ref[index + 1, f, z] + new[f][z])
                mixed = (1.0 - weight) * done + weight * before(done)
                moved = pltpu.roll(mixed, (z * chunk - BELOW) % LANES, 1)
                packed = moved if z == 0 else jnp.where(lane < z * chunk, packed, moved)
            sent = jnp.where(crossing, turn(packed, (hop + 1) % peers), turn(packed, hop % peers))
            out_ref[pl.ds(f * rows + row, peers, stride=FIELDS * rows), :] = sent
        low, here = here, high


def place_kernel(cells, peers, chunk, shift_ref, in_ref, out_ref):
    rows = out_ref.shape[2]
    block = FIELDS * rows
    per_group = 8 // rows
    amounts = [shift_ref[x] % cells for x in range(rows)]
    lanes = peers * chunk
    member = row_index((8, LANES)) % rows
    for group in range(FIELDS // per_group):
        pieces = [in_ref[k * block + group * 8 : k * block + group * 8 + 8, :] for k in range(peers)]
        for z in range(PLANES):
            joined = jnp.concatenate(
                [piece[:, z * chunk : (z + 1) * chunk] for piece in pieces], axis=1
            )
            tiles = [joined[:, i : i + LANES] for i in range(0, lanes, LANES)]
            result = shift_cells(tiles, amounts[0], cells)
            for x in range(1, rows):
                moved = shift_cells(tiles, amounts[x], cells)
                result = [jnp.where(member == x, m, r) for m, r in zip(moved, result)]
            result = jnp.concatenate(result, axis=1)[:, :cells]
            for g in range(per_group):
                out_ref[group * per_group + g, z] = result[g * rows : (g + 1) * rows]


def solution(mesh):
    places, peers = (mesh.shape["gx"], mesh.shape["gy"])

    def groups_from(start):
        return [
            [(start + pair + p) % places * peers + k for p in range(2) for k in range(peers)]
            for pair in range(0, places, 2)
        ]

    smem = pl.BlockSpec(memory_space=pltpu.SMEM)
    vmem = pl.BlockSpec(memory_space=pltpu.VMEM)

    def shards(state, shear_offset, remap_shift, frac_index):
        rows, cells = state.shape[2:]
        chunk = -(-cells // peers)
        message = jax.ShapeDtypeStruct((2 * peers * SLOT, LANES), jnp.float32)
        first, second = pl.pallas_call(
            lambda *refs: pack_kernel(cells, peers, chunk, *refs),
            out_shape=(message, message),
            in_specs=[smem, vmem],
            out_specs=(vmem, vmem),
            name="pack",
        )(shear_offset, state)
        axes = ("gx", "gy")
        first = lax.all_to_all(
            first, axes, 0, 0, axis_index_groups=groups_from(0), tiled=True
        )
        second = lax.all_to_all(
            second, axes, 0, 0, axis_index_groups=groups_from(1), tiled=True
        )
        block = FIELDS * rows
        moved = pl.pallas_call(
            lambda *refs: step_kernel(cells, peers, chunk, rows, *refs),
            out_shape=jax.ShapeDtypeStruct((peers * block, LANES), jnp.float32),
            in_specs=[smem, smem, smem, vmem, vmem],
            out_specs=vmem,
            scratch_shapes=[
                pltpu.VMEM((rows + 2 * SENT, FIELDS, PLANES, peers, LANES), jnp.float32),
                pltpu.VMEM((rows + 2, FIELDS, PLANES, peers, LANES), jnp.float32),
            ],
            name="step",
        )(shear_offset, remap_shift, frac_index, first, second)
        moved = lax.all_to_all(moved, "gy", 0, 0, tiled=True)
        return pl.pallas_call(
            lambda *refs: place_kernel(cells, peers, chunk, *refs),
            out_shape=jax.ShapeDtypeStruct(state.shape, jnp.float32),
            in_specs=[smem, vmem],
            out_specs=vmem,
            name="place",
        )(remap_shift, moved)

    placed = (P(None, None, "gx", "gy"), P(), P("gx"), P("gx"))
    return jax.shard_map(
        shards, mesh=mesh, in_specs=placed, out_specs=P(None, None, "gx", "gy"), check_vma=False
    )
```

```python
import jax
import jax.numpy as jnp
from jax import lax
from jax.experimental import pallas as pl
from jax.experimental.pallas import tpu as pltpu
from jax.sharding import PartitionSpec as P

FRAC = 16

ADIABATIC = 5.0 / 3.0
ROTATION = 1.0
SHEAR_RATE = 1.5
MAX_SPEED = 5.0
TIME_STEP = 0.05

LANES = 128
FIELDS = 8
PLANES = 2
BELOW = 3
ABOVE = 3
SENT = 2
SLOT = FIELDS * PLANES * SENT
HALF_STEP = 0.5 * TIME_STEP
DIFFUSE = 0.5 * MAX_SPEED * TIME_STEP
EDGE = 0.25 * TIME_STEP


def lane_index(shape):
    return lax.broadcasted_iota(jnp.int32, shape, 1)


def row_index(shape):
    return lax.broadcasted_iota(jnp.int32, shape, 0)


def after(value):
    return pltpu.roll(value, LANES - 1, 1)


def before(value):
    return pltpu.roll(value, 1, 1)


def roll_tiles(tiles, amount):
    count = len(tiles)
    part = amount % LANES
    whole = amount // LANES
    turned = [pltpu.roll(tile, part, 1) for tile in tiles]
    low = lane_index(tiles[0].shape) < part
    tiles = [jnp.where(low, turned[i - 1], turned[i]) for i in range(count)]
    bit = 1
    while bit < count:
        tiles = [
            jnp.where((whole // bit) % 2 == 1, tiles[(i - bit) % count], tiles[i])
            for i in range(count)
        ]
        bit *= 2
    return tiles


def shift_cells(tiles, amount, cells):
    total = len(tiles) * LANES
    high = roll_tiles(tiles, amount)
    low = roll_tiles(tiles, (amount + total - cells) % total)
    lane = lane_index(tiles[0].shape)
    return [
        jnp.where(lane + i * LANES >= amount, high[i], low[i]) for i in range(len(tiles))
    ]


def shear_amounts(shear, cells, peers):
    total = cells * peers
    return shear, (total - shear) % total


def pack_kernel(cells, peers, chunk, shear_ref, state_ref, *refs):
    up_refs, down_refs, own_refs = (refs[i * peers : (i + 1) * peers] for i in range(3))
    up_ref, down_ref, own_ref = refs[3 * peers :]
    width = chunk + BELOW + ABOVE
    half = width // 2
    rows = state_ref.shape[2]
    place = lax.axis_index("gx")
    places = lax.axis_size("gx")
    part = lax.axis_index("gy")
    lower, upper = shear_amounts(shear_ref[0], cells, peers)
    up_turn = jnp.where(place == places - 1, lower % cells, 0)
    down_turn = jnp.where(place == 0, upper % cells, 0)

    def stacked(pieces):
        return jnp.concatenate(pieces, axis=0)

    def tiles_of(value):
        spare = -cells % LANES
        pad = jnp.zeros((value.shape[0], spare), value.dtype)
        value = jnp.concatenate([value, pad], axis=1)
        return [value[:, i : i + LANES] for i in range(0, cells + spare, LANES)]

    def turned(value, amount):
        return jnp.concatenate(shift_cells(tiles_of(value), amount, cells), axis=1)[:, :cells]

    def windows(value):
        top = peers * chunk + ABOVE - cells
        wide = jnp.concatenate([value[:, cells - BELOW :], value, value[:, :top]], axis=1)
        return [wide[:, k * chunk : k * chunk + width] for k in range(peers)]

    def put(ref, row, values):
        for k, value in enumerate(values):
            ref[k, row : row + 8, 0 : value.shape[1]] = value

    per_group = 8 // SENT
    groups = FIELDS * PLANES // per_group
    for group in range(groups):
        members = range(group * per_group, (group + 1) * per_group)
        blocks = [state_ref[fz // PLANES, fz % PLANES] for fz in members]
        bottom = stacked([b[:SENT] for b in blocks])
        top = stacked([b[rows - SENT :] for b in blocks])
        to_down = windows(turned(bottom, down_turn))
        if group == 0:
            faces = [state_ref[5, z][SENT : SENT + 1] for z in range(PLANES)]
            pieces = [faces[i // SENT] for i in range(PLANES * SENT)]
            faces = windows(turned(stacked(pieces * (8 // len(pieces))), down_turn))
            to_down = [
                jnp.concatenate(
                    [
                        value,
                        jnp.where(
                            row_index((8, half)) % SENT == 0, face[:, :half], face[:, half:]
                        ),
                    ],
                    axis=1,
                )
                for value, face in zip(to_down, faces)
            ]
        put(up_ref, group * 8, windows(turned(top, up_turn)))
        put(down_ref, group * 8, to_down)
        put(own_ref, group * 8, windows(bottom))
        put(own_ref, SLOT + group * 8, windows(top))
    for d in range(peers):
        target = part ^ d
        up_refs[d][...] = up_ref[target]
        down_refs[d][...] = down_ref[target]
        own_refs[d][...] = own_ref[target]


def cell_terms(state, next_face_x):
    planes = range(PLANES)
    face_z = state[7]
    out = []
    for z in planes:
        density, mom_x, mom_y, mom_z, energy, face_x, face_y = (state[f][z] for f in range(7))
        cen_x = 0.5 * (face_x + next_face_x[z])
        cen_y = 0.5 * (face_y + after(face_y))
        cen_z = 0.5 * (face_z[z] + face_z[(z + 1) % PLANES])
        inverse = 1.0 / density
        vel_x, vel_y, vel_z = (mom_x * inverse, mom_y * inverse, mom_z * inverse)
        magnetic = 0.5 * (cen_x * cen_x + cen_y * cen_y + cen_z * cen_z)
        kinetic = 0.5 * (mom_x * vel_x + mom_y * vel_y + mom_z * vel_z)
        pressure = (ADIABATIC - 1.0) * (energy - kinetic - magnetic) + magnetic
        vel_dot = vel_x * cen_x + vel_y * cen_y + vel_z * cen_z
        scaled_p = HALF_STEP * pressure
        total = energy + pressure
        sv_x, sv_y, sv_z = (HALF_STEP * vel_x, HALF_STEP * vel_y, HALF_STEP * vel_z)
        sb_x, sb_y, sb_z = (HALF_STEP * cen_x, HALF_STEP * cen_y, HALF_STEP * cen_z)
        xx = mom_x * sv_x - cen_x * sb_x + scaled_p
        yy = mom_y * sv_y - cen_y * sb_y + scaled_p
        zz = mom_z * sv_z - cen_z * sb_z + scaled_p
        xy = mom_x * sv_y - cen_x * sb_y
        xz = mom_x * sv_z - cen_x * sb_z
        yz = mom_y * sv_z - cen_y * sb_z
        diffuse = [DIFFUSE * state[f][z] for f in range(5)]
        flux_x = [HALF_STEP * mom_x, xx, xy, xz, total * sv_x - sb_x * vel_dot]
        flux_y = [HALF_STEP * mom_y, xy, yy, yz, total * sv_y - sb_y * vel_dot]
        flux_z = [HALF_STEP * mom_z, xz, yz, zz, total * sv_z - sb_z * vel_dot]
        out.append(
            dict(
                diffuse=diffuse,
                low_x=[f + d for f, d in zip(flux_x, diffuse)],
                high_x=[f - d for f, d in zip(flux_x, diffuse)],
                low_y=[f + d for f, d in zip(flux_y, diffuse)],
                high_y=[f - d for f, d in zip(flux_y, diffuse)],
                flux_z=flux_z,
                shear=xy,
                e_x=EDGE * (vel_z * cen_y - vel_y * cen_z),
                e_y=EDGE * (vel_x * cen_z - vel_z * cen_x),
                e_z=EDGE * (vel_y * cen_x - vel_x * cen_y),
            )
        )
    return out


def plane_sum(terms, name):
    total = terms[0][name]
    for z in range(1, PLANES):
        total = total + terms[z][name]
    return total


def face_x_change(here, low):
    edge_y = plane_sum(here, "e_y") + plane_sum(low, "e_y")
    edge_y = [edge_y] * PLANES
    out = []
    for z in range(PLANES):
        pair = here[z]["e_z"] + low[z]["e_z"]
        out.append((edge_y[(z + 1) % PLANES] - edge_y[z]) - (after(pair) - before(pair)))
    return out


def row_step(state, low, here, high):
    new = [[None] * PLANES for f in range(FIELDS)]
    faces = [
        [
            (here[z - 1]["flux_z"][f] + here[z]["flux_z"][f])
            - (here[z]["diffuse"][f] - here[z - 1]["diffuse"][f])
            for f in range(5)
        ]
        for z in range(PLANES)
    ]
    for z in range(PLANES):
        cell = here[z]
        for f in range(5):
            along_x = high[z]["high_x"][f] - low[z]["low_x"][f]
            along_y = after(cell["high_y"][f]) - before(cell["low_y"][f])
            along_z = faces[(z + 1) % PLANES][f] - faces[z][f]
            kept = state[f][z] - 4.0 * cell["diffuse"][f]
            new[f][z] = kept - (along_x + along_y + along_z)
        mom_x, mom_y = (state[1][z], state[2][z])
        new[1][z] = new[1][z] + (TIME_STEP * 2.0 * ROTATION) * mom_y
        new[2][z] = new[2][z] - (TIME_STEP * (2.0 - SHEAR_RATE) * ROTATION) * mom_x
        new[4][z] = new[4][z] + (2.0 * SHEAR_RATE * ROTATION) * cell["shear"]
    change_x = face_x_change(here, low)
    exz = plane_sum(here, "e_x")
    edge_x = [exz + before(exz)] * PLANES
    along_y = after(exz) - before(exz)
    along_x = plane_sum(high, "e_y") - plane_sum(low, "e_y")
    for z in range(PLANES):
        pair = here[z]["e_z"] + low[z]["e_z"]
        pair_up = high[z]["e_z"] + here[z]["e_z"]
        edge = pair + before(pair)
        edge_up = pair_up + before(pair_up)
        new[5][z] = state[5][z] + change_x[z]
        new[6][z] = state[6][z] + ((edge_up - edge) - (edge_x[(z + 1) % PLANES] - edge_x[z]))
        new[7][z] = state[7][z] + (along_y - along_x)
    return new


def step_kernel(cells, peers, chunk, rows, shear_ref, shift_ref, frac_ref, *refs):
    messages = [refs[i * peers : (i + 1) * peers] for i in range(3)]
    out_refs = refs[3 * peers : 4 * peers]
    low_ref, high_ref, own_ref, out_ref, state_ref, mid_ref = refs[4 * peers :]
    width = chunk + BELOW + ABOVE
    half = width // 2
    place = lax.axis_index("gx")
    places = lax.axis_size("gx")
    part = lax.axis_index("gy")
    shape = (peers, LANES)
    lane = lane_index(shape)
    lower, upper = shear_amounts(shear_ref[0], cells, peers)
    lower = jnp.where(place == 0, lower, 0)
    upper = jnp.where(place == places - 1, upper, 0)
    column = part * chunk - BELOW + lane

    for kind, ref in enumerate((low_ref, high_ref, own_ref)):
        size = ref.shape[0] // peers
        for d in range(peers):
            at = pl.multiple_of((part ^ d) * size, 8)
            ref[pl.ds(at, size), :] = messages[kind][d][...]

    def load(ref, row):
        return ref[pl.ds(row, peers, stride=ref.shape[0] // peers), :]

    def turn(value, amount):
        return pltpu.roll(value, amount, 0)

    def strips(value, amount):
        hop = amount // cells
        source = column - amount % cells
        pick = turn(value, hop % peers)
        pick = jnp.where(source < 0, turn(value, (hop + 1) % peers), pick)
        pick = jnp.where(source < -cells, turn(value, (hop + 2) % peers), pick)
        return jnp.where(source >= cells, turn(value, (hop + peers - 1) % peers), pick)

    def own_strips(value):
        pick = jnp.where(column < 0, turn(value, 1), value)
        return jnp.where(column >= cells, turn(value, peers - 1), pick)

    for f in range(FIELDS):
        for z in range(PLANES):
            for g in range(SENT):
                at = (f * PLANES + z) * SENT + g
                state_ref[g, f, z] = strips(load(low_ref, at), lower)
                state_ref[SENT + g, f, z] = own_strips(load(own_ref, at))
                state_ref[rows + g, f, z] = own_strips(load(own_ref, SLOT + at))
                state_ref[SENT + rows + g, f, z] = strips(load(high_ref, at), upper)
    face_high = []
    for z in range(PLANES):
        parts = [
            pltpu.roll(load(high_ref, z * SENT + g), LANES - width + g * half, 1)
            for g in range(SENT)
        ]
        face_high.append(strips(jnp.where(lane < half, parts[0], parts[1]), upper))

    def row_of(ref, index):
        return [[ref[index, f, z] for z in range(PLANES)] for f in range(FIELDS)]

    def faces_of(ref, index):
        return [ref[index, 5, z] for z in range(PLANES)]

    count = rows + 2 * SENT
    low = cell_terms(row_of(state_ref, 0), faces_of(state_ref, 1))
    here = cell_terms(row_of(state_ref, 1), faces_of(state_ref, 2))
    for index in range(1, count - 1):
        beyond = face_high if index + 2 == count else faces_of(state_ref, index + 2)
        high = cell_terms(row_of(state_ref, index + 1), beyond)
        new = row_step(row_of(state_ref, index), low, here, high)
        for f in range(FIELDS):
            for z in range(PLANES):
                mid_ref[index - 1, f, z] = new[f][z]
        low, here = here, high
    change = face_x_change(here, low)
    mid_face = [state_ref[count - 1, 5, z] + change[z] for z in range(PLANES)]

    count = rows + 2
    low = cell_terms(row_of(mid_ref, 0), faces_of(mid_ref, 1))
    here = cell_terms(row_of(mid_ref, 1), faces_of(mid_ref, 2))
    for index in range(1, count - 1):
        beyond = mid_face if index + 2 == count else faces_of(mid_ref, index + 2)
        high = cell_terms(row_of(mid_ref, index + 1), beyond)
        new = row_step(row_of(mid_ref, index), low, here, high)
        row = index - 1
        shift = shift_ref[row]
        hop = shift // cells
        crossing = part * chunk + lane % chunk + shift % cells >= cells
        weight = (frac_ref[row].astype(jnp.float32) + 0.5) / FRAC
        for f in range(FIELDS):
            packed = None
            for z in range(PLANES):
                done = 0.5 * (state_ref[index + 1, f, z] + new[f][z])
                mixed = (1.0 - weight) * done + weight * before(done)
                moved = pltpu.roll(mixed, (z * chunk - BELOW) % LANES, 1)
                packed = moved if z == 0 else jnp.where(lane < z * chunk, packed, moved)
            sent = jnp.where(crossing, turn(packed, (hop + 1) % peers), turn(packed, hop % peers))
            out_ref[pl.ds(f * rows + row, peers, stride=FIELDS * rows), :] = sent
        low, here = here, high
    size = FIELDS * rows
    for d in range(peers):
        at = pl.multiple_of((part ^ d) * size, 8)
        out_refs[d][...] = out_ref[pl.ds(at, size), :]


def place_kernel(cells, peers, chunk, shift_ref, *refs):
    in_refs, out_ref, in_ref = (refs[:peers], refs[peers], refs[peers + 1])
    rows = out_ref.shape[2]
    block = FIELDS * rows
    part = lax.axis_index("gy")
    for d in range(peers):
        in_ref[pl.ds(pl.multiple_of((part ^ d) * block, 8), block), :] = in_refs[d][...]
    per_group = 8 // rows
    amounts = [shift_ref[x] % cells for x in range(rows)]
    lanes = peers * chunk
    member = row_index((8, LANES)) % rows
    for group in range(FIELDS // per_group):
        pieces = [in_ref[k * block + group * 8 : k * block + group * 8 + 8, :] for k in range(peers)]
        for z in range(PLANES):
            joined = jnp.concatenate(
                [piece[:, z * chunk : (z + 1) * chunk] for piece in pieces], axis=1
            )
            tiles = [joined[:, i : i + LANES] for i in range(0, lanes, LANES)]
            result = shift_cells(tiles, amounts[0], cells)
            for x in range(1, rows):
                moved = shift_cells(tiles, amounts[x], cells)
                result = [jnp.where(member == x, m, r) for m, r in zip(moved, result)]
            result = jnp.concatenate(result, axis=1)[:, :cells]
            for g in range(per_group):
                out_ref[group * per_group + g, z] = result[g * rows : (g + 1) * rows]


def solution(mesh):
    places, peers = (mesh.shape["gx"], mesh.shape["gy"])
    smem = pl.BlockSpec(memory_space=pltpu.SMEM)
    vmem = pl.BlockSpec(memory_space=pltpu.VMEM)

    def array(*shape):
        return jax.ShapeDtypeStruct(shape, jnp.float32)

    def scratch(*shape):
        return pltpu.VMEM(shape, jnp.float32)

    def exchange(message, step, bits):
        if step == 0 and bits == 0:
            return message
        route = [
            (x * peers + y, (x + step) % places * peers + (y ^ bits))
            for x in range(places)
            for y in range(peers)
        ]
        return lax.ppermute(message, ("gx", "gy"), route)

    def shards(state, shear_offset, remap_shift, frac_index):
        rows, cells = state.shape[2:]
        chunk = -(-cells // peers)
        own = FIELDS * PLANES * rows
        messages = pl.pallas_call(
            lambda *refs: pack_kernel(cells, peers, chunk, *refs),
            out_shape=[array(size, LANES) for size in (SLOT, SLOT, own) for d in range(peers)],
            in_specs=[smem, vmem],
            out_specs=[vmem] * (3 * peers),
            scratch_shapes=[scratch(peers, size, LANES) for size in (SLOT, SLOT, own)],
            name="pack",
        )(shear_offset, state)
        steps = [step for step in (1, -1, 0) for d in range(peers)]
        bits = list(range(peers)) * 3
        messages = [exchange(*each) for each in zip(messages, steps, bits)]
        block = FIELDS * rows
        moved = pl.pallas_call(
            lambda *refs: step_kernel(cells, peers, chunk, rows, *refs),
            out_shape=[array(block, LANES) for d in range(peers)],
            in_specs=[smem] * 3 + [vmem] * (3 * peers),
            out_specs=[vmem] * peers,
            scratch_shapes=[
                scratch(peers * SLOT, LANES),
                scratch(peers * SLOT, LANES),
                scratch(peers * own, LANES),
                scratch(peers * block, LANES),
                scratch(rows + 2 * SENT, FIELDS, PLANES, peers, LANES),
                scratch(rows + 2, FIELDS, PLANES, peers, LANES),
            ],
            name="step",
        )(shear_offset, remap_shift, frac_index, *messages)
        moved = [exchange(message, 0, d) for d, message in enumerate(moved)]
        return pl.pallas_call(
            lambda *refs: place_kernel(cells, peers, chunk, *refs),
            out_shape=array(*state.shape),
            in_specs=[smem] + [vmem] * peers,
            out_specs=vmem,
            scratch_shapes=[scratch(peers * block, LANES)],
            name="place",
        )(remap_shift, *moved)

    placed = (P(None, None, "gx", "gy"), P(), P("gx"), P("gx"))
    return jax.shard_map(
        shards, mesh=mesh, in_specs=placed, out_specs=P(None, None, "gx", "gy"), check_vma=False
    )
```

```python
import jax
import jax.numpy as jnp
from jax import lax
from jax.experimental import pallas as pl
from jax.experimental.pallas import tpu as pltpu
from jax.sharding import PartitionSpec as P

FRAC = 16

ADIABATIC = 5.0 / 3.0
ROTATION = 1.0
SHEAR_RATE = 1.5
MAX_SPEED = 5.0
TIME_STEP = 0.05

LANES = 128
FIELDS = 8
PLANES = 2
BELOW = 3
ABOVE = 3
SENT = 2
SLOT = FIELDS * PLANES * SENT
HALF_STEP = 0.5 * TIME_STEP
DIFFUSE = 0.5 * MAX_SPEED * TIME_STEP
EDGE = 0.25 * TIME_STEP


def lane_index(shape):
    return lax.broadcasted_iota(jnp.int32, shape, 1)


def row_index(shape):
    return lax.broadcasted_iota(jnp.int32, shape, 0)


def after(value):
    return pltpu.roll(value, LANES - 1, 1)


def before(value):
    return pltpu.roll(value, 1, 1)


def roll_tiles(tiles, amount):
    count = len(tiles)
    part = amount % LANES
    whole = amount // LANES
    turned = [pltpu.roll(tile, part, 1) for tile in tiles]
    low = lane_index(tiles[0].shape) < part
    tiles = [jnp.where(low, turned[i - 1], turned[i]) for i in range(count)]
    bit = 1
    while bit < count:
        tiles = [
            jnp.where((whole // bit) % 2 == 1, tiles[(i - bit) % count], tiles[i])
            for i in range(count)
        ]
        bit *= 2
    return tiles


def shift_cells(tiles, amount, cells):
    total = len(tiles) * LANES
    high = roll_tiles(tiles, amount)
    low = roll_tiles(tiles, (amount + total - cells) % total)
    lane = lane_index(tiles[0].shape)
    return [
        jnp.where(lane + i * LANES >= amount, high[i], low[i]) for i in range(len(tiles))
    ]


def shear_amounts(shear, cells, peers):
    total = cells * peers
    return shear, (total - shear) % total


def pack_kernel(cells, peers, chunk, shear_ref, state_ref, low_ref, high_ref, out_ref):
    width = chunk + BELOW + ABOVE
    half = width // 2
    rows = state_ref.shape[2]
    place = lax.axis_index("gx")
    places = lax.axis_size("gx")
    lower, upper = shear_amounts(shear_ref[0], cells, peers)
    low_turn = jnp.where(place == 0, lower % cells, 0)
    high_turn = jnp.where(place == places - 1, upper % cells, 0)

    def stacked(pieces):
        return jnp.concatenate(pieces, axis=0)

    def tiles_of(value):
        spare = -cells % LANES
        pad = jnp.zeros((value.shape[0], spare), value.dtype)
        value = jnp.concatenate([value, pad], axis=1)
        return [value[:, i : i + LANES] for i in range(0, cells + spare, LANES)]

    def turned(value, amount):
        return jnp.concatenate(shift_cells(tiles_of(value), amount, cells), axis=1)[:, :cells]

    def windows(value):
        top = peers * chunk + ABOVE - cells
        wide = jnp.concatenate([value[:, cells - BELOW :], value, value[:, :top]], axis=1)
        return [wide[:, k * chunk : k * chunk + width] for k in range(peers)]

    def put(row, values):
        for k, value in enumerate(values):
            out_ref[k, row : row + 8, 0 : value.shape[1]] = value

    per_group = 8 // SENT
    groups = FIELDS * PLANES // per_group
    for group in range(groups):
        members = [divmod(m, PLANES) for m in range(group * per_group, (group + 1) * per_group)]
        blocks = [state_ref[f, z] for f, z in members]
        put(group * 8, windows(stacked([b[:SENT] for b in blocks])))
        put(SLOT + group * 8, windows(stacked([b[rows - SENT :] for b in blocks])))
        low = stacked([low_ref[f, z] for f, z in members])
        put(2 * SLOT + group * 8, windows(turned(low, low_turn)))
        blocks = [high_ref[f, z] for f, z in members]
        high = windows(turned(stacked([b[:SENT] for b in blocks]), high_turn))
        if group == 0:
            faces = [high_ref[5, z][SENT : SENT + 1] for z in range(PLANES)]
            pieces = [faces[i // SENT] for i in range(PLANES * SENT)]
            faces = windows(turned(stacked(pieces * (8 // len(pieces))), high_turn))
            first = row_index((8, half)) % SENT == 0
            high = [
                jnp.concatenate([value, jnp.where(first, face[:, :half], face[:, half:])], axis=1)
                for value, face in zip(high, faces)
            ]
        put(3 * SLOT + group * 8, high)


def cell_terms(state, next_face_x):
    planes = range(PLANES)
    face_z = state[7]
    out = []
    for z in planes:
        density, mom_x, mom_y, mom_z, energy, face_x, face_y = (state[f][z] for f in range(7))
        cen_x = 0.5 * (face_x + next_face_x[z])
        cen_y = 0.5 * (face_y + after(face_y))
        cen_z = 0.5 * (face_z[z] + face_z[(z + 1) % PLANES])
        inverse = 1.0 / density
        vel_x, vel_y, vel_z = (mom_x * inverse, mom_y * inverse, mom_z * inverse)
        magnetic = 0.5 * (cen_x * cen_x + cen_y * cen_y + cen_z * cen_z)
        kinetic = 0.5 * (mom_x * vel_x + mom_y * vel_y + mom_z * vel_z)
        pressure = (ADIABATIC - 1.0) * (energy - kinetic - magnetic) + magnetic
        vel_dot = vel_x * cen_x + vel_y * cen_y + vel_z * cen_z
        scaled_p = HALF_STEP * pressure
        total = energy + pressure
        sv_x, sv_y, sv_z = (HALF_STEP * vel_x, HALF_STEP * vel_y, HALF_STEP * vel_z)
        sb_x, sb_y, sb_z = (HALF_STEP * cen_x, HALF_STEP * cen_y, HALF_STEP * cen_z)
        xx = mom_x * sv_x - cen_x * sb_x + scaled_p
        yy = mom_y * sv_y - cen_y * sb_y + scaled_p
        zz = mom_z * sv_z - cen_z * sb_z + scaled_p
        xy = mom_x * sv_y - cen_x * sb_y
        xz = mom_x * sv_z - cen_x * sb_z
        yz = mom_y * sv_z - cen_y * sb_z
        diffuse = [DIFFUSE * state[f][z] for f in range(5)]
        flux_x = [HALF_STEP * mom_x, xx, xy, xz, total * sv_x - sb_x * vel_dot]
        flux_y = [HALF_STEP * mom_y, xy, yy, yz, total * sv_y - sb_y * vel_dot]
        flux_z = [HALF_STEP * mom_z, xz, yz, zz, total * sv_z - sb_z * vel_dot]
        out.append(
            dict(
                diffuse=diffuse,
                low_x=[f + d for f, d in zip(flux_x, diffuse)],
                high_x=[f - d for f, d in zip(flux_x, diffuse)],
                low_y=[f + d for f, d in zip(flux_y, diffuse)],
                high_y=[f - d for f, d in zip(flux_y, diffuse)],
                flux_z=flux_z,
                shear=xy,
                e_x=EDGE * (vel_z * cen_y - vel_y * cen_z),
                e_y=EDGE * (vel_x * cen_z - vel_z * cen_x),
                e_z=EDGE * (vel_y * cen_x - vel_x * cen_y),
            )
        )
    return out


def plane_sum(terms, name):
    total = terms[0][name]
    for z in range(1, PLANES):
        total = total + terms[z][name]
    return total


def face_x_change(here, low):
    edge_y = plane_sum(here, "e_y") + plane_sum(low, "e_y")
    edge_y = [edge_y] * PLANES
    out = []
    for z in range(PLANES):
        pair = here[z]["e_z"] + low[z]["e_z"]
        out.append((edge_y[(z + 1) % PLANES] - edge_y[z]) - (after(pair) - before(pair)))
    return out


def row_step(state, low, here, high):
    new = [[None] * PLANES for f in range(FIELDS)]
    faces = [
        [
            (here[z - 1]["flux_z"][f] + here[z]["flux_z"][f])
            - (here[z]["diffuse"][f] - here[z - 1]["diffuse"][f])
            for f in range(5)
        ]
        for z in range(PLANES)
    ]
    for z in range(PLANES):
        cell = here[z]
        for f in range(5):
            along_x = high[z]["high_x"][f] - low[z]["low_x"][f]
            along_y = after(cell["high_y"][f]) - before(cell["low_y"][f])
            along_z = faces[(z + 1) % PLANES][f] - faces[z][f]
            kept = state[f][z] - 4.0 * cell["diffuse"][f]
            new[f][z] = kept - (along_x + along_y + along_z)
        mom_x, mom_y = (state[1][z], state[2][z])
        new[1][z] = new[1][z] + (TIME_STEP * 2.0 * ROTATION) * mom_y
        new[2][z] = new[2][z] - (TIME_STEP * (2.0 - SHEAR_RATE) * ROTATION) * mom_x
        new[4][z] = new[4][z] + (2.0 * SHEAR_RATE * ROTATION) * cell["shear"]
    change_x = face_x_change(here, low)
    exz = plane_sum(here, "e_x")
    edge_x = [exz + before(exz)] * PLANES
    along_y = after(exz) - before(exz)
    along_x = plane_sum(high, "e_y") - plane_sum(low, "e_y")
    for z in range(PLANES):
        pair = here[z]["e_z"] + low[z]["e_z"]
        pair_up = high[z]["e_z"] + here[z]["e_z"]
        edge = pair + before(pair)
        edge_up = pair_up + before(pair_up)
        new[5][z] = state[5][z] + change_x[z]
        new[6][z] = state[6][z] + ((edge_up - edge) - (edge_x[(z + 1) % PLANES] - edge_x[z]))
        new[7][z] = state[7][z] + (along_y - along_x)
    return new


def step_kernel(
    cells, peers, chunk, rows, shear_ref, shift_ref, frac_ref, in_ref, out_ref, state_ref, mid_ref
):
    width = chunk + BELOW + ABOVE
    half = width // 2
    place = lax.axis_index("gx")
    places = lax.axis_size("gx")
    part = lax.axis_index("gy")
    shape = (peers, LANES)
    lane = lane_index(shape)
    lower, upper = shear_amounts(shear_ref[0], cells, peers)
    lower = jnp.where(place == 0, lower, 0)
    upper = jnp.where(place == places - 1, upper, 0)
    column = part * chunk - BELOW + lane

    def load(row):
        return in_ref[pl.ds(row, peers, stride=in_ref.shape[0] // peers), :]

    def turn(value, amount):
        return pltpu.roll(value, amount, 0)

    def strips(value, amount):
        hop = amount // cells
        source = column - amount % cells
        pick = turn(value, hop % peers)
        pick = jnp.where(source < 0, turn(value, (hop + 1) % peers), pick)
        pick = jnp.where(source < -cells, turn(value, (hop + 2) % peers), pick)
        return jnp.where(source >= cells, turn(value, (hop + peers - 1) % peers), pick)

    def own_strips(value):
        pick = jnp.where(column < 0, turn(value, 1), value)
        return jnp.where(column >= cells, turn(value, peers - 1), pick)

    for f in range(FIELDS):
        for z in range(PLANES):
            for g in range(SENT):
                at = (f * PLANES + z) * SENT + g
                state_ref[g, f, z] = strips(load(2 * SLOT + at), lower)
                state_ref[SENT + g, f, z] = own_strips(load(at))
                state_ref[rows + g, f, z] = own_strips(load(SLOT + at))
                state_ref[SENT + rows + g, f, z] = strips(load(3 * SLOT + at), upper)
    face_high = []
    for z in range(PLANES):
        parts = [
            pltpu.roll(load(3 * SLOT + z * SENT + g), LANES - width + g * half, 1)
            for g in range(SENT)
        ]
        face_high.append(strips(jnp.where(lane < half, parts[0], parts[1]), upper))

    def row_of(ref, index):
        return [[ref[index, f, z] for z in range(PLANES)] for f in range(FIELDS)]

    def faces_of(ref, index):
        return [ref[index, 5, z] for z in range(PLANES)]

    count = rows + 2 * SENT
    low = cell_terms(row_of(state_ref, 0), faces_of(state_ref, 1))
    here = cell_terms(row_of(state_ref, 1), faces_of(state_ref, 2))
    for index in range(1, count - 1):
        beyond = face_high if index + 2 == count else faces_of(state_ref, index + 2)
        high = cell_terms(row_of(state_ref, index + 1), beyond)
        new = row_step(row_of(state_ref, index), low, here, high)
        for f in range(FIELDS):
            for z in range(PLANES):
                mid_ref[index - 1, f, z] = new[f][z]
        low, here = here, high
    change = face_x_change(here, low)
    mid_face = [state_ref[count - 1, 5, z] + change[z] for z in range(PLANES)]

    count = rows + 2
    low = cell_terms(row_of(mid_ref, 0), faces_of(mid_ref, 1))
    here = cell_terms(row_of(mid_ref, 1), faces_of(mid_ref, 2))
    for index in range(1, count - 1):
        beyond = mid_face if index + 2 == count else faces_of(mid_ref, index + 2)
        high = cell_terms(row_of(mid_ref, index + 1), beyond)
        new = row_step(row_of(mid_ref, index), low, here, high)
        row = index - 1
        shift = shift_ref[row]
        hop = shift // cells
        crossing = part * chunk + lane % chunk + shift % cells >= cells
        weight = (frac_ref[row].astype(jnp.float32) + 0.5) / FRAC
        for f in range(FIELDS):
            packed = None
            for z in range(PLANES):
                done = 0.5 * (state_ref[index + 1, f, z] + new[f][z])
                mixed = (1.0 - weight) * done + weight * before(done)
                moved = pltpu.roll(mixed, (z * chunk - BELOW) % LANES, 1)
                packed = moved if z == 0 else jnp.where(lane < z * chunk, packed, moved)
            sent = jnp.where(crossing, turn(packed, (hop + 1) % peers), turn(packed, hop % peers))
            out_ref[pl.ds(f * rows + row, peers, stride=FIELDS * rows), :] = sent
        low, here = here, high


def place_kernel(cells, peers, chunk, shift_ref, in_ref, out_ref):
    rows = out_ref.shape[2]
    part = lax.axis_index("gy")
    per_group = 8 // rows
    amounts = [shift_ref[x] % cells for x in range(rows)]
    lanes = peers * chunk
    member = row_index((8, LANES)) % rows
    for group in range(FIELDS // per_group):
        pieces = [in_ref[k, part, group * 8 : group * 8 + 8, :] for k in range(peers)]
        for z in range(PLANES):
            joined = jnp.concatenate(
                [piece[:, z * chunk : (z + 1) * chunk] for piece in pieces], axis=1
            )
            tiles = [joined[:, i : i + LANES] for i in range(0, lanes, LANES)]
            result = shift_cells(tiles, amounts[0], cells)
            for x in range(1, rows):
                moved = shift_cells(tiles, amounts[x], cells)
                result = [jnp.where(member == x, m, r) for m, r in zip(moved, result)]
            result = jnp.concatenate(result, axis=1)[:, :cells]
            for g in range(per_group):
                out_ref[group * per_group + g, z] = result[g * rows : (g + 1) * rows]


def solution(mesh):
    places, peers = (mesh.shape["gx"], mesh.shape["gy"])
    smem = pl.BlockSpec(memory_space=pltpu.SMEM)
    vmem = pl.BlockSpec(memory_space=pltpu.VMEM)

    def array(*shape):
        return jax.ShapeDtypeStruct(shape, jnp.float32)

    def scratch(*shape):
        return pltpu.VMEM(shape, jnp.float32)

    def shards(state, shear_offset, remap_shift, frac_index):
        rows, cells = state.shape[2:]
        chunk = -(-cells // peers)
        up = [(x, (x + 1) % places) for x in range(places)]
        low = lax.ppermute(state[:, :, rows - SENT :], "gx", up)
        high = lax.ppermute(state[:, :, : SENT + 1], "gx", [(j, i) for i, j in up])
        size = 2 * SLOT + FIELDS * PLANES * rows
        message = pl.pallas_call(
            lambda *refs: pack_kernel(cells, peers, chunk, *refs),
            out_shape=array(peers, size, LANES),
            in_specs=[smem] + [vmem] * 3,
            out_specs=vmem,
            name="pack",
        )(shear_offset, state, low, high)
        message = lax.all_to_all(message, "gy", 0, 0, tiled=True)
        block = FIELDS * rows
        moved = pl.pallas_call(
            lambda *refs: step_kernel(cells, peers, chunk, rows, *refs),
            out_shape=array(peers * block, LANES),
            in_specs=[smem] * 3 + [vmem],
            out_specs=vmem,
            scratch_shapes=[
                scratch(rows + 2 * SENT, FIELDS, PLANES, peers, LANES),
                scratch(rows + 2, FIELDS, PLANES, peers, LANES),
            ],
            name="step",
        )(shear_offset, remap_shift, frac_index, message.reshape(peers * size, LANES))
        moved = lax.all_gather(moved, "gy", axis=0)
        return pl.pallas_call(
            lambda *refs: place_kernel(cells, peers, chunk, *refs),
            out_shape=array(*state.shape),
            in_specs=[smem, vmem],
            out_specs=vmem,
            name="place",
        )(remap_shift, moved.reshape(peers, peers, block, LANES))

    placed = (P(None, None, "gx", "gy"), P(), P("gx"), P("gx"))
    return jax.shard_map(
        shards, mesh=mesh, in_specs=placed, out_specs=P(None, None, "gx", "gy"), check_vma=False
    )
```

```python
import jax
import jax.numpy as jnp
from jax import lax
from jax.experimental import pallas as pl
from jax.experimental.pallas import tpu as pltpu
from jax.sharding import PartitionSpec as P

FRAC = 16

ADIABATIC = 5.0 / 3.0
ROTATION = 1.0
SHEAR_RATE = 1.5
MAX_SPEED = 5.0
TIME_STEP = 0.05

LANES = 128
SUBLANES = 8
FIELDS = 8
PLANES = 2
FACE_X = 5
BELOW = 3
ABOVE = 3
SENT = 2
HALF_STEP = 0.5 * TIME_STEP
DIFFUSE = 0.5 * MAX_SPEED * TIME_STEP
EDGE = 0.25 * TIME_STEP


def lane_index():
    return lax.broadcasted_iota(jnp.int32, (SUBLANES, LANES), 1)


def row_index():
    return lax.broadcasted_iota(jnp.int32, (SUBLANES, LANES), 0)


def turn_lanes(value, amount):
    return pltpu.roll(value, amount, 1)


def turn_rows(value, amount):
    amount %= SUBLANES
    return pltpu.roll(value, amount, 0) if amount else value


def radial_next(value):
    return turn_rows(value, -1)


def radial_prev(value):
    return turn_rows(value, 1)


def tiles_for(columns):
    return -(-columns // LANES)


def plan(shear, cells, peers):
    rest = shear % cells
    middle = cells // 2
    near = (rest >= middle - 5) & (rest <= middle + 5)
    own = jnp.where(near, middle - 12, middle)
    up = (own - shear) % cells
    down = (own + shear) % cells
    up_hop = (shear - own + up) // cells
    down_hop = (shear + own) // cells
    return own, up, down, up_hop, down_hop


def pair_kernel(cells, peers, shear_ref, state_ref, below_ref, joined_ref, up_ref, down_ref):
    place = lax.axis_index("gx")
    places = lax.axis_size("gx")
    own, up, down, _, _ = plan(shear_ref[0], cells, peers)
    up = jnp.where(place == places - 1, up, own)
    down = jnp.where(place == 0, down, own)
    lane = lane_index()
    row = row_index()
    single = tiles_for(cells)
    gap = cells % LANES
    double = joined_ref.shape[1]
    window = up_ref.shape[1]

    def tiles_of(ref, f):
        both = [ref[f, z] for z in range(PLANES)]
        value = jnp.concatenate(both, axis=0)
        return [value[:, i * LANES : min((i + 1) * LANES, cells)] for i in range(single)]

    def widened(tile):
        spare = LANES - tile.shape[1]
        if spare == 0:
            return tile
        return jnp.concatenate([tile, jnp.zeros((SUBLANES, spare), tile.dtype)], axis=1)

    for f in range(FIELDS):
        lower = [widened(t) for t in tiles_of(below_ref, f)]
        upper = [turn_lanes(widened(t), gap) for t in tiles_of(state_ref, f)]
        for i in range(single):
            if i < single - 1:
                joined_ref[f, i] = lower[i]
            else:
                joined_ref[f, i] = jnp.where(lane < gap, lower[i], upper[0])
        for i in range(single, double):
            k = i - single
            joined_ref[f, i] = jnp.where(lane < gap, upper[k], upper[min(k + 1, single - 1)])

    def cut(f, start):
        return cut_window(joined_ref, f, start, window)

    late = row % 4 >= SENT
    for pair in range(FIELDS // 2):
        ups = [cut(2 * pair + i, up) for i in range(2)]
        downs = [cut(2 * pair + i, down) for i in range(2)]
        for t in range(window):
            up_ref[pair, t] = jnp.where(late, ups[0][t], turn_rows(ups[1][t], -SENT))
            down_ref[pair, t] = jnp.where(late, turn_rows(downs[1][t], SENT), downs[0][t])
    for t, value in enumerate(cut(FACE_X, down)):
        down_ref[FIELDS // 2, t] = value


def cut_window(joined_ref, f, start, count):
    whole = start // LANES
    part = start % LANES
    last = joined_ref.shape[1] - 1
    tiles = [joined_ref[f, jnp.minimum(whole + t, last)] for t in range(count + 1)]
    turned = [turn_lanes(tile, (LANES - part) % LANES) for tile in tiles]
    here = lane_index() < LANES - part
    return [jnp.where(here, turned[t], turned[t + 1]) for t in range(count)]


def cell_terms(state, next_face_x, next_face_y):
    planes = range(PLANES)
    face_z = state[7]
    out = []
    for z in planes:
        density, mom_x, mom_y, mom_z, energy, face_x, face_y = (state[f][z] for f in range(7))
        cen_x = 0.5 * (face_x + next_face_x[z])
        cen_y = 0.5 * (face_y + next_face_y[z])
        cen_z = 0.5 * (face_z[z] + face_z[(z + 1) % PLANES])
        inverse = 1.0 / density
        vel_x, vel_y, vel_z = (mom_x * inverse, mom_y * inverse, mom_z * inverse)
        magnetic = 0.5 * (cen_x * cen_x + cen_y * cen_y + cen_z * cen_z)
        kinetic = 0.5 * (mom_x * vel_x + mom_y * vel_y + mom_z * vel_z)
        pressure = (ADIABATIC - 1.0) * (energy - kinetic - magnetic) + magnetic
        vel_dot = vel_x * cen_x + vel_y * cen_y + vel_z * cen_z
        scaled_p = HALF_STEP * pressure
        total = energy + pressure
        sv_x, sv_y, sv_z = (HALF_STEP * vel_x, HALF_STEP * vel_y, HALF_STEP * vel_z)
        sb_x, sb_y, sb_z = (HALF_STEP * cen_x, HALF_STEP * cen_y, HALF_STEP * cen_z)
        xx = mom_x * sv_x - cen_x * sb_x + scaled_p
        yy = mom_y * sv_y - cen_y * sb_y + scaled_p
        zz = mom_z * sv_z - cen_z * sb_z + scaled_p
        xy = mom_x * sv_y - cen_x * sb_y
        xz = mom_x * sv_z - cen_x * sb_z
        yz = mom_y * sv_z - cen_y * sb_z
        diffuse = [DIFFUSE * state[f][z] for f in range(5)]
        flux_x = [HALF_STEP * mom_x, xx, xy, xz, total * sv_x - sb_x * vel_dot]
        flux_y = [HALF_STEP * mom_y, xy, yy, yz, total * sv_y - sb_y * vel_dot]
        flux_z = [HALF_STEP * mom_z, xz, yz, zz, total * sv_z - sb_z * vel_dot]
        e_z = EDGE * (vel_y * cen_x - vel_x * cen_y)
        pair = e_z + radial_prev(e_z)
        out.append(
            dict(
                diffuse=diffuse,
                along_x=[
                    radial_next(f - d) - radial_prev(f + d) for f, d in zip(flux_x, diffuse)
                ],
                low_y=[turn_lanes(f + d, 1) for f, d in zip(flux_y, diffuse)],
                high_y=[turn_lanes(f - d, LANES - 1) for f, d in zip(flux_y, diffuse)],
                flux_z=flux_z,
                shear=xy,
                e_x=EDGE * (vel_z * cen_y - vel_y * cen_z),
                e_y=EDGE * (vel_x * cen_z - vel_z * cen_x),
                pair=pair,
                low_pair=turn_lanes(pair, 1),
                high_pair=turn_lanes(pair, LANES - 1),
            )
        )
    e_x, e_y = (
        [sum((cell[name] for cell in out[1:]), out[0][name]) for name in ("e_x", "e_y")]
    )
    shared = dict(
        e_x=e_x,
        low_e_x=turn_lanes(e_x, 1),
        high_e_x=turn_lanes(e_x, LANES - 1),
        edge_y=[e_y + radial_prev(e_y)] * PLANES,
        along_x=radial_next(e_y) - radial_prev(e_y),
    )
    return out, shared


def tile_step(state, low, here, high):
    lane = lane_index()
    cells_low, shared_low = low
    cells, shared = here
    cells_high, shared_high = high

    def before(turned_low, turned):
        return jnp.where(lane > 0, turned, turned_low)

    def after(turned, turned_high):
        return jnp.where(lane < LANES - 1, turned, turned_high)

    new = [[None] * PLANES for f in range(FIELDS)]
    faces = [
        [
            (cells[z - 1]["flux_z"][f] + cells[z]["flux_z"][f])
            - (cells[z]["diffuse"][f] - cells[z - 1]["diffuse"][f])
            for f in range(5)
        ]
        for z in range(PLANES)
    ]
    low_e_x = before(shared_low["low_e_x"], shared["low_e_x"])
    along_y = after(shared["high_e_x"], shared_high["high_e_x"]) - low_e_x
    edge_x = [shared["e_x"] + low_e_x] * PLANES
    edge_y = shared["edge_y"]
    for z in range(PLANES):
        cell = cells[z]
        up = (z + 1) % PLANES
        for f in range(5):
            high_y = after(cell["high_y"][f], cells_high[z]["high_y"][f])
            low_y = before(cells_low[z]["low_y"][f], cell["low_y"][f])
            along_z = faces[up][f] - faces[z][f]
            kept = state[f][z] - 4.0 * cell["diffuse"][f]
            new[f][z] = kept - (cell["along_x"][f] + (high_y - low_y) + along_z)
        mom_x, mom_y = (state[1][z], state[2][z])
        new[1][z] = new[1][z] + (TIME_STEP * 2.0 * ROTATION) * mom_y
        new[2][z] = new[2][z] - (TIME_STEP * (2.0 - SHEAR_RATE) * ROTATION) * mom_x
        new[4][z] = new[4][z] + (2.0 * SHEAR_RATE * ROTATION) * cell["shear"]
        low_pair = before(cells_low[z]["low_pair"], cell["low_pair"])
        high_pair = after(cell["high_pair"], cells_high[z]["high_pair"])
        edge_z = cell["pair"] + low_pair
        new[5][z] = state[5][z] + ((edge_y[up] - edge_y[z]) - (high_pair - low_pair))
        new[6][z] = state[6][z] + ((radial_next(edge_z) - edge_z) - (edge_x[up] - edge_x[z]))
        new[7][z] = state[7][z] + (along_y - shared["along_x"])
    return new


def step_kernel(
    cells, peers, rows,
    shear_ref, frac_ref, joined_ref, up_ref, down_ref, out_ref, state_ref, mid_ref,
):
    own = plan(shear_ref[0], cells, peers)[0]
    lane = lane_index()
    row = row_index()
    window = up_ref.shape[1]
    single = tiles_for(cells)

    for f in range(FIELDS):
        pair, second = divmod(f, 2)
        for t, tile in enumerate(cut_window(joined_ref, f, own, window)):
            up = up_ref[pair, t]
            down = down_ref[pair, t]
            for z in range(PLANES):
                up_at = z * 4 + (0 if second else SENT)
                down_at = z * 4 + (SENT if second else 0)
                value = turn_rows(tile, -z * 4)
                value = jnp.where(row < rows, value, turn_rows(down, rows - down_at))
                value = jnp.where(row < rows + SENT, value, turn_rows(up, rows + SENT - up_at))
                state_ref[t, f, z] = value
    last = rows + SENT - 1

    def faces_beyond(t, face_x):
        beyond = down_ref[FIELDS // 2, t]
        return [
            jnp.where(row == last, turn_rows(beyond, last - (z * 4 + SENT)), radial_next(face_x[z]))
            for z in range(PLANES)
        ]

    def terms(ref, t, count, beyond):
        state = [[ref[t, f, z] for z in range(PLANES)] for f in range(FIELDS)]
        if beyond:
            next_face_x = faces_beyond(t, state[FACE_X])
        else:
            next_face_x = [radial_next(face) for face in state[FACE_X]]
        next_face_y = []
        for z in range(PLANES):
            here = turn_lanes(state[6][z], LANES - 1)
            if t + 1 < count:
                there = turn_lanes(ref[t + 1, 6, z], LANES - 1)
                here = jnp.where(lane < LANES - 1, here, there)
            next_face_y.append(here)
        return state, cell_terms(state, next_face_x, next_face_y)

    low = here = terms(state_ref, 0, window, True)
    for t in range(window):
        high = terms(state_ref, t + 1, window, True) if t + 1 < window else here
        new = tile_step(here[0], low[1], here[1], high[1])
        for f in range(FIELDS):
            for z in range(PLANES):
                if t < single or f == 6:
                    mid_ref[t, f, z] = new[f][z]
        low, here = here, high

    weight = jnp.zeros((SUBLANES, LANES), jnp.float32)
    for x in range(rows):
        level = (frac_ref[x].astype(jnp.float32) + 0.5) / FRAC
        weight = jnp.where(row == x, level, weight)
    keep = 1.0 - weight
    low = here = terms(mid_ref, 0, window, False)
    low_done = None
    low_moved = None

    def emit(t, moved):
        for f in range(FIELDS):
            out_ref[f, t] = moved[f]

    for t in range(single):
        high = terms(mid_ref, t + 1, window, False) if t + 1 < single else here
        new = tile_step(here[0], low[1], here[1], high[1])
        done = []
        moved = []
        for f in range(FIELDS):
            mixed = []
            turned = []
            for z in range(PLANES):
                value = 0.5 * (state_ref[t, f, z] + new[f][z])
                below = turn_lanes(value, 1)
                turned.append(below)
                if t:
                    below = jnp.where(lane > 0, below, low_done[f][z])
                mixed.append(keep * value + weight * below)
            done.append(turned)
            both = jnp.where(row < rows, mixed[0], turn_rows(mixed[1], 4))
            moved.append(turn_lanes(both, LANES - BELOW))
        if t:
            emit(
                t - 1,
                [jnp.where(lane < LANES - BELOW, a, b) for a, b in zip(low_moved, moved)],
            )
        low_done, low_moved = done, moved
        low, here = here, high
    emit(single - 1, low_moved)


def row_sources(shift, own, cells, peers, target):
    total = cells * peers
    offset = cells - BELOW - own
    shift = (shift + total - offset) % total
    hop = shift // cells
    rest = shift % cells
    upper = (target + 2 * peers - hop) % peers
    lower = (target + 2 * peers - hop - 1) % peers
    return upper, lower, rest


def turned_rows(cells, peers, rows, shift_ref, own, part, target, block_ref, out_ref):
    row = row_index()
    lane = lane_index()
    count = out_ref.shape[1]
    spare = count * LANES - cells
    plans = []
    for x in range(rows):
        upper, lower, rest = row_sources(shift_ref[x], own, cells, peers, target)
        first = upper % 2 == part % 2
        block = jnp.where(first, upper, lower) // 2
        amount = jnp.where(first, rest, rest + spare)
        plans.append((block, amount // LANES, amount % LANES))
    for f in range(FIELDS):
        result = None
        for x, (block, whole, fine) in enumerate(plans):
            tiles = [block_ref[block, f, (t + count - whole) % count] for t in range(count)]
            tiles = [turn_lanes(tile, fine) for tile in tiles]
            tiles = [jnp.where(lane < fine, tiles[t - 1], tiles[t]) for t in range(count)]
            if x == 0:
                result = tiles
            else:
                result = [jnp.where(row % rows == x, a, b) for a, b in zip(tiles, result)]
        for t in range(count):
            out_ref[f, t] = result[t]


def gather_kernel(cells, peers, rows, shear_ref, shift_ref, *refs):
    in_refs, block_ref, out_ref = (refs[:-2], refs[-2], refs[-1])
    part = lax.axis_index("gy")
    own = plan(shear_ref[0], cells, peers)[0]
    for i, ref in enumerate(in_refs):
        block_ref[(part // 2) ^ i] = ref[...]
    turned_rows(cells, peers, rows, shift_ref, own, part, part ^ 1, block_ref, out_ref)


def keep_kernel(cells, peers, rows, shear_ref, shift_ref, block_ref, out_ref):
    part = lax.axis_index("gy")
    own = plan(shear_ref[0], cells, peers)[0]
    turned_rows(cells, peers, rows, shift_ref, own, part, part, block_ref, out_ref)


def merge_kernel(cells, peers, rows, shear_ref, shift_ref, mine_ref, other_ref, out_ref):
    part = lax.axis_index("gy")
    own = plan(shear_ref[0], cells, peers)[0]
    row = row_index() % rows
    lane = lane_index()
    count = mine_ref.shape[1]
    border = jnp.zeros((SUBLANES, LANES), jnp.int32)
    first = jnp.zeros((SUBLANES, LANES), jnp.int32)
    for x in range(rows):
        upper, _, rest = row_sources(shift_ref[x], own, cells, peers, part)
        border = jnp.where(row == x, rest, border)
        first = jnp.where(row == x, (upper + part + 1) % 2, first)
    masks = [(lane + t * LANES >= border) == (first == 1) for t in range(count)]
    for f in range(FIELDS):
        tiles = [jnp.where(masks[t], mine_ref[f, t], other_ref[f, t]) for t in range(count)]
        value = jnp.concatenate(tiles, axis=1)[:, :cells]
        for z in range(PLANES):
            out_ref[f, z] = value[z * rows : (z + 1) * rows]


def solution(mesh):
    places, peers = (mesh.shape["gx"], mesh.shape["gy"])
    smem = pl.BlockSpec(memory_space=pltpu.SMEM)
    vmem = pl.BlockSpec(memory_space=pltpu.VMEM)
    axes = ("gx", "gy")

    def array(*shape):
        return jax.ShapeDtypeStruct(shape + (SUBLANES, LANES), jnp.float32)

    def scratch(*shape):
        return pltpu.VMEM(shape + (SUBLANES, LANES), jnp.float32)

    def device(x, y):
        return x % places * peers + y % peers

    devices = [(x, y) for x in range(places) for y in range(peers)]

    def ghosts(up_hop, down_hop, up, down):
        rise = [(device(x, y), device(x + 1, y + up_hop * (x == places - 1))) for x, y in devices]
        fall = [(device(x, y), device(x - 1, y - down_hop * (x == 0))) for x, y in devices]
        return lax.ppermute(up, axes, rise), lax.ppermute(down, axes, fall)

    def shards(state, shear_offset, remap_shift, frac_index):
        rows, cells = state.shape[2:]
        single = tiles_for(cells)
        double = tiles_for(2 * cells)
        window = tiles_for(BELOW + cells + ABOVE)
        below = lax.ppermute(state, "gy", [(i, (i + 1) % peers) for i in range(peers)])
        joined, up, down = pl.pallas_call(
            lambda *refs: pair_kernel(cells, peers, *refs),
            out_shape=[
                array(FIELDS, double),
                array(FIELDS // 2, window),
                array(FIELDS // 2 + 1, window),
            ],
            in_specs=[smem, vmem, vmem],
            out_specs=[vmem] * 3,
            name="pair",
        )(shear_offset, state, below)
        _, _, _, up_hop, down_hop = plan(shear_offset[0], cells, peers)
        branches = [
            lambda u, d, i=i: ghosts(i // 2 + i % 2, i // 2, u, d) for i in range(2 * peers)
        ]
        which = (2 * down_hop + (up_hop - down_hop)) % (2 * peers)
        up, down = lax.switch(which, branches, up, down)
        block = pl.pallas_call(
            lambda *refs: step_kernel(cells, peers, rows, *refs),
            out_shape=array(FIELDS, single),
            in_specs=[smem] * 2 + [vmem] * 3,
            out_specs=vmem,
            scratch_shapes=[scratch(window, FIELDS, PLANES)] * 2,
            name="step",
        )(shear_offset, frac_index, joined, up, down)

        def exchange(value, bits):
            return lax.ppermute(value, "gy", [(i, i ^ bits) for i in range(peers)])

        blocks = [block] + [exchange(block, bits) for bits in range(2, peers, 2)]
        blocks, other = pl.pallas_call(
            lambda *refs: gather_kernel(cells, peers, rows, *refs),
            out_shape=[array(peers // 2, FIELDS, single), array(FIELDS, single)],
            in_specs=[smem] * 2 + [vmem] * (peers // 2),
            out_specs=[vmem] * 2,
            name="gather",
        )(shear_offset, remap_shift, *blocks)
        other = exchange(other, 1)
        mine = pl.pallas_call(
            lambda *refs: keep_kernel(cells, peers, rows, *refs),
            out_shape=array(FIELDS, single),
            in_specs=[smem] * 2 + [vmem],
            out_specs=vmem,
            name="keep",
        )(shear_offset, remap_shift, blocks)
        return pl.pallas_call(
            lambda *refs: merge_kernel(cells, peers, rows, *refs),
            out_shape=jax.ShapeDtypeStruct(state.shape, jnp.float32),
            in_specs=[smem] * 2 + [vmem] * 2,
            out_specs=vmem,
            name="merge",
        )(shear_offset, remap_shift, mine, other)

    placed = (P(None, None, "gx", "gy"), P(), P("gx"), P("gx"))
    return jax.shard_map(
        shards, mesh=mesh, in_specs=placed, out_specs=P(None, None, "gx", "gy"), check_vma=False
    )
```

```python
import jax
import jax.numpy as jnp
from jax import lax
from jax.experimental import pallas as pl
from jax.experimental.pallas import tpu as pltpu
from jax.sharding import PartitionSpec as P

FRAC = 16

ADIABATIC = 5.0 / 3.0
ROTATION = 1.0
SHEAR_RATE = 1.5
MAX_SPEED = 5.0
TIME_STEP = 0.05

LANES = 128
SUBLANES = 8
FIELDS = 8
PLANES = 2
FACE_X = 5
BELOW = 3
ABOVE = 3
SENT = 2
HALF_STEP = 0.5 * TIME_STEP
DIFFUSE = 0.5 * MAX_SPEED * TIME_STEP
EDGE = 0.25 * TIME_STEP


def lane_index():
    return lax.broadcasted_iota(jnp.int32, (SUBLANES, LANES), 1)


def row_index():
    return lax.broadcasted_iota(jnp.int32, (SUBLANES, LANES), 0)


def turn_lanes(value, amount):
    return pltpu.roll(value, amount, 1)


def turn_rows(value, amount):
    amount %= SUBLANES
    return pltpu.roll(value, amount, 0) if amount else value


def radial_next(value):
    return turn_rows(value, -1)


def radial_prev(value):
    return turn_rows(value, 1)


def tiles_for(columns):
    return -(-columns // LANES)


def plan(shear, cells, peers):
    rest = shear % cells
    middle = cells // 2
    near = (rest >= middle - 5) & (rest <= middle + 5)
    own = jnp.where(near, middle - 12, middle)
    up = (own - shear) % cells
    down = (own + shear) % cells
    up_hop = (shear - own + up) // cells
    down_hop = (shear + own) // cells
    return own, up, down, up_hop, down_hop


def pair_kernel(cells, peers, shear_ref, state_ref, below_ref, joined_ref, up_ref, down_ref):
    place = lax.axis_index("gx")
    places = lax.axis_size("gx")
    own, up, down, _, _ = plan(shear_ref[0], cells, peers)
    up = jnp.where(place == places - 1, up, own)
    down = jnp.where(place == 0, down, own)
    lane = lane_index()
    row = row_index()
    single = tiles_for(cells)
    gap = cells % LANES
    double = joined_ref.shape[1]
    window = up_ref.shape[1]

    def tiles_of(ref, f):
        both = [ref[f, z] for z in range(PLANES)]
        value = jnp.concatenate(both, axis=0)
        return [value[:, i * LANES : min((i + 1) * LANES, cells)] for i in range(single)]

    def widened(tile):
        spare = LANES - tile.shape[1]
        if spare == 0:
            return tile
        return jnp.concatenate([tile, jnp.zeros((SUBLANES, spare), tile.dtype)], axis=1)

    for f in range(FIELDS):
        lower = [widened(t) for t in tiles_of(below_ref, f)]
        upper = [turn_lanes(widened(t), gap) for t in tiles_of(state_ref, f)]
        for i in range(single):
            if i < single - 1:
                joined_ref[f, i] = lower[i]
            else:
                joined_ref[f, i] = jnp.where(lane < gap, lower[i], upper[0])
        for i in range(single, double):
            k = i - single
            joined_ref[f, i] = jnp.where(lane < gap, upper[k], upper[min(k + 1, single - 1)])

    def cut(f, start):
        return cut_window(joined_ref, f, start, window)

    late = row % 4 >= SENT
    for pair in range(FIELDS // 2):
        ups = [cut(2 * pair + i, up) for i in range(2)]
        downs = [cut(2 * pair + i, down) for i in range(2)]
        for t in range(window):
            up_ref[pair, t] = jnp.where(late, ups[0][t], turn_rows(ups[1][t], -SENT))
            down_ref[pair, t] = jnp.where(late, turn_rows(downs[1][t], SENT), downs[0][t])
    for t, value in enumerate(cut(FACE_X, down)):
        down_ref[FIELDS // 2, t] = value


def cut_window(joined_ref, f, start, count):
    whole = start // LANES
    part = start % LANES
    last = joined_ref.shape[1] - 1
    tiles = [joined_ref[f, jnp.minimum(whole + t, last)] for t in range(count + 1)]
    turned = [turn_lanes(tile, (LANES - part) % LANES) for tile in tiles]
    here = lane_index() < LANES - part
    return [jnp.where(here, turned[t], turned[t + 1]) for t in range(count)]


def cell_terms(state, next_face_x, next_face_y):
    planes = range(PLANES)
    face_z = state[7]
    out = []
    for z in planes:
        density, mom_x, mom_y, mom_z, energy, face_x, face_y = (state[f][z] for f in range(7))
        cen_x = 0.5 * (face_x + next_face_x[z])
        cen_y = 0.5 * (face_y + next_face_y[z])
        cen_z = 0.5 * (face_z[z] + face_z[(z + 1) % PLANES])
        inverse = 1.0 / density
        vel_x, vel_y, vel_z = (mom_x * inverse, mom_y * inverse, mom_z * inverse)
        magnetic = 0.5 * (cen_x * cen_x + cen_y * cen_y + cen_z * cen_z)
        kinetic = 0.5 * (mom_x * vel_x + mom_y * vel_y + mom_z * vel_z)
        pressure = (ADIABATIC - 1.0) * (energy - kinetic - magnetic) + magnetic
        vel_dot = vel_x * cen_x + vel_y * cen_y + vel_z * cen_z
        scaled_p = HALF_STEP * pressure
        total = energy + pressure
        sv_x, sv_y, sv_z = (HALF_STEP * vel_x, HALF_STEP * vel_y, HALF_STEP * vel_z)
        sb_x, sb_y, sb_z = (HALF_STEP * cen_x, HALF_STEP * cen_y, HALF_STEP * cen_z)
        xx = mom_x * sv_x - cen_x * sb_x + scaled_p
        yy = mom_y * sv_y - cen_y * sb_y + scaled_p
        zz = mom_z * sv_z - cen_z * sb_z + scaled_p
        xy = mom_x * sv_y - cen_x * sb_y
        xz = mom_x * sv_z - cen_x * sb_z
        yz = mom_y * sv_z - cen_y * sb_z
        diffuse = [DIFFUSE * state[f][z] for f in range(5)]
        flux_x = [HALF_STEP * mom_x, xx, xy, xz, total * sv_x - sb_x * vel_dot]
        flux_y = [HALF_STEP * mom_y, xy, yy, yz, total * sv_y - sb_y * vel_dot]
        flux_z = [HALF_STEP * mom_z, xz, yz, zz, total * sv_z - sb_z * vel_dot]
        e_z = EDGE * (vel_y * cen_x - vel_x * cen_y)
        pair = e_z + radial_prev(e_z)
        out.append(
            dict(
                diffuse=diffuse,
                along_x=[
                    radial_next(f - d) - radial_prev(f + d) for f, d in zip(flux_x, diffuse)
                ],
                low_y=[turn_lanes(f + d, 1) for f, d in zip(flux_y, diffuse)],
                high_y=[turn_lanes(f - d, LANES - 1) for f, d in zip(flux_y, diffuse)],
                flux_z=flux_z,
                shear=xy,
                e_x=EDGE * (vel_z * cen_y - vel_y * cen_z),
                e_y=EDGE * (vel_x * cen_z - vel_z * cen_x),
                pair=pair,
                low_pair=turn_lanes(pair, 1),
                high_pair=turn_lanes(pair, LANES - 1),
            )
        )
    e_x, e_y = (
        [sum((cell[name] for cell in out[1:]), out[0][name]) for name in ("e_x", "e_y")]
    )
    shared = dict(
        e_x=e_x,
        low_e_x=turn_lanes(e_x, 1),
        high_e_x=turn_lanes(e_x, LANES - 1),
        edge_y=[e_y + radial_prev(e_y)] * PLANES,
        along_x=radial_next(e_y) - radial_prev(e_y),
    )
    return out, shared


def tile_step(state, low, here, high):
    lane = lane_index()
    cells_low, shared_low = low
    cells, shared = here
    cells_high, shared_high = high

    def before(turned_low, turned):
        return jnp.where(lane > 0, turned, turned_low)

    def after(turned, turned_high):
        return jnp.where(lane < LANES - 1, turned, turned_high)

    new = [[None] * PLANES for f in range(FIELDS)]
    faces = [
        [
            (cells[z - 1]["flux_z"][f] + cells[z]["flux_z"][f])
            - (cells[z]["diffuse"][f] - cells[z - 1]["diffuse"][f])
            for f in range(5)
        ]
        for z in range(PLANES)
    ]
    low_e_x = before(shared_low["low_e_x"], shared["low_e_x"])
    along_y = after(shared["high_e_x"], shared_high["high_e_x"]) - low_e_x
    edge_x = [shared["e_x"] + low_e_x] * PLANES
    edge_y = shared["edge_y"]
    for z in range(PLANES):
        cell = cells[z]
        up = (z + 1) % PLANES
        for f in range(5):
            high_y = after(cell["high_y"][f], cells_high[z]["high_y"][f])
            low_y = before(cells_low[z]["low_y"][f], cell["low_y"][f])
            along_z = faces[up][f] - faces[z][f]
            kept = state[f][z] - 4.0 * cell["diffuse"][f]
            new[f][z] = kept - (cell["along_x"][f] + (high_y - low_y) + along_z)
        mom_x, mom_y = (state[1][z], state[2][z])
        new[1][z] = new[1][z] + (TIME_STEP * 2.0 * ROTATION) * mom_y
        new[2][z] = new[2][z] - (TIME_STEP * (2.0 - SHEAR_RATE) * ROTATION) * mom_x
        new[4][z] = new[4][z] + (2.0 * SHEAR_RATE * ROTATION) * cell["shear"]
        low_pair = before(cells_low[z]["low_pair"], cell["low_pair"])
        high_pair = after(cell["high_pair"], cells_high[z]["high_pair"])
        edge_z = cell["pair"] + low_pair
        new[5][z] = state[5][z] + ((edge_y[up] - edge_y[z]) - (high_pair - low_pair))
        new[6][z] = state[6][z] + ((radial_next(edge_z) - edge_z) - (edge_x[up] - edge_x[z]))
        new[7][z] = state[7][z] + (along_y - shared["along_x"])
    return new


def step_kernel(
    cells, peers, rows,
    shear_ref, frac_ref, joined_ref, up_ref, down_ref, out_ref, state_ref, mid_ref,
):
    own = plan(shear_ref[0], cells, peers)[0]
    lane = lane_index()
    row = row_index()
    window = up_ref.shape[1]
    single = tiles_for(cells)

    for f in range(FIELDS):
        pair, second = divmod(f, 2)
        for t, tile in enumerate(cut_window(joined_ref, f, own, window)):
            up = up_ref[pair, t]
            down = down_ref[pair, t]
            for z in range(PLANES):
                up_at = z * 4 + (0 if second else SENT)
                down_at = z * 4 + (SENT if second else 0)
                value = turn_rows(tile, -z * 4)
                value = jnp.where(row < rows, value, turn_rows(down, rows - down_at))
                value = jnp.where(row < rows + SENT, value, turn_rows(up, rows + SENT - up_at))
                state_ref[t, f, z] = value
    last = rows + SENT - 1

    def faces_beyond(t, face_x):
        beyond = down_ref[FIELDS // 2, t]
        return [
            jnp.where(row == last, turn_rows(beyond, last - (z * 4 + SENT)), radial_next(face_x[z]))
            for z in range(PLANES)
        ]

    def terms(ref, t, count, beyond):
        state = [[ref[t, f, z] for z in range(PLANES)] for f in range(FIELDS)]
        if beyond:
            next_face_x = faces_beyond(t, state[FACE_X])
        else:
            next_face_x = [radial_next(face) for face in state[FACE_X]]
        next_face_y = []
        for z in range(PLANES):
            here = turn_lanes(state[6][z], LANES - 1)
            if t + 1 < count:
                there = turn_lanes(ref[t + 1, 6, z], LANES - 1)
                here = jnp.where(lane < LANES - 1, here, there)
            next_face_y.append(here)
        return state, cell_terms(state, next_face_x, next_face_y)

    low = here = terms(state_ref, 0, window, True)
    for t in range(window):
        high = terms(state_ref, t + 1, window, True) if t + 1 < window else here
        new = tile_step(here[0], low[1], here[1], high[1])
        for f in range(FIELDS):
            for z in range(PLANES):
                if t < single or f == 6:
                    mid_ref[t, f, z] = new[f][z]
        low, here = here, high

    weight = jnp.zeros((SUBLANES, LANES), jnp.float32)
    for x in range(rows):
        level = (frac_ref[x].astype(jnp.float32) + 0.5) / FRAC
        weight = jnp.where(row == x, level, weight)
    keep = 1.0 - weight
    low = here = terms(mid_ref, 0, window, False)
    low_done = None
    low_moved = None

    def emit(t, moved):
        for f in range(FIELDS):
            out_ref[f, t] = moved[f]

    for t in range(single):
        high = terms(mid_ref, t + 1, window, False) if t + 1 < single else here
        new = tile_step(here[0], low[1], here[1], high[1])
        done = []
        moved = []
        for f in range(FIELDS):
            mixed = []
            turned = []
            for z in range(PLANES):
                value = 0.5 * (state_ref[t, f, z] + new[f][z])
                below = turn_lanes(value, 1)
                turned.append(below)
                if t:
                    below = jnp.where(lane > 0, below, low_done[f][z])
                mixed.append(keep * value + weight * below)
            done.append(turned)
            both = jnp.where(row < rows, mixed[0], turn_rows(mixed[1], 4))
            moved.append(turn_lanes(both, LANES - BELOW))
        if t:
            emit(
                t - 1,
                [jnp.where(lane < LANES - BELOW, a, b) for a, b in zip(low_moved, moved)],
            )
        low_done, low_moved = done, moved
        low, here = here, high
    emit(single - 1, low_moved)


def row_sources(shift, own, cells, peers, target):
    total = cells * peers
    offset = cells - BELOW - own
    shift = (shift + total - offset) % total
    hop = shift // cells
    rest = shift % cells
    upper = (target + 2 * peers - hop) % peers
    lower = (target + 2 * peers - hop - 1) % peers
    return upper, lower, rest


def turned_rows(cells, peers, rows, shift_ref, own, part, target, block_ref, out_ref):
    row = row_index()
    lane = lane_index()
    count = out_ref.shape[1]
    spare = count * LANES - cells
    plans = []
    for x in range(rows):
        upper, lower, rest = row_sources(shift_ref[x], own, cells, peers, target)
        first = upper % 2 == part % 2
        block = jnp.where(first, upper, lower) // 2
        amount = jnp.where(first, rest, rest + spare)
        plans.append((block, amount // LANES, amount % LANES))
    for f in range(FIELDS):
        result = None
        for x, (block, whole, fine) in enumerate(plans):
            tiles = [block_ref[block, f, (t + count - whole) % count] for t in range(count)]
            tiles = [turn_lanes(tile, fine) for tile in tiles]
            tiles = [jnp.where(lane < fine, tiles[t - 1], tiles[t]) for t in range(count)]
            if x == 0:
                result = tiles
            else:
                result = [jnp.where(row % rows == x, a, b) for a, b in zip(tiles, result)]
        for t in range(count):
            out_ref[f, t] = result[t]


def gather_kernel(cells, peers, rows, shear_ref, shift_ref, *refs):
    in_refs, block_ref, out_ref = (refs[:-2], refs[-2], refs[-1])
    part = lax.axis_index("gy")
    own = plan(shear_ref[0], cells, peers)[0]
    for i, ref in enumerate(in_refs):
        block_ref[(part // 2) ^ i] = ref[...]
    turned_rows(cells, peers, rows, shift_ref, own, part, part ^ 1, block_ref, out_ref)


def keep_kernel(cells, peers, rows, shear_ref, shift_ref, block_ref, out_ref):
    part = lax.axis_index("gy")
    own = plan(shear_ref[0], cells, peers)[0]
    turned_rows(cells, peers, rows, shift_ref, own, part, part, block_ref, out_ref)


def merge_kernel(cells, peers, rows, shear_ref, shift_ref, mine_ref, other_ref, out_ref):
    part = lax.axis_index("gy")
    own = plan(shear_ref[0], cells, peers)[0]
    row = row_index() % rows
    lane = lane_index()
    count = mine_ref.shape[1]
    border = jnp.zeros((SUBLANES, LANES), jnp.int32)
    first = jnp.zeros((SUBLANES, LANES), jnp.int32)
    for x in range(rows):
        upper, _, rest = row_sources(shift_ref[x], own, cells, peers, part)
        border = jnp.where(row == x, rest, border)
        first = jnp.where(row == x, (upper + part + 1) % 2, first)
    masks = [(lane + t * LANES >= border) == (first == 1) for t in range(count)]
    for f in range(FIELDS):
        tiles = [jnp.where(masks[t], mine_ref[f, t], other_ref[f, t]) for t in range(count)]
        value = jnp.concatenate(tiles, axis=1)[:, :cells]
        for z in range(PLANES):
            out_ref[f, z] = value[z * rows : (z + 1) * rows]


def solution(mesh):
    places, peers = (mesh.shape["gx"], mesh.shape["gy"])
    smem = pl.BlockSpec(memory_space=pltpu.SMEM)
    vmem = pl.BlockSpec(memory_space=pltpu.VMEM)
    params = pltpu.CompilerParams(vmem_limit_bytes=8 * 2**20)
    axes = ("gx", "gy")

    def array(*shape):
        return jax.ShapeDtypeStruct(shape + (SUBLANES, LANES), jnp.float32)

    def scratch(*shape):
        return pltpu.VMEM(shape + (SUBLANES, LANES), jnp.float32)

    def device(x, y):
        return x % places * peers + y % peers

    devices = [(x, y) for x in range(places) for y in range(peers)]

    def ghosts(up_hop, down_hop, up, down):
        rise = [(device(x, y), device(x + 1, y + up_hop * (x == places - 1))) for x, y in devices]
        fall = [(device(x, y), device(x - 1, y - down_hop * (x == 0))) for x, y in devices]
        return lax.ppermute(up, axes, rise), lax.ppermute(down, axes, fall)

    def shards(state, shear_offset, remap_shift, frac_index):
        rows, cells = state.shape[2:]
        single = tiles_for(cells)
        double = tiles_for(2 * cells)
        window = tiles_for(BELOW + cells + ABOVE)
        below = lax.ppermute(state, "gy", [(i, (i + 1) % peers) for i in range(peers)])
        joined, up, down = pl.pallas_call(
            lambda *refs: pair_kernel(cells, peers, *refs),
            out_shape=[
                array(FIELDS, double),
                array(FIELDS // 2, window),
                array(FIELDS // 2 + 1, window),
            ],
            in_specs=[smem, vmem, vmem],
            out_specs=[vmem] * 3,
            compiler_params=params,
            name="pair",
        )(shear_offset, state, below)
        _, _, _, up_hop, down_hop = plan(shear_offset[0], cells, peers)
        branches = [
            lambda u, d, i=i: ghosts(i // 2 + i % 2, i // 2, u, d) for i in range(2 * peers)
        ]
        which = (2 * down_hop + (up_hop - down_hop)) % (2 * peers)
        up, down = lax.switch(which, branches, up, down)
        block = pl.pallas_call(
            lambda *refs: step_kernel(cells, peers, rows, *refs),
            out_shape=array(FIELDS, single),
            in_specs=[smem] * 2 + [vmem] * 3,
            out_specs=vmem,
            scratch_shapes=[scratch(window, FIELDS, PLANES)] * 2,
            compiler_params=params,
            name="step",
        )(shear_offset, frac_index, joined, up, down)

        def exchange(value, bits):
            return lax.ppermute(value, "gy", [(i, i ^ bits) for i in range(peers)])

        blocks = [block] + [exchange(block, bits) for bits in range(2, peers, 2)]
        blocks, other = pl.pallas_call(
            lambda *refs: gather_kernel(cells, peers, rows, *refs),
            out_shape=[array(peers // 2, FIELDS, single), array(FIELDS, single)],
            in_specs=[smem] * 2 + [vmem] * (peers // 2),
            out_specs=[vmem] * 2,
            compiler_params=params,
            name="gather",
        )(shear_offset, remap_shift, *blocks)
        other = exchange(other, 1)
        mine = pl.pallas_call(
            lambda *refs: keep_kernel(cells, peers, rows, *refs),
            out_shape=array(FIELDS, single),
            in_specs=[smem] * 2 + [vmem],
            out_specs=vmem,
            compiler_params=params,
            name="keep",
        )(shear_offset, remap_shift, blocks)
        return pl.pallas_call(
            lambda *refs: merge_kernel(cells, peers, rows, *refs),
            out_shape=jax.ShapeDtypeStruct(state.shape, jnp.float32),
            in_specs=[smem] * 2 + [vmem] * 2,
            out_specs=vmem,
            compiler_params=params,
            name="merge",
        )(shear_offset, remap_shift, mine, other)

    placed = (P(None, None, "gx", "gy"), P(), P("gx"), P("gx"))
    return jax.shard_map(
        shards, mesh=mesh, in_specs=placed, out_specs=P(None, None, "gx", "gy"), check_vma=False
    )
```

```python
import jax
import jax.numpy as jnp
from jax import lax
from jax.experimental import pallas as pl
from jax.experimental.pallas import tpu as pltpu
from jax.sharding import PartitionSpec as P

FRAC = 16

ADIABATIC = 5.0 / 3.0
ROTATION = 1.0
SHEAR_RATE = 1.5
MAX_SPEED = 5.0
TIME_STEP = 0.05

LANES = 128
SUBLANES = 8
FIELDS = 8
PLANES = 2
FACE_X = 5
BELOW = 3
ABOVE = 3
SENT = 2
HALF_STEP = 0.5 * TIME_STEP
DIFFUSE = 0.5 * MAX_SPEED * TIME_STEP
EDGE = 0.25 * TIME_STEP


def lane_index():
    return lax.broadcasted_iota(jnp.int32, (SUBLANES, LANES), 1)


def row_index():
    return lax.broadcasted_iota(jnp.int32, (SUBLANES, LANES), 0)


def turn_lanes(value, amount):
    return pltpu.roll(value, amount, 1)


def turn_rows(value, amount):
    amount %= SUBLANES
    return pltpu.roll(value, amount, 0) if amount else value


def radial_next(value):
    return turn_rows(value, -1)


def radial_prev(value):
    return turn_rows(value, 1)


def tiles_for(columns):
    return -(-columns // LANES)


def plan(shear, cells, peers):
    rest = shear % cells
    middle = cells // 2
    near = (rest >= middle - 5) & (rest <= middle + 5)
    own = jnp.where(near, middle - 12, middle)
    up = (own - shear) % cells
    down = (own + shear) % cells
    up_hop = (shear - own + up) // cells
    down_hop = (shear + own) // cells
    return own, up, down, up_hop, down_hop


def block_tiles(ref, f, cells):
    value = jnp.concatenate([ref[f, z] for z in range(PLANES)], axis=0)
    tiles = []
    for i in range(0, cells, LANES):
        tile = value[:, i : min(i + LANES, cells)]
        spare = LANES - tile.shape[1]
        if spare:
            tile = jnp.concatenate([tile, jnp.zeros((SUBLANES, spare), tile.dtype)], axis=1)
        tiles.append(tile)
    return tiles


def join_tiles(lower, upper, cells, put):
    gap = cells % LANES
    lane = lane_index()
    single = len(lower)
    upper = [turn_lanes(tile, gap) for tile in upper]
    for i in range(single - 1):
        put(i, lower[i])
    put(single - 1, jnp.where(lane < gap, lower[-1], upper[0]))
    for k in range(single):
        put(single + k, jnp.where(lane < gap, upper[k], upper[min(k + 1, single - 1)]))


def cut_window(joined_ref, f, start, count):
    whole = start // LANES
    part = start % LANES
    last = joined_ref.shape[1] - 1
    tiles = [joined_ref[f, jnp.minimum(whole + t, last)] for t in range(count + 1)]
    turned = [turn_lanes(tile, (LANES - part) % LANES) for tile in tiles]
    here = lane_index() < LANES - part
    return [jnp.where(here, turned[t], turned[t + 1]) for t in range(count)]


def edge_kernel(cells, rows, state_ref, up_ref, down_ref):
    row = row_index()
    late = row % rows >= SENT
    single = tiles_for(cells)
    faces = jnp.zeros((SUBLANES, LANES), jnp.float32)
    for pair in range(FIELDS // 2):
        first, second = (block_tiles(state_ref, 2 * pair + i, cells) for i in range(2))
        for t in range(single):
            up_ref[pair * single + t] = jnp.where(late, first[t], turn_rows(second[t], -SENT))
            down_ref[pair * single + t] = jnp.where(late, turn_rows(second[t], SENT), first[t])
        if FACE_X // 2 == pair:
            for t, tile in enumerate((first, second)[FACE_X % 2]):
                for z in range(PLANES):
                    at = t * PLANES + z
                    faces = jnp.where(row == at, turn_rows(tile, at - (z * rows + SENT)), faces)
    down_ref[FIELDS // 2 * single] = faces


def join_kernel(cells, peers, shear_ref, state_ref, below_ref, out_ref, joined_ref):
    own = plan(shear_ref[0], cells, peers)[0]
    for f in range(FIELDS):

        def put(i, tile):
            joined_ref[f, i] = tile

        lower, upper = (block_tiles(ref, f, cells) for ref in (below_ref, state_ref))
        join_tiles(lower, upper, cells, put)
        for t, tile in enumerate(cut_window(joined_ref, f, own, out_ref.shape[1])):
            out_ref[f, t] = tile


def cell_terms(state, next_face_x, next_face_y):
    planes = range(PLANES)
    face_z = state[7]
    out = []
    for z in planes:
        density, mom_x, mom_y, mom_z, energy, face_x, face_y = (state[f][z] for f in range(7))
        cen_x = 0.5 * (face_x + next_face_x[z])
        cen_y = 0.5 * (face_y + next_face_y[z])
        cen_z = 0.5 * (face_z[z] + face_z[(z + 1) % PLANES])
        inverse = 1.0 / density
        vel_x, vel_y, vel_z = (mom_x * inverse, mom_y * inverse, mom_z * inverse)
        magnetic = 0.5 * (cen_x * cen_x + cen_y * cen_y + cen_z * cen_z)
        kinetic = 0.5 * (mom_x * vel_x + mom_y * vel_y + mom_z * vel_z)
        pressure = (ADIABATIC - 1.0) * (energy - kinetic - magnetic) + magnetic
        vel_dot = vel_x * cen_x + vel_y * cen_y + vel_z * cen_z
        scaled_p = HALF_STEP * pressure
        total = energy + pressure
        sv_x, sv_y, sv_z = (HALF_STEP * vel_x, HALF_STEP * vel_y, HALF_STEP * vel_z)
        sb_x, sb_y, sb_z = (HALF_STEP * cen_x, HALF_STEP * cen_y, HALF_STEP * cen_z)
        xx = mom_x * sv_x - cen_x * sb_x + scaled_p
        yy = mom_y * sv_y - cen_y * sb_y + scaled_p
        zz = mom_z * sv_z - cen_z * sb_z + scaled_p
        xy = mom_x * sv_y - cen_x * sb_y
        xz = mom_x * sv_z - cen_x * sb_z
        yz = mom_y * sv_z - cen_y * sb_z
        diffuse = [DIFFUSE * state[f][z] for f in range(5)]
        flux_x = [HALF_STEP * mom_x, xx, xy, xz, total * sv_x - sb_x * vel_dot]
        flux_y = [HALF_STEP * mom_y, xy, yy, yz, total * sv_y - sb_y * vel_dot]
        flux_z = [HALF_STEP * mom_z, xz, yz, zz, total * sv_z - sb_z * vel_dot]
        e_z = EDGE * (vel_y * cen_x - vel_x * cen_y)
        pair = e_z + radial_prev(e_z)
        out.append(
            dict(
                diffuse=diffuse,
                along_x=[
                    radial_next(f - d) - radial_prev(f + d) for f, d in zip(flux_x, diffuse)
                ],
                low_y=[turn_lanes(f + d, 1) for f, d in zip(flux_y, diffuse)],
                high_y=[turn_lanes(f - d, LANES - 1) for f, d in zip(flux_y, diffuse)],
                flux_z=flux_z,
                shear=xy,
                e_x=EDGE * (vel_z * cen_y - vel_y * cen_z),
                e_y=EDGE * (vel_x * cen_z - vel_z * cen_x),
                pair=pair,
                low_pair=turn_lanes(pair, 1),
                high_pair=turn_lanes(pair, LANES - 1),
            )
        )
    e_x, e_y = (
        [sum((cell[name] for cell in out[1:]), out[0][name]) for name in ("e_x", "e_y")]
    )
    shared = dict(
        e_x=e_x,
        low_e_x=turn_lanes(e_x, 1),
        high_e_x=turn_lanes(e_x, LANES - 1),
        edge_y=[e_y + radial_prev(e_y)] * PLANES,
        along_x=radial_next(e_y) - radial_prev(e_y),
    )
    return out, shared


def tile_step(state, low, here, high):
    lane = lane_index()
    cells_low, shared_low = low
    cells, shared = here
    cells_high, shared_high = high

    def before(turned_low, turned):
        return jnp.where(lane > 0, turned, turned_low)

    def after(turned, turned_high):
        return jnp.where(lane < LANES - 1, turned, turned_high)

    new = [[None] * PLANES for f in range(FIELDS)]
    faces = [
        [
            (cells[z - 1]["flux_z"][f] + cells[z]["flux_z"][f])
            - (cells[z]["diffuse"][f] - cells[z - 1]["diffuse"][f])
            for f in range(5)
        ]
        for z in range(PLANES)
    ]
    low_e_x = before(shared_low["low_e_x"], shared["low_e_x"])
    along_y = after(shared["high_e_x"], shared_high["high_e_x"]) - low_e_x
    edge_x = [shared["e_x"] + low_e_x] * PLANES
    edge_y = shared["edge_y"]
    for z in range(PLANES):
        cell = cells[z]
        up = (z + 1) % PLANES
        for f in range(5):
            high_y = after(cell["high_y"][f], cells_high[z]["high_y"][f])
            low_y = before(cells_low[z]["low_y"][f], cell["low_y"][f])
            along_z = faces[up][f] - faces[z][f]
            kept = state[f][z] - 4.0 * cell["diffuse"][f]
            new[f][z] = kept - (cell["along_x"][f] + (high_y - low_y) + along_z)
        mom_x, mom_y = (state[1][z], state[2][z])
        new[1][z] = new[1][z] + (TIME_STEP * 2.0 * ROTATION) * mom_y
        new[2][z] = new[2][z] - (TIME_STEP * (2.0 - SHEAR_RATE) * ROTATION) * mom_x
        new[4][z] = new[4][z] + (2.0 * SHEAR_RATE * ROTATION) * cell["shear"]
        low_pair = before(cells_low[z]["low_pair"], cell["low_pair"])
        high_pair = after(cell["high_pair"], cells_high[z]["high_pair"])
        edge_z = cell["pair"] + low_pair
        new[5][z] = state[5][z] + ((edge_y[up] - edge_y[z]) - (high_pair - low_pair))
        new[6][z] = state[6][z] + ((radial_next(edge_z) - edge_z) - (edge_x[up] - edge_x[z]))
        new[7][z] = state[7][z] + (along_y - shared["along_x"])
    return new


def step_kernel(
    cells, peers, rows,
    shear_ref, frac_ref, block_ref, up_ref, up_below_ref, down_ref, down_below_ref,
    out_ref, state_ref, mid_ref, joined_ref, ghost_ref,
):
    place = lax.axis_index("gx")
    places = lax.axis_size("gx")
    own, up_start, down_start, _, _ = plan(shear_ref[0], cells, peers)
    up_start = jnp.where(place == 0, up_start, own)
    down_start = jnp.where(place == places - 1, down_start, own)
    lane = lane_index()
    row = row_index()
    window = block_ref.shape[1]
    single = tiles_for(cells)
    pairs = FIELDS // 2

    def ghosts(index, tiles, start):
        def put(i, tile):
            joined_ref[index, i] = tile

        join_tiles(*tiles, cells, put)
        for t, tile in enumerate(cut_window(joined_ref, index, start, window)):
            ghost_ref[index, t] = tile

    for pair in range(pairs):
        span = range(pair * single, (pair + 1) * single)
        ghosts(pair, [[ref[i] for i in span] for ref in (up_below_ref, up_ref)], up_start)
        tiles = [[ref[i] for i in span] for ref in (down_below_ref, down_ref)]
        ghosts(pairs + pair, tiles, down_start)
    faces = [ref[pairs * single] for ref in (down_below_ref, down_ref)]
    tiles = [[turn_rows(face, -t * PLANES) for t in range(single)] for face in faces]
    ghosts(2 * pairs, tiles, down_start)

    for f in range(FIELDS):
        pair, second = divmod(f, 2)
        for t in range(window):
            tile = block_ref[f, t]
            up = ghost_ref[pair, t]
            down = ghost_ref[pairs + pair, t]
            for z in range(PLANES):
                up_at = z * rows + (0 if second else SENT)
                down_at = z * rows + (SENT if second else 0)
                value = turn_rows(tile, -z * rows)
                value = jnp.where(row < rows, value, turn_rows(down, rows - down_at))
                value = jnp.where(row < rows + SENT, value, turn_rows(up, rows + SENT - up_at))
                state_ref[t, f, z] = value
    last = rows + SENT - 1

    def faces_beyond(t, face_x):
        beyond = ghost_ref[2 * pairs, t]
        return [
            jnp.where(row == last, turn_rows(beyond, last - z), radial_next(face_x[z]))
            for z in range(PLANES)
        ]

    def terms(ref, t, count, beyond):
        state = [[ref[t, f, z] for z in range(PLANES)] for f in range(FIELDS)]
        if beyond:
            next_face_x = faces_beyond(t, state[FACE_X])
        else:
            next_face_x = [radial_next(face) for face in state[FACE_X]]
        next_face_y = []
        for z in range(PLANES):
            here = turn_lanes(state[6][z], LANES - 1)
            if t + 1 < count:
                there = turn_lanes(ref[t + 1, 6, z], LANES - 1)
                here = jnp.where(lane < LANES - 1, here, there)
            next_face_y.append(here)
        return state, cell_terms(state, next_face_x, next_face_y)

    low = here = terms(state_ref, 0, window, True)
    for t in range(window):
        high = terms(state_ref, t + 1, window, True) if t + 1 < window else here
        new = tile_step(here[0], low[1], here[1], high[1])
        for f in range(FIELDS):
            for z in range(PLANES):
                if t < single or f == 6:
                    mid_ref[t, f, z] = new[f][z]
        low, here = here, high

    weight = jnp.zeros((SUBLANES, LANES), jnp.float32)
    for x in range(rows):
        level = (frac_ref[x].astype(jnp.float32) + 0.5) / FRAC
        weight = jnp.where(row == x, level, weight)
    keep = 1.0 - weight
    low = here = terms(mid_ref, 0, window, False)
    low_done = None
    low_moved = None

    def emit(t, moved):
        for f in range(FIELDS):
            out_ref[f, t] = moved[f]

    for t in range(single):
        high = terms(mid_ref, t + 1, window, False) if t + 1 < single else here
        new = tile_step(here[0], low[1], here[1], high[1])
        done = []
        moved = []
        for f in range(FIELDS):
            mixed = []
            turned = []
            for z in range(PLANES):
                value = 0.5 * (state_ref[t, f, z] + new[f][z])
                below = turn_lanes(value, 1)
                turned.append(below)
                if t:
                    below = jnp.where(lane > 0, below, low_done[f][z])
                mixed.append(keep * value + weight * below)
            done.append(turned)
            both = jnp.where(row < rows, mixed[0], turn_rows(mixed[1], rows))
            moved.append(turn_lanes(both, LANES - BELOW))
        if t:
            emit(
                t - 1,
                [jnp.where(lane < LANES - BELOW, a, b) for a, b in zip(low_moved, moved)],
            )
        low_done, low_moved = done, moved
        low, here = here, high
    emit(single - 1, low_moved)


def row_sources(shift, own, cells, peers, target):
    total = cells * peers
    offset = cells - BELOW - own
    shift = (shift + total - offset) % total
    hop = shift // cells
    rest = shift % cells
    upper = (target + 2 * peers - hop) % peers
    lower = (target + 2 * peers - hop - 1) % peers
    return upper, lower, rest


def turned_rows(cells, peers, rows, shift_ref, own, part, target, block_ref, out_ref):
    row = row_index()
    lane = lane_index()
    count = out_ref.shape[1]
    spare = count * LANES - cells
    plans = []
    for x in range(rows):
        upper, lower, rest = row_sources(shift_ref[x], own, cells, peers, target)
        first = upper % 2 == part % 2
        block = jnp.where(first, upper, lower) // 2
        amount = jnp.where(first, rest, rest + spare)
        plans.append((block, amount // LANES, amount % LANES))
    for f in range(FIELDS):
        result = None
        for x, (block, whole, fine) in enumerate(plans):
            tiles = [block_ref[block, f, (t + count - whole) % count] for t in range(count)]
            tiles = [turn_lanes(tile, fine) for tile in tiles]
            tiles = [jnp.where(lane < fine, tiles[t - 1], tiles[t]) for t in range(count)]
            if x == 0:
                result = tiles
            else:
                result = [jnp.where(row % rows == x, a, b) for a, b in zip(tiles, result)]
        for t in range(count):
            out_ref[f, t] = result[t]


def gather_kernel(cells, peers, rows, shear_ref, shift_ref, *refs):
    in_refs, block_ref, out_ref = (refs[:-2], refs[-2], refs[-1])
    part = lax.axis_index("gy")
    own = plan(shear_ref[0], cells, peers)[0]
    for i, ref in enumerate(in_refs):
        block_ref[(part // 2) ^ i] = ref[...]
    turned_rows(cells, peers, rows, shift_ref, own, part, part ^ 1, block_ref, out_ref)


def keep_kernel(cells, peers, rows, shear_ref, shift_ref, block_ref, out_ref):
    part = lax.axis_index("gy")
    own = plan(shear_ref[0], cells, peers)[0]
    turned_rows(cells, peers, rows, shift_ref, own, part, part, block_ref, out_ref)


def merge_kernel(cells, peers, rows, shear_ref, shift_ref, mine_ref, other_ref, out_ref):
    part = lax.axis_index("gy")
    own = plan(shear_ref[0], cells, peers)[0]
    row = row_index() % rows
    lane = lane_index()
    count = mine_ref.shape[1]
    border = jnp.zeros((SUBLANES, LANES), jnp.int32)
    first = jnp.zeros((SUBLANES, LANES), jnp.int32)
    for x in range(rows):
        upper, _, rest = row_sources(shift_ref[x], own, cells, peers, part)
        border = jnp.where(row == x, rest, border)
        first = jnp.where(row == x, (upper + part + 1) % 2, first)
    masks = [(lane + t * LANES >= border) == (first == 1) for t in range(count)]
    for f in range(FIELDS):
        tiles = [jnp.where(masks[t], mine_ref[f, t], other_ref[f, t]) for t in range(count)]
        value = jnp.concatenate(tiles, axis=1)[:, :cells]
        for z in range(PLANES):
            out_ref[f, z] = value[z * rows : (z + 1) * rows]


def solution(mesh):
    places, peers = (mesh.shape["gx"], mesh.shape["gy"])
    smem = pl.BlockSpec(memory_space=pltpu.SMEM)
    vmem = pl.BlockSpec(memory_space=pltpu.VMEM)
    params = pltpu.CompilerParams(vmem_limit_bytes=8 * 2**20)
    axes = ("gx", "gy")

    def array(*shape):
        return jax.ShapeDtypeStruct(shape + (SUBLANES, LANES), jnp.float32)

    def scratch(*shape):
        return pltpu.VMEM(shape + (SUBLANES, LANES), jnp.float32)

    def device(x, y):
        return x % places * peers + y % peers

    devices = [(x, y) for x in range(places) for y in range(peers)]

    def ghosts(up_hop, down_hop, up, down):
        rise = [(device(x, y), device(x + 1, y + up_hop * (x == places - 1))) for x, y in devices]
        fall = [(device(x, y), device(x - 1, y - down_hop * (x == 0))) for x, y in devices]
        return lax.ppermute(up, axes, rise), lax.ppermute(down, axes, fall)

    def shards(state, shear_offset, remap_shift, frac_index):
        rows, cells = state.shape[2:]
        single = tiles_for(cells)
        double = tiles_for(2 * cells)
        window = tiles_for(BELOW + cells + ABOVE)
        pairs = FIELDS // 2

        def onward(value):
            return lax.ppermute(value, "gy", [(i, (i + 1) % peers) for i in range(peers)])

        below = onward(state)
        up, down = pl.pallas_call(
            lambda *refs: edge_kernel(cells, rows, *refs),
            out_shape=[array(pairs * single), array(pairs * single + 1)],
            in_specs=[vmem],
            out_specs=[vmem] * 2,
            compiler_params=params,
            name="edge",
        )(state)
        _, _, _, up_hop, down_hop = plan(shear_offset[0], cells, peers)
        branches = [
            lambda u, d, i=i: ghosts(i // 2 + i % 2, i // 2, u, d) for i in range(2 * peers)
        ]
        which = (2 * down_hop + (up_hop - down_hop)) % (2 * peers)
        up, down = lax.switch(which, branches, up, down)
        up_below, down_below = onward(up), onward(down)
        block = pl.pallas_call(
            lambda *refs: join_kernel(cells, peers, *refs),
            out_shape=array(FIELDS, window),
            in_specs=[smem, vmem, vmem],
            out_specs=vmem,
            scratch_shapes=[scratch(FIELDS, double)],
            compiler_params=params,
            name="join",
        )(shear_offset, state, below)
        block = pl.pallas_call(
            lambda *refs: step_kernel(cells, peers, rows, *refs),
            out_shape=array(FIELDS, single),
            in_specs=[smem] * 2 + [vmem] * 5,
            out_specs=vmem,
            scratch_shapes=[scratch(window, FIELDS, PLANES)] * 2
            + [scratch(FIELDS + 1, double), scratch(FIELDS + 1, window)],
            compiler_params=params,
            name="step",
        )(shear_offset, frac_index, block, up, up_below, down, down_below)

        def exchange(value, bits):
            return lax.ppermute(value, "gy", [(i, i ^ bits) for i in range(peers)])

        blocks = [block] + [exchange(block, bits) for bits in range(2, peers, 2)]
        blocks, other = pl.pallas_call(
            lambda *refs: gather_kernel(cells, peers, rows, *refs),
            out_shape=[array(peers // 2, FIELDS, single), array(FIELDS, single)],
            in_specs=[smem] * 2 + [vmem] * (peers // 2),
            out_specs=[vmem] * 2,
            compiler_params=params,
            name="gather",
        )(shear_offset, remap_shift, *blocks)
        other = exchange(other, 1)
        mine = pl.pallas_call(
            lambda *refs: keep_kernel(cells, peers, rows, *refs),
            out_shape=array(FIELDS, single),
            in_specs=[smem] * 2 + [vmem],
            out_specs=vmem,
            compiler_params=params,
            name="keep",
        )(shear_offset, remap_shift, blocks)
        return pl.pallas_call(
            lambda *refs: merge_kernel(cells, peers, rows, *refs),
            out_shape=jax.ShapeDtypeStruct(state.shape, jnp.float32),
            in_specs=[smem] * 2 + [vmem] * 2,
            out_specs=vmem,
            compiler_params=params,
            name="merge",
        )(shear_offset, remap_shift, mine, other)

    placed = (P(None, None, "gx", "gy"), P(), P("gx"), P("gx"))
    return jax.shard_map(
        shards, mesh=mesh, in_specs=placed, out_specs=P(None, None, "gx", "gy"), check_vma=False
    )
```

```python
import jax
import jax.numpy as jnp
from jax import lax
from jax.experimental import pallas as pl
from jax.experimental.pallas import tpu as pltpu
from jax.sharding import PartitionSpec as P

FRAC = 16

ADIABATIC = 5.0 / 3.0
ROTATION = 1.0
SHEAR_RATE = 1.5
MAX_SPEED = 5.0
TIME_STEP = 0.05

LANES = 128
SUBLANES = 8
FIELDS = 8
PLANES = 2
FACE_X = 5
BELOW = 3
ABOVE = 3
TAIL = 4
SENT = 2
HALF_STEP = 0.5 * TIME_STEP
DIFFUSE = 0.5 * MAX_SPEED * TIME_STEP
EDGE = 0.25 * TIME_STEP


def lane_index():
    return lax.broadcasted_iota(jnp.int32, (SUBLANES, LANES), 1)


def row_index():
    return lax.broadcasted_iota(jnp.int32, (SUBLANES, LANES), 0)


def turn_lanes(value, amount):
    return pltpu.roll(value, amount, 1)


def turn_rows(value, amount):
    amount %= SUBLANES
    return pltpu.roll(value, amount, 0) if amount else value


def radial_next(value):
    return turn_rows(value, -1)


def radial_prev(value):
    return turn_rows(value, 1)


def tiles_for(columns):
    return -(-columns // LANES)


def plan(shear, cells, peers):
    rest = shear % cells
    middle = cells // 2
    near = (rest >= middle - 5) & (rest <= middle + 5)
    own = jnp.where(near, middle - 12, middle)
    up = (own - shear) % cells
    down = (own + shear) % cells
    up_hop = (shear - own + up) // cells
    down_hop = (shear + own) // cells
    return own, up, down, up_hop, down_hop


def block_tiles(ref, f, cells):
    value = jnp.concatenate([ref[f, z] for z in range(PLANES)], axis=0)
    tiles = []
    for i in range(0, cells, LANES):
        tile = value[:, i : min(i + LANES, cells)]
        spare = LANES - tile.shape[1]
        if spare:
            tile = jnp.concatenate([tile, jnp.zeros((SUBLANES, spare), tile.dtype)], axis=1)
        tiles.append(tile)
    return tiles


def lay_kernel(cells, state_ref, out_ref):
    for f in range(FIELDS):
        for t, tile in enumerate(block_tiles(state_ref, f, cells)):
            out_ref[f, t] = turn_lanes(tile, cells % LANES)


def pair_kernel(cells, peers, rows, shear_ref, upper_ref, below_ref, joined_ref, up_ref, down_ref):
    place = lax.axis_index("gx")
    places = lax.axis_size("gx")
    own, up, down, _, _ = plan(shear_ref[0], cells, peers)
    up = jnp.where(place == places - 1, up, own)
    down = jnp.where(place == 0, down, own)
    lane = lane_index()
    row = row_index()
    single = tiles_for(cells)
    gap = cells % LANES
    window = single + 1
    for f in range(FIELDS):
        lower = block_tiles(below_ref, f, cells)
        upper = [upper_ref[f, t] for t in range(single)]
        for i in range(single - 1):
            joined_ref[f, i] = lower[i]
        joined_ref[f, single - 1] = jnp.where(lane < gap, lower[-1], upper[0])
        for k in range(single):
            following = upper[min(k + 1, single - 1)]
            joined_ref[f, single + k] = jnp.where(lane < gap, upper[k], following)

    late = row % rows >= SENT
    pairs = FIELDS // 2
    up_tail = down_tail = jnp.zeros((SUBLANES, LANES), jnp.float32)

    def tail(tile, index, so_far):
        return jnp.where(lane // TAIL == index, turn_lanes(tile, index * TAIL), so_far)

    for pair in range(pairs):
        ups = [cut_window(joined_ref, 2 * pair + i, up, window) for i in range(2)]
        downs = [cut_window(joined_ref, 2 * pair + i, down, window) for i in range(2)]
        ups = [jnp.where(late, a, turn_rows(b, -SENT)) for a, b in zip(*ups)]
        downs = [jnp.where(late, turn_rows(b, SENT), a) for a, b in zip(*downs)]
        for t in range(single):
            up_ref[pair * single + t] = ups[t]
            down_ref[pair * single + t] = downs[t]
        up_tail = tail(ups[single], pair, up_tail)
        down_tail = tail(downs[single], pair, down_tail)
    faces = jnp.zeros((SUBLANES, LANES), jnp.float32)
    tiles = cut_window(joined_ref, FACE_X, down, window)
    for t in range(single):
        for z in range(PLANES):
            at = t * PLANES + z
            faces = jnp.where(row == at, turn_rows(tiles[t], at - (z * rows + SENT)), faces)
    down_ref[pairs * single] = faces
    up_ref[pairs * single] = up_tail
    down_ref[pairs * single + 1] = tail(tiles[single], pairs, down_tail)


def cut_window(joined_ref, f, start, count):
    whole = start // LANES
    part = start % LANES
    last = joined_ref.shape[1] - 1
    tiles = [joined_ref[f, jnp.minimum(whole + t, last)] for t in range(count + 1)]
    turned = [turn_lanes(tile, (LANES - part) % LANES) for tile in tiles]
    here = lane_index() < LANES - part
    return [jnp.where(here, turned[t], turned[t + 1]) for t in range(count)]


def cell_terms(state, next_face_x, next_face_y):
    planes = range(PLANES)
    face_z = state[7]
    out = []
    for z in planes:
        density, mom_x, mom_y, mom_z, energy, face_x, face_y = (state[f][z] for f in range(7))
        cen_x = 0.5 * (face_x + next_face_x[z])
        cen_y = 0.5 * (face_y + next_face_y[z])
        cen_z = 0.5 * (face_z[z] + face_z[(z + 1) % PLANES])
        inverse = 1.0 / density
        vel_x, vel_y, vel_z = (mom_x * inverse, mom_y * inverse, mom_z * inverse)
        magnetic = 0.5 * (cen_x * cen_x + cen_y * cen_y + cen_z * cen_z)
        kinetic = 0.5 * (mom_x * vel_x + mom_y * vel_y + mom_z * vel_z)
        pressure = (ADIABATIC - 1.0) * (energy - kinetic - magnetic) + magnetic
        vel_dot = vel_x * cen_x + vel_y * cen_y + vel_z * cen_z
        scaled_p = HALF_STEP * pressure
        total = energy + pressure
        sv_x, sv_y, sv_z = (HALF_STEP * vel_x, HALF_STEP * vel_y, HALF_STEP * vel_z)
        sb_x, sb_y, sb_z = (HALF_STEP * cen_x, HALF_STEP * cen_y, HALF_STEP * cen_z)
        xx = mom_x * sv_x - cen_x * sb_x + scaled_p
        yy = mom_y * sv_y - cen_y * sb_y + scaled_p
        zz = mom_z * sv_z - cen_z * sb_z + scaled_p
        xy = mom_x * sv_y - cen_x * sb_y
        xz = mom_x * sv_z - cen_x * sb_z
        yz = mom_y * sv_z - cen_y * sb_z
        diffuse = [DIFFUSE * state[f][z] for f in range(5)]
        flux_x = [HALF_STEP * mom_x, xx, xy, xz, total * sv_x - sb_x * vel_dot]
        flux_y = [HALF_STEP * mom_y, xy, yy, yz, total * sv_y - sb_y * vel_dot]
        flux_z = [HALF_STEP * mom_z, xz, yz, zz, total * sv_z - sb_z * vel_dot]
        e_z = EDGE * (vel_y * cen_x - vel_x * cen_y)
        pair = e_z + radial_prev(e_z)
        out.append(
            dict(
                diffuse=diffuse,
                along_x=[
                    radial_next(f - d) - radial_prev(f + d) for f, d in zip(flux_x, diffuse)
                ],
                low_y=[turn_lanes(f + d, 1) for f, d in zip(flux_y, diffuse)],
                high_y=[turn_lanes(f - d, LANES - 1) for f, d in zip(flux_y, diffuse)],
                flux_z=flux_z,
                shear=xy,
                e_x=EDGE * (vel_z * cen_y - vel_y * cen_z),
                e_y=EDGE * (vel_x * cen_z - vel_z * cen_x),
                pair=pair,
                low_pair=turn_lanes(pair, 1),
                high_pair=turn_lanes(pair, LANES - 1),
            )
        )
    e_x, e_y = (
        [sum((cell[name] for cell in out[1:]), out[0][name]) for name in ("e_x", "e_y")]
    )
    shared = dict(
        e_x=e_x,
        low_e_x=turn_lanes(e_x, 1),
        high_e_x=turn_lanes(e_x, LANES - 1),
        edge_y=[e_y + radial_prev(e_y)] * PLANES,
        along_x=radial_next(e_y) - radial_prev(e_y),
    )
    return out, shared


def tile_step(state, low, here, high):
    lane = lane_index()
    cells_low, shared_low = low
    cells, shared = here
    cells_high, shared_high = high

    def before(turned_low, turned):
        return jnp.where(lane > 0, turned, turned_low)

    def after(turned, turned_high):
        return jnp.where(lane < LANES - 1, turned, turned_high)

    new = [[None] * PLANES for f in range(FIELDS)]
    faces = [
        [
            (cells[z - 1]["flux_z"][f] + cells[z]["flux_z"][f])
            - (cells[z]["diffuse"][f] - cells[z - 1]["diffuse"][f])
            for f in range(5)
        ]
        for z in range(PLANES)
    ]
    low_e_x = before(shared_low["low_e_x"], shared["low_e_x"])
    along_y = after(shared["high_e_x"], shared_high["high_e_x"]) - low_e_x
    edge_x = [shared["e_x"] + low_e_x] * PLANES
    edge_y = shared["edge_y"]
    for z in range(PLANES):
        cell = cells[z]
        up = (z + 1) % PLANES
        for f in range(5):
            high_y = after(cell["high_y"][f], cells_high[z]["high_y"][f])
            low_y = before(cells_low[z]["low_y"][f], cell["low_y"][f])
            along_z = faces[up][f] - faces[z][f]
            kept = state[f][z] - 4.0 * cell["diffuse"][f]
            new[f][z] = kept - (cell["along_x"][f] + (high_y - low_y) + along_z)
        mom_x, mom_y = (state[1][z], state[2][z])
        new[1][z] = new[1][z] + (TIME_STEP * 2.0 * ROTATION) * mom_y
        new[2][z] = new[2][z] - (TIME_STEP * (2.0 - SHEAR_RATE) * ROTATION) * mom_x
        new[4][z] = new[4][z] + (2.0 * SHEAR_RATE * ROTATION) * cell["shear"]
        low_pair = before(cells_low[z]["low_pair"], cell["low_pair"])
        high_pair = after(cell["high_pair"], cells_high[z]["high_pair"])
        edge_z = cell["pair"] + low_pair
        new[5][z] = state[5][z] + ((edge_y[up] - edge_y[z]) - (high_pair - low_pair))
        new[6][z] = state[6][z] + ((radial_next(edge_z) - edge_z) - (edge_x[up] - edge_x[z]))
        new[7][z] = state[7][z] + (along_y - shared["along_x"])
    return new


def step_kernel(
    cells, peers, rows,
    shear_ref, frac_ref, joined_ref, up_hbm, down_hbm,
    out_ref, state_ref, mid_ref, up_ref, down_ref, up_sem, down_sem,
):
    up_copy = pltpu.make_async_copy(up_hbm, up_ref, up_sem)
    down_copy = pltpu.make_async_copy(down_hbm, down_ref, down_sem)
    up_copy.start()
    down_copy.start()
    own = plan(shear_ref[0], cells, peers)[0]
    lane = lane_index()
    row = row_index()
    single = tiles_for(cells)
    window = single + 1
    pairs = FIELDS // 2

    for f in range(FIELDS):
        for t, tile in enumerate(cut_window(joined_ref, f, own, window)):
            for z in range(PLANES):
                state_ref[t, f, z] = turn_rows(tile, -z * rows)
    up_copy.wait()
    down_copy.wait()
    for f in range(FIELDS):
        pair, second = divmod(f, 2)
        for t in range(window):
            if t < single:
                up = up_ref[pair * single + t]
                down = down_ref[pair * single + t]
            else:
                back = (LANES - pair * TAIL) % LANES
                up = turn_lanes(up_ref[pairs * single], back)
                down = turn_lanes(down_ref[pairs * single + 1], back)
            for z in range(PLANES):
                up_at = z * rows + (0 if second else SENT)
                down_at = z * rows + (SENT if second else 0)
                value = state_ref[t, f, z]
                value = jnp.where(row < rows, value, turn_rows(down, rows - down_at))
                value = jnp.where(row < rows + SENT, value, turn_rows(up, rows + SENT - up_at))
                state_ref[t, f, z] = value
    last = rows + SENT - 1

    def faces_beyond(t, face_x):
        if t < single:
            beyond = [turn_rows(down_ref[pairs * single], last - t * PLANES - z) for z in range(PLANES)]
        else:
            tile = turn_lanes(down_ref[pairs * single + 1], LANES - pairs * TAIL)
            beyond = [turn_rows(tile, last - (z * rows + SENT)) for z in range(PLANES)]
        return [jnp.where(row == last, b, radial_next(face)) for b, face in zip(beyond, face_x)]

    def terms(ref, t, count, beyond):
        state = [[ref[t, f, z] for z in range(PLANES)] for f in range(FIELDS)]
        if beyond:
            next_face_x = faces_beyond(t, state[FACE_X])
        else:
            next_face_x = [radial_next(face) for face in state[FACE_X]]
        next_face_y = []
        for z in range(PLANES):
            here = turn_lanes(state[6][z], LANES - 1)
            if t + 1 < count:
                there = turn_lanes(ref[t + 1, 6, z], LANES - 1)
                here = jnp.where(lane < LANES - 1, here, there)
            next_face_y.append(here)
        return state, cell_terms(state, next_face_x, next_face_y)

    low = here = terms(state_ref, 0, window, True)
    for t in range(window):
        high = terms(state_ref, t + 1, window, True) if t + 1 < window else here
        new = tile_step(here[0], low[1], here[1], high[1])
        for f in range(FIELDS):
            for z in range(PLANES):
                if t < single or f == 6:
                    mid_ref[t, f, z] = new[f][z]
        low, here = here, high

    weight = jnp.zeros((SUBLANES, LANES), jnp.float32)
    for x in range(rows):
        level = (frac_ref[x].astype(jnp.float32) + 0.5) / FRAC
        weight = jnp.where(row == x, level, weight)
    keep = 1.0 - weight
    low = here = terms(mid_ref, 0, window, False)
    low_done = None
    low_moved = None

    def emit(t, moved):
        for f in range(FIELDS):
            out_ref[f, t] = moved[f]

    for t in range(single):
        high = terms(mid_ref, t + 1, window, False) if t + 1 < single else here
        new = tile_step(here[0], low[1], here[1], high[1])
        done = []
        moved = []
        for f in range(FIELDS):
            mixed = []
            turned = []
            for z in range(PLANES):
                value = 0.5 * (state_ref[t, f, z] + new[f][z])
                below = turn_lanes(value, 1)
                turned.append(below)
                if t:
                    below = jnp.where(lane > 0, below, low_done[f][z])
                mixed.append(keep * value + weight * below)
            done.append(turned)
            both = jnp.where(row < rows, mixed[0], turn_rows(mixed[1], rows))
            moved.append(turn_lanes(both, LANES - BELOW))
        if t:
            emit(
                t - 1,
                [jnp.where(lane < LANES - BELOW, a, b) for a, b in zip(low_moved, moved)],
            )
        low_done, low_moved = done, moved
        low, here = here, high
    emit(single - 1, low_moved)


def row_sources(shift, own, cells, peers, target):
    total = cells * peers
    offset = cells - BELOW - own
    shift = (shift + total - offset) % total
    hop = shift // cells
    rest = shift % cells
    upper = (target + 2 * peers - hop) % peers
    lower = (target + 2 * peers - hop - 1) % peers
    return upper, lower, rest


def turned_rows(cells, peers, rows, shift_ref, own, part, target, block_ref, out_ref):
    row = row_index()
    lane = lane_index()
    count = out_ref.shape[1]
    spare = count * LANES - cells
    plans = []
    for x in range(rows):
        upper, lower, rest = row_sources(shift_ref[x], own, cells, peers, target)
        first = upper % 2 == part % 2
        block = jnp.where(first, upper, lower) // 2
        amount = jnp.where(first, rest, rest + spare)
        plans.append((block, amount // LANES, amount % LANES))
    for f in range(FIELDS):
        result = None
        for x, (block, whole, fine) in enumerate(plans):
            tiles = [block_ref[block, f, (t + count - whole) % count] for t in range(count)]
            tiles = [turn_lanes(tile, fine) for tile in tiles]
            tiles = [jnp.where(lane < fine, tiles[t - 1], tiles[t]) for t in range(count)]
            if x == 0:
                result = tiles
            else:
                result = [jnp.where(row % rows == x, a, b) for a, b in zip(tiles, result)]
        for t in range(count):
            out_ref[f, t] = result[t]


def gather_kernel(cells, peers, rows, shear_ref, shift_ref, *refs):
    in_refs, block_ref, out_ref = (refs[:-2], refs[-2], refs[-1])
    part = lax.axis_index("gy")
    own = plan(shear_ref[0], cells, peers)[0]
    for i, ref in enumerate(in_refs):
        block_ref[(part // 2) ^ i] = ref[...]
    turned_rows(cells, peers, rows, shift_ref, own, part, part ^ 1, block_ref, out_ref)


def keep_kernel(cells, peers, rows, shear_ref, shift_ref, block_ref, out_ref):
    part = lax.axis_index("gy")
    own = plan(shear_ref[0], cells, peers)[0]
    turned_rows(cells, peers, rows, shift_ref, own, part, part, block_ref, out_ref)


def merge_kernel(
    cells, peers, rows, shear_ref, shift_ref, mine_ref, other_ref, out_hbm, out_ref, out_sem
):
    part = lax.axis_index("gy")
    own = plan(shear_ref[0], cells, peers)[0]
    row = row_index() % rows
    lane = lane_index()
    count = mine_ref.shape[1]
    border = jnp.zeros((SUBLANES, LANES), jnp.int32)
    first = jnp.zeros((SUBLANES, LANES), jnp.int32)
    for x in range(rows):
        upper, _, rest = row_sources(shift_ref[x], own, cells, peers, part)
        border = jnp.where(row == x, rest, border)
        first = jnp.where(row == x, (upper + part + 1) % 2, first)
    masks = [(lane + t * LANES >= border) == (first == 1) for t in range(count)]
    for f in range(FIELDS):
        tiles = [jnp.where(masks[t], mine_ref[f, t], other_ref[f, t]) for t in range(count)]
        value = jnp.concatenate(tiles, axis=1)[:, :cells]
        for z in range(PLANES):
            out_ref[f, z] = value[z * rows : (z + 1) * rows]
        pltpu.make_async_copy(out_ref.at[f], out_hbm.at[f], out_sem.at[f]).start()
    for f in range(FIELDS):
        pltpu.make_async_copy(out_ref.at[f], out_hbm.at[f], out_sem.at[f]).wait()


def solution(mesh):
    places, peers = (mesh.shape["gx"], mesh.shape["gy"])
    smem = pl.BlockSpec(memory_space=pltpu.SMEM)
    vmem = pl.BlockSpec(memory_space=pltpu.VMEM)
    hbm = pl.BlockSpec(memory_space=pltpu.HBM)
    params = pltpu.CompilerParams(vmem_limit_bytes=8 * 2**20)
    axes = ("gx", "gy")

    def array(*shape):
        return jax.ShapeDtypeStruct(shape + (SUBLANES, LANES), jnp.float32)

    def scratch(*shape):
        return pltpu.VMEM(shape + (SUBLANES, LANES), jnp.float32)

    def device(x, y):
        return x % places * peers + y % peers

    devices = [(x, y) for x in range(places) for y in range(peers)]

    def ghosts(up_hop, down_hop, up, down):
        rise = [(device(x, y), device(x + 1, y + up_hop * (x == places - 1))) for x, y in devices]
        fall = [(device(x, y), device(x - 1, y - down_hop * (x == 0))) for x, y in devices]
        up = lax.ppermute(up, axes, rise)
        return up, lax.ppermute(down, axes, fall)

    def shards(state, shear_offset, remap_shift, frac_index):
        rows, cells = state.shape[2:]
        single = tiles_for(cells)
        double = tiles_for(2 * cells)
        window = tiles_for(BELOW + cells + ABOVE)
        below = lax.ppermute(state, "gy", [(i, (i + 1) % peers) for i in range(peers)])
        upper = pl.pallas_call(
            lambda *refs: lay_kernel(cells, *refs),
            out_shape=array(FIELDS, single),
            in_specs=[vmem],
            out_specs=vmem,
            compiler_params=params,
            name="lay",
        )(state)
        edge = FIELDS // 2 * single + 2
        joined, up, down = pl.pallas_call(
            lambda *refs: pair_kernel(cells, peers, rows, *refs),
            out_shape=[array(FIELDS, double), array(edge), array(edge)],
            in_specs=[smem, vmem, vmem],
            out_specs=[vmem] * 3,
            compiler_params=params,
            name="pair",
        )(shear_offset, upper, below)
        _, _, _, up_hop, down_hop = plan(shear_offset[0], cells, peers)
        branches = [
            lambda u, d, i=i: ghosts(i // 2 + i % 2, i // 2, u, d) for i in range(2 * peers)
        ]
        which = (2 * down_hop + (up_hop - down_hop)) % (2 * peers)
        up, down = lax.switch(which, branches, up, down)
        block = pl.pallas_call(
            lambda *refs: step_kernel(cells, peers, rows, *refs),
            out_shape=array(FIELDS, single),
            in_specs=[smem] * 2 + [vmem] + [hbm] * 2,
            out_specs=vmem,
            scratch_shapes=[scratch(window, FIELDS, PLANES)] * 2
            + [scratch(edge), scratch(edge)]
            + [pltpu.SemaphoreType.DMA] * 2,
            compiler_params=params,
            name="step",
        )(shear_offset, frac_index, joined, up, down)

        def exchange(value, bits):
            return lax.ppermute(value, "gy", [(i, i ^ bits) for i in range(peers)])

        blocks = [block] + [exchange(block, bits) for bits in range(2, peers, 2)]
        blocks, other = pl.pallas_call(
            lambda *refs: gather_kernel(cells, peers, rows, *refs),
            out_shape=[array(peers // 2, FIELDS, single), array(FIELDS, single)],
            in_specs=[smem] * 2 + [vmem] * (peers // 2),
            out_specs=[vmem] * 2,
            compiler_params=params,
            name="gather",
        )(shear_offset, remap_shift, *blocks)
        other = exchange(other, 1)
        mine = pl.pallas_call(
            lambda *refs: keep_kernel(cells, peers, rows, *refs),
            out_shape=array(FIELDS, single),
            in_specs=[smem] * 2 + [vmem],
            out_specs=vmem,
            compiler_params=params,
            name="keep",
        )(shear_offset, remap_shift, blocks)
        return pl.pallas_call(
            lambda *refs: merge_kernel(cells, peers, rows, *refs),
            out_shape=jax.ShapeDtypeStruct(state.shape, jnp.float32),
            in_specs=[smem] * 2 + [vmem] * 2,
            out_specs=hbm,
            scratch_shapes=[
                pltpu.VMEM(state.shape, jnp.float32),
                pltpu.SemaphoreType.DMA((FIELDS,)),
            ],
            compiler_params=params,
            name="merge",
        )(shear_offset, remap_shift, mine, other)

    placed = (P(None, None, "gx", "gy"), P(), P("gx"), P("gx"))
    return jax.shard_map(
        shards, mesh=mesh, in_specs=placed, out_specs=P(None, None, "gx", "gy"), check_vma=False
    )
```

```python
import jax
import jax.numpy as jnp
from jax import lax
from jax.experimental import pallas as pl
from jax.experimental.pallas import tpu as pltpu
from jax.sharding import PartitionSpec as P

FRAC = 16

ADIABATIC = 5.0 / 3.0
ROTATION = 1.0
SHEAR_RATE = 1.5
MAX_SPEED = 5.0
TIME_STEP = 0.05

LANES = 128
LANE_BITS = 7
SUBLANES = 8
FIELDS = 8
PLANES = 2
FACE_X = 5
BELOW = 3
ABOVE = 3
TAIL = 4
SENT = 2
HALF_STEP = 0.5 * TIME_STEP
DIFFUSE = 0.5 * MAX_SPEED * TIME_STEP
EDGE = 0.25 * TIME_STEP


def lane_index():
    return lax.broadcasted_iota(jnp.int32, (SUBLANES, LANES), 1)


def row_index():
    return lax.broadcasted_iota(jnp.int32, (SUBLANES, LANES), 0)


def turn_lanes(value, amount):
    return pltpu.roll(value, amount, 1)


def turn_rows(value, amount):
    amount %= SUBLANES
    return pltpu.roll(value, amount, 0) if amount else value


def radial_next(value):
    return turn_rows(value, -1)


def radial_prev(value):
    return turn_rows(value, 1)


def tiles_for(columns):
    return -(-columns // LANES)


def hops_of(columns, cells, peers):
    hops = sum(jnp.where(columns >= k * cells, 1, 0) for k in range(1, peers))
    return hops, columns - hops * cells


def plan(shear, cells, peers):
    hops, rest = hops_of(shear, cells, peers)
    middle = cells // 2
    near = (rest >= middle - 5) & (rest <= middle + 5)
    own = jnp.where(near, middle - 12, middle)
    up_hop = jnp.where(rest > own, 1, 0)
    down_hop = jnp.where(rest + own >= cells, 1, 0)
    up = own - rest + up_hop * cells
    down = own + rest - down_hop * cells
    return own, up, down, hops + up_hop, hops + down_hop


def block_tiles(ref, f, cells):
    value = jnp.concatenate([ref[f, z] for z in range(PLANES)], axis=0)
    tiles = []
    for i in range(0, cells, LANES):
        tile = value[:, i : min(i + LANES, cells)]
        spare = LANES - tile.shape[1]
        if spare:
            tile = jnp.concatenate([tile, jnp.zeros((SUBLANES, spare), tile.dtype)], axis=1)
        tiles.append(tile)
    return tiles


def lay_kernel(cells, frac_ref, state_ref, out_ref, weight_ref):
    weight = jnp.zeros((SUBLANES, LANES), jnp.float32)
    for x in range(state_ref.shape[2]):
        level = (frac_ref[x].astype(jnp.float32) + 0.5) / FRAC
        weight = jnp.where(row_index() == x, level, weight)
    weight_ref[...] = weight
    for f in range(FIELDS):
        for t, tile in enumerate(block_tiles(state_ref, f, cells)):
            out_ref[f, t] = turn_lanes(tile, cells % LANES)


def pair_kernel(cells, peers, rows, shear_ref, upper_ref, below_ref, joined_ref, up_ref, down_ref):
    place = lax.axis_index("gx")
    places = lax.axis_size("gx")
    own, up, down, _, _ = plan(shear_ref[0], cells, peers)
    up = jnp.where(place == places - 1, up, own)
    down = jnp.where(place == 0, down, own)
    lane = lane_index()
    row = row_index()
    single = tiles_for(cells)
    gap = cells % LANES
    window = single + 1
    for f in range(FIELDS):
        lower = block_tiles(below_ref, f, cells)
        upper = [upper_ref[f, t] for t in range(single)]
        for i in range(single - 1):
            joined_ref[f, i] = lower[i]
        joined_ref[f, single - 1] = jnp.where(lane < gap, lower[-1], upper[0])
        for k in range(single):
            following = upper[min(k + 1, single - 1)]
            joined_ref[f, single + k] = jnp.where(lane < gap, upper[k], following)

    late = row % rows >= SENT
    pairs = FIELDS // 2
    up_tail = down_tail = jnp.zeros((SUBLANES, LANES), jnp.float32)

    def tail(tile, index, so_far):
        return jnp.where(lane // TAIL == index, turn_lanes(tile, index * TAIL), so_far)

    for pair in range(pairs):
        ups = [cut_window(joined_ref, 2 * pair + i, up, window) for i in range(2)]
        downs = [cut_window(joined_ref, 2 * pair + i, down, window) for i in range(2)]
        ups = [jnp.where(late, a, turn_rows(b, -SENT)) for a, b in zip(*ups)]
        downs = [jnp.where(late, turn_rows(b, SENT), a) for a, b in zip(*downs)]
        for t in range(single):
            up_ref[pair * single + t] = ups[t]
            down_ref[pair * single + t] = downs[t]
        up_tail = tail(ups[single], pair, up_tail)
        down_tail = tail(downs[single], pair, down_tail)
    faces = jnp.zeros((SUBLANES, LANES), jnp.float32)
    tiles = cut_window(joined_ref, FACE_X, down, window)
    for t in range(single):
        for z in range(PLANES):
            at = t * PLANES + z
            faces = jnp.where(row == at, turn_rows(tiles[t], at - (z * rows + SENT)), faces)
    down_ref[pairs * single] = faces
    up_ref[pairs * single] = up_tail
    down_ref[pairs * single + 1] = tail(tiles[single], pairs, down_tail)


def cut_window(joined_ref, f, start, count):
    whole = start >> LANE_BITS
    part = start & (LANES - 1)
    last = joined_ref.shape[1] - 1
    tiles = [joined_ref[f, jnp.minimum(whole + t, last)] for t in range(count + 1)]
    turned = [turn_lanes(tile, (LANES - part) & (LANES - 1)) for tile in tiles]
    here = lane_index() < LANES - part
    return [jnp.where(here, turned[t], turned[t + 1]) for t in range(count)]


def cell_terms(state, next_face_x, next_face_y):
    planes = range(PLANES)
    face_z = state[7]
    out = []
    for z in planes:
        density, mom_x, mom_y, mom_z, energy, face_x, face_y = (state[f][z] for f in range(7))
        cen_x = 0.5 * (face_x + next_face_x[z])
        cen_y = 0.5 * (face_y + next_face_y[z])
        cen_z = 0.5 * (face_z[z] + face_z[(z + 1) % PLANES])
        inverse = 1.0 / density
        vel_x, vel_y, vel_z = (mom_x * inverse, mom_y * inverse, mom_z * inverse)
        magnetic = 0.5 * (cen_x * cen_x + cen_y * cen_y + cen_z * cen_z)
        kinetic = 0.5 * (mom_x * vel_x + mom_y * vel_y + mom_z * vel_z)
        pressure = (ADIABATIC - 1.0) * (energy - kinetic - magnetic) + magnetic
        vel_dot = vel_x * cen_x + vel_y * cen_y + vel_z * cen_z
        scaled_p = HALF_STEP * pressure
        total = energy + pressure
        sv_x, sv_y, sv_z = (HALF_STEP * vel_x, HALF_STEP * vel_y, HALF_STEP * vel_z)
        sb_x, sb_y, sb_z = (HALF_STEP * cen_x, HALF_STEP * cen_y, HALF_STEP * cen_z)
        xx = mom_x * sv_x - cen_x * sb_x + scaled_p
        yy = mom_y * sv_y - cen_y * sb_y + scaled_p
        zz = mom_z * sv_z - cen_z * sb_z + scaled_p
        xy = mom_x * sv_y - cen_x * sb_y
        xz = mom_x * sv_z - cen_x * sb_z
        yz = mom_y * sv_z - cen_y * sb_z
        diffuse = [DIFFUSE * state[f][z] for f in range(5)]
        flux_x = [HALF_STEP * mom_x, xx, xy, xz, total * sv_x - sb_x * vel_dot]
        flux_y = [HALF_STEP * mom_y, xy, yy, yz, total * sv_y - sb_y * vel_dot]
        flux_z = [HALF_STEP * mom_z, xz, yz, zz, total * sv_z - sb_z * vel_dot]
        e_z = EDGE * (vel_y * cen_x - vel_x * cen_y)
        pair = e_z + radial_prev(e_z)
        out.append(
            dict(
                diffuse=diffuse,
                along_x=[
                    radial_next(f - d) - radial_prev(f + d) for f, d in zip(flux_x, diffuse)
                ],
                low_y=[turn_lanes(f + d, 1) for f, d in zip(flux_y, diffuse)],
                high_y=[turn_lanes(f - d, LANES - 1) for f, d in zip(flux_y, diffuse)],
                flux_z=flux_z,
                shear=xy,
                e_x=EDGE * (vel_z * cen_y - vel_y * cen_z),
                e_y=EDGE * (vel_x * cen_z - vel_z * cen_x),
                pair=pair,
                low_pair=turn_lanes(pair, 1),
                high_pair=turn_lanes(pair, LANES - 1),
            )
        )
    e_x, e_y = (
        [sum((cell[name] for cell in out[1:]), out[0][name]) for name in ("e_x", "e_y")]
    )
    shared = dict(
        e_x=e_x,
        low_e_x=turn_lanes(e_x, 1),
        high_e_x=turn_lanes(e_x, LANES - 1),
        edge_y=[e_y + radial_prev(e_y)] * PLANES,
        along_x=radial_next(e_y) - radial_prev(e_y),
    )
    return out, shared


def tile_step(state, low, here, high):
    lane = lane_index()
    cells_low, shared_low = low
    cells, shared = here
    cells_high, shared_high = high

    def before(turned_low, turned):
        return jnp.where(lane > 0, turned, turned_low)

    def after(turned, turned_high):
        return jnp.where(lane < LANES - 1, turned, turned_high)

    new = [[None] * PLANES for f in range(FIELDS)]
    faces = [
        [
            (cells[z - 1]["flux_z"][f] + cells[z]["flux_z"][f])
            - (cells[z]["diffuse"][f] - cells[z - 1]["diffuse"][f])
            for f in range(5)
        ]
        for z in range(PLANES)
    ]
    low_e_x = before(shared_low["low_e_x"], shared["low_e_x"])
    along_y = after(shared["high_e_x"], shared_high["high_e_x"]) - low_e_x
    edge_x = [shared["e_x"] + low_e_x] * PLANES
    edge_y = shared["edge_y"]
    for z in range(PLANES):
        cell = cells[z]
        up = (z + 1) % PLANES
        for f in range(5):
            high_y = after(cell["high_y"][f], cells_high[z]["high_y"][f])
            low_y = before(cells_low[z]["low_y"][f], cell["low_y"][f])
            along_z = faces[up][f] - faces[z][f]
            kept = state[f][z] - 4.0 * cell["diffuse"][f]
            new[f][z] = kept - (cell["along_x"][f] + (high_y - low_y) + along_z)
        mom_x, mom_y = (state[1][z], state[2][z])
        new[1][z] = new[1][z] + (TIME_STEP * 2.0 * ROTATION) * mom_y
        new[2][z] = new[2][z] - (TIME_STEP * (2.0 - SHEAR_RATE) * ROTATION) * mom_x
        new[4][z] = new[4][z] + (2.0 * SHEAR_RATE * ROTATION) * cell["shear"]
        low_pair = before(cells_low[z]["low_pair"], cell["low_pair"])
        high_pair = after(cell["high_pair"], cells_high[z]["high_pair"])
        edge_z = cell["pair"] + low_pair
        new[5][z] = state[5][z] + ((edge_y[up] - edge_y[z]) - (high_pair - low_pair))
        new[6][z] = state[6][z] + ((radial_next(edge_z) - edge_z) - (edge_x[up] - edge_x[z]))
        new[7][z] = state[7][z] + (along_y - shared["along_x"])
    return new


def step_kernel(
    cells, peers, rows,
    shear_ref, weight_ref, joined_ref, up_hbm, down_hbm,
    out_ref, state_ref, mid_ref, up_ref, down_ref, up_sem, down_sem,
):
    up_copy = pltpu.make_async_copy(up_hbm, up_ref, up_sem)
    down_copy = pltpu.make_async_copy(down_hbm, down_ref, down_sem)
    up_copy.start()
    down_copy.start()
    own = plan(shear_ref[0], cells, peers)[0]
    lane = lane_index()
    row = row_index()
    single = tiles_for(cells)
    window = single + 1
    pairs = FIELDS // 2

    for f in range(FIELDS):
        for t, tile in enumerate(cut_window(joined_ref, f, own, window)):
            for z in range(PLANES):
                state_ref[t, f, z] = turn_rows(tile, -z * rows)
    up_copy.wait()
    down_copy.wait()
    for f in range(FIELDS):
        pair, second = divmod(f, 2)
        for t in range(window):
            if t < single:
                up = up_ref[pair * single + t]
                down = down_ref[pair * single + t]
            else:
                back = (LANES - pair * TAIL) % LANES
                up = turn_lanes(up_ref[pairs * single], back)
                down = turn_lanes(down_ref[pairs * single + 1], back)
            for z in range(PLANES):
                up_at = z * rows + (0 if second else SENT)
                down_at = z * rows + (SENT if second else 0)
                value = state_ref[t, f, z]
                value = jnp.where(row < rows, value, turn_rows(down, rows - down_at))
                value = jnp.where(row < rows + SENT, value, turn_rows(up, rows + SENT - up_at))
                state_ref[t, f, z] = value
    last = rows + SENT - 1

    def faces_beyond(t, face_x):
        if t < single:
            beyond = [turn_rows(down_ref[pairs * single], last - t * PLANES - z) for z in range(PLANES)]
        else:
            tile = turn_lanes(down_ref[pairs * single + 1], LANES - pairs * TAIL)
            beyond = [turn_rows(tile, last - (z * rows + SENT)) for z in range(PLANES)]
        return [jnp.where(row == last, b, radial_next(face)) for b, face in zip(beyond, face_x)]

    def terms(ref, t, count, beyond):
        state = [[ref[t, f, z] for z in range(PLANES)] for f in range(FIELDS)]
        if beyond:
            next_face_x = faces_beyond(t, state[FACE_X])
        else:
            next_face_x = [radial_next(face) for face in state[FACE_X]]
        next_face_y = []
        for z in range(PLANES):
            here = turn_lanes(state[6][z], LANES - 1)
            if t + 1 < count:
                there = turn_lanes(ref[t + 1, 6, z], LANES - 1)
                here = jnp.where(lane < LANES - 1, here, there)
            next_face_y.append(here)
        return state, cell_terms(state, next_face_x, next_face_y)

    low = here = terms(state_ref, 0, window, True)
    for t in range(window):
        high = terms(state_ref, t + 1, window, True) if t + 1 < window else here
        new = tile_step(here[0], low[1], here[1], high[1])
        for f in range(FIELDS):
            for z in range(PLANES):
                if t < single or f == 6:
                    mid_ref[t, f, z] = new[f][z]
        low, here = here, high

    weight = weight_ref[...]
    keep = 1.0 - weight
    low = here = terms(mid_ref, 0, window, False)
    low_done = None
    low_moved = None

    def emit(t, moved):
        for f in range(FIELDS):
            out_ref[f, t] = moved[f]

    for t in range(single):
        high = terms(mid_ref, t + 1, window, False) if t + 1 < single else here
        new = tile_step(here[0], low[1], here[1], high[1])
        done = []
        moved = []
        for f in range(FIELDS):
            mixed = []
            turned = []
            for z in range(PLANES):
                value = 0.5 * (state_ref[t, f, z] + new[f][z])
                below = turn_lanes(value, 1)
                turned.append(below)
                if t:
                    below = jnp.where(lane > 0, below, low_done[f][z])
                mixed.append(keep * value + weight * below)
            done.append(turned)
            both = jnp.where(row < rows, mixed[0], turn_rows(mixed[1], rows))
            moved.append(turn_lanes(both, LANES - BELOW))
        if t:
            emit(
                t - 1,
                [jnp.where(lane < LANES - BELOW, a, b) for a, b in zip(low_moved, moved)],
            )
        low_done, low_moved = done, moved
        low, here = here, high
    emit(single - 1, low_moved)


def row_sources(shift, own, cells, peers, target):
    shift = shift - (cells - BELOW - own)
    shift = jnp.where(shift < 0, shift + cells * peers, shift)
    hops, rest = hops_of(shift, cells, peers)
    upper = (target + peers - hops) & (peers - 1)
    lower = (target + peers - 1 - hops) & (peers - 1)
    return upper, lower, rest


def turned_rows(cells, peers, rows, shift_ref, own, part, target, block_ref, out_ref):
    row = row_index()
    lane = lane_index()
    count = out_ref.shape[1]
    spare = count * LANES - cells
    plans = []
    for x in range(rows):
        upper, lower, rest = row_sources(shift_ref[x], own, cells, peers, target)
        first = ((upper ^ part) & 1) == 0
        block = jnp.where(first, upper, lower) >> 1
        amount = jnp.where(first, rest, rest + spare)
        whole = amount >> LANE_BITS
        sources = [t - whole for t in range(count)]
        sources = [jnp.where(t < 0, t + count, t) for t in sources]
        plans.append((block, sources, amount & (LANES - 1)))
    for f in range(FIELDS):
        result = None
        for x, (block, sources, fine) in enumerate(plans):
            tiles = [block_ref[block, f, t] for t in sources]
            tiles = [turn_lanes(tile, fine) for tile in tiles]
            tiles = [jnp.where(lane < fine, tiles[t - 1], tiles[t]) for t in range(count)]
            if x == 0:
                result = tiles
            else:
                result = [jnp.where(row % rows == x, a, b) for a, b in zip(tiles, result)]
        for t in range(count):
            out_ref[f, t] = result[t]


def gather_kernel(cells, peers, rows, shear_ref, shift_ref, *refs):
    in_refs, block_ref, out_ref = (refs[:-2], refs[-2], refs[-1])
    part = lax.axis_index("gy")
    own = plan(shear_ref[0], cells, peers)[0]
    for i, ref in enumerate(reversed(in_refs)):
        block_ref[(part >> 1) ^ i] = ref[...]
    turned_rows(cells, peers, rows, shift_ref, own, part, part ^ 1, block_ref, out_ref)


def keep_kernel(cells, peers, rows, shear_ref, shift_ref, block_ref, out_ref):
    part = lax.axis_index("gy")
    own = plan(shear_ref[0], cells, peers)[0]
    turned_rows(cells, peers, rows, shift_ref, own, part, part, block_ref, out_ref)


def merge_kernel(
    cells, peers, rows, shear_ref, shift_ref, mine_ref, other_ref, out_hbm, out_ref, out_sem
):
    part = lax.axis_index("gy")
    own = plan(shear_ref[0], cells, peers)[0]
    row = row_index() % rows
    lane = lane_index()
    count = mine_ref.shape[1]
    border = jnp.zeros((SUBLANES, LANES), jnp.int32)
    first = jnp.zeros((SUBLANES, LANES), jnp.int32)
    for x in range(rows):
        upper, _, rest = row_sources(shift_ref[x], own, cells, peers, part)
        border = jnp.where(row == x, rest, border)
        first = jnp.where(row == x, ((upper ^ part) & 1) ^ 1, first)
    masks = [(lane + t * LANES >= border) == (first == 1) for t in range(count)]
    for f in range(FIELDS):
        tiles = [jnp.where(masks[t], mine_ref[f, t], other_ref[f, t]) for t in range(count)]
        value = jnp.concatenate(tiles, axis=1)[:, :cells]
        for z in range(PLANES):
            out_ref[f, z] = value[z * rows : (z + 1) * rows]
        pltpu.make_async_copy(out_ref.at[f], out_hbm.at[f], out_sem.at[f]).start()
    for f in range(FIELDS):
        pltpu.make_async_copy(out_ref.at[f], out_hbm.at[f], out_sem.at[f]).wait()


def solution(mesh):
    places, peers = (mesh.shape["gx"], mesh.shape["gy"])
    smem = pl.BlockSpec(memory_space=pltpu.SMEM)
    vmem = pl.BlockSpec(memory_space=pltpu.VMEM)
    hbm = pl.BlockSpec(memory_space=pltpu.HBM)
    params = pltpu.CompilerParams(vmem_limit_bytes=8 * 2**20)
    axes = ("gx", "gy")

    def array(*shape):
        return jax.ShapeDtypeStruct(shape + (SUBLANES, LANES), jnp.float32)

    def scratch(*shape):
        return pltpu.VMEM(shape + (SUBLANES, LANES), jnp.float32)

    def device(x, y):
        return x % places * peers + y % peers

    devices = [(x, y) for x in range(places) for y in range(peers)]

    def ghosts(up_hop, down_hop, up, down):
        rise = [(device(x, y), device(x + 1, y + up_hop * (x == places - 1))) for x, y in devices]
        fall = [(device(x, y), device(x - 1, y - down_hop * (x == 0))) for x, y in devices]
        up = lax.ppermute(up, axes, rise)
        return up, lax.ppermute(down, axes, fall)

    def shards(state, shear_offset, remap_shift, frac_index):
        rows, cells = state.shape[2:]
        single = tiles_for(cells)
        double = tiles_for(2 * cells)
        window = tiles_for(BELOW + cells + ABOVE)
        below = lax.ppermute(state, "gy", [(i, (i + 1) % peers) for i in range(peers)])
        upper, weight = pl.pallas_call(
            lambda *refs: lay_kernel(cells, *refs),
            out_shape=[array(FIELDS, single), array()],
            in_specs=[smem, vmem],
            out_specs=[vmem] * 2,
            compiler_params=params,
            name="lay",
        )(frac_index, state)
        edge = FIELDS // 2 * single + 2
        joined, up, down = pl.pallas_call(
            lambda *refs: pair_kernel(cells, peers, rows, *refs),
            out_shape=[array(FIELDS, double), array(edge), array(edge)],
            in_specs=[smem, vmem, vmem],
            out_specs=[vmem] * 3,
            compiler_params=params,
            name="pair",
        )(shear_offset, upper, below)
        _, _, _, up_hop, down_hop = plan(shear_offset[0], cells, peers)
        branches = [
            lambda u, d, i=i: ghosts(i // 2 + i % 2, i // 2, u, d) for i in range(2 * peers)
        ]
        which = (down_hop + up_hop) & (2 * peers - 1)
        up, down = lax.switch(which, branches, up, down)
        block = pl.pallas_call(
            lambda *refs: step_kernel(cells, peers, rows, *refs),
            out_shape=array(FIELDS, single),
            in_specs=[smem] + [vmem] * 2 + [hbm] * 2,
            out_specs=vmem,
            scratch_shapes=[scratch(window, FIELDS, PLANES)] * 2
            + [scratch(edge), scratch(edge)]
            + [pltpu.SemaphoreType.DMA] * 2,
            compiler_params=params,
            name="step",
        )(shear_offset, weight, joined, up, down)

        def exchange(value, bits):
            return lax.ppermute(value, "gy", [(i, i ^ bits) for i in range(peers)])

        far = [exchange(block, bits) for bits in range(peers - 2, 0, -2)]
        blocks = far + [block]
        blocks, other = pl.pallas_call(
            lambda *refs: gather_kernel(cells, peers, rows, *refs),
            out_shape=[array(peers // 2, FIELDS, single), array(FIELDS, single)],
            in_specs=[smem] * 2 + [vmem] * (peers // 2),
            out_specs=[vmem] * 2,
            compiler_params=params,
            name="gather",
        )(shear_offset, remap_shift, *blocks)
        other = exchange(other, 1)
        mine = pl.pallas_call(
            lambda *refs: keep_kernel(cells, peers, rows, *refs),
            out_shape=array(FIELDS, single),
            in_specs=[smem] * 2 + [vmem],
            out_specs=vmem,
            compiler_params=params,
            name="keep",
        )(shear_offset, remap_shift, blocks)
        return pl.pallas_call(
            lambda *refs: merge_kernel(cells, peers, rows, *refs),
            out_shape=jax.ShapeDtypeStruct(state.shape, jnp.float32),
            in_specs=[smem] * 2 + [vmem] * 2,
            out_specs=hbm,
            scratch_shapes=[
                pltpu.VMEM(state.shape, jnp.float32),
                pltpu.SemaphoreType.DMA((FIELDS,)),
            ],
            compiler_params=params,
            name="merge",
        )(shear_offset, remap_shift, mine, other)

    placed = (P(None, None, "gx", "gy"), P(), P("gx"), P("gx"))
    return jax.shard_map(
        shards, mesh=mesh, in_specs=placed, out_specs=P(None, None, "gx", "gy"), check_vma=False
    )
```

```python
import jax
import jax.numpy as jnp
from jax import lax
from jax.experimental import pallas as pl
from jax.experimental.pallas import tpu as pltpu
from jax.sharding import PartitionSpec as P

FRAC = 16

ADIABATIC = 5.0 / 3.0
ROTATION = 1.0
SHEAR_RATE = 1.5
MAX_SPEED = 5.0
TIME_STEP = 0.05

LANES = 128
LANE_BITS = 7
SUBLANES = 8
FIELDS = 8
PLANES = 2
FACE_X = 5
BELOW = 3
ABOVE = 3
SENT = 2
HALF_STEP = 0.5 * TIME_STEP
DIFFUSE = 0.5 * MAX_SPEED * TIME_STEP
EDGE = 0.25 * TIME_STEP


def lane_index():
    return lax.broadcasted_iota(jnp.int32, (SUBLANES, LANES), 1)


def row_index():
    return lax.broadcasted_iota(jnp.int32, (SUBLANES, LANES), 0)


def turn_lanes(value, amount):
    return pltpu.roll(value, amount, 1)


def turn_rows(value, amount):
    amount %= SUBLANES
    return pltpu.roll(value, amount, 0) if amount else value


def radial_next(value):
    return turn_rows(value, -1)


def radial_prev(value):
    return turn_rows(value, 1)


def tiles_for(columns):
    return -(-columns // LANES)


def hops_of(columns, cells, peers):
    hops = sum(jnp.where(columns >= k * cells, 1, 0) for k in range(1, peers))
    return hops, columns - hops * cells


def plan(shear, cells, peers):
    hops, rest = hops_of(shear, cells, peers)
    middle = cells // 2
    near = (rest >= middle - 5) & (rest <= middle + 5)
    own = jnp.where(near, middle - 12, middle)
    up_hop = jnp.where(rest > own, 1, 0)
    down_hop = jnp.where(rest + own >= cells, 1, 0)
    up = own - rest + up_hop * cells
    down = own + rest - down_hop * cells
    return own, up, down, hops + up_hop, hops + down_hop


def block_tiles(ref, f, cells):
    value = jnp.concatenate([ref[f, z] for z in range(PLANES)], axis=0)
    tiles = []
    for i in range(0, cells, LANES):
        tile = value[:, i : min(i + LANES, cells)]
        spare = LANES - tile.shape[1]
        if spare:
            tile = jnp.concatenate([tile, jnp.zeros((SUBLANES, spare), tile.dtype)], axis=1)
        tiles.append(tile)
    return tiles


def join_tiles(lower, upper, cells, put):
    gap = cells % LANES
    lane = lane_index()
    single = len(lower)
    upper = [turn_lanes(tile, gap) for tile in upper]
    for i in range(single - 1):
        put(i, lower[i])
    put(single - 1, jnp.where(lane < gap, lower[-1], upper[0]))
    for k in range(single):
        put(single + k, jnp.where(lane < gap, upper[k], upper[min(k + 1, single - 1)]))


def cut_window(joined_ref, f, start, count):
    whole = start >> LANE_BITS
    part = start & (LANES - 1)
    last = joined_ref.shape[1] - 1
    tiles = [joined_ref[f, jnp.minimum(whole + t, last)] for t in range(count + 1)]
    turned = [turn_lanes(tile, (LANES - part) & (LANES - 1)) for tile in tiles]
    here = lane_index() < LANES - part
    return [jnp.where(here, turned[t], turned[t + 1]) for t in range(count)]


def edge_kernel(cells, rows, state_ref, up_ref, down_ref):
    row = row_index()
    late = row % rows >= SENT
    single = tiles_for(cells)
    faces = jnp.zeros((SUBLANES, LANES), jnp.float32)
    for pair in range(FIELDS // 2):
        first, second = (block_tiles(state_ref, 2 * pair + i, cells) for i in range(2))
        for t in range(single):
            up_ref[pair * single + t] = jnp.where(late, first[t], turn_rows(second[t], -SENT))
            down_ref[pair * single + t] = jnp.where(late, turn_rows(second[t], SENT), first[t])
        if FACE_X // 2 == pair:
            for t, tile in enumerate((first, second)[FACE_X % 2]):
                for z in range(PLANES):
                    at = t * PLANES + z
                    faces = jnp.where(row == at, turn_rows(tile, at - (z * rows + SENT)), faces)
    down_ref[FIELDS // 2 * single] = faces


def join_kernel(
    cells, peers, shear_ref, frac_ref, state_ref, below_ref, out_ref, weight_ref, joined_ref
):
    weight = jnp.zeros((SUBLANES, LANES), jnp.float32)
    for x in range(state_ref.shape[2]):
        level = (frac_ref[x].astype(jnp.float32) + 0.5) / FRAC
        weight = jnp.where(row_index() == x, level, weight)
    weight_ref[...] = weight
    own = plan(shear_ref[0], cells, peers)[0]
    for f in range(FIELDS):

        def put(i, tile):
            joined_ref[f, i] = tile

        lower, upper = (block_tiles(ref, f, cells) for ref in (below_ref, state_ref))
        join_tiles(lower, upper, cells, put)
        for t, tile in enumerate(cut_window(joined_ref, f, own, out_ref.shape[1])):
            out_ref[f, t] = tile


def cell_terms(state, next_face_x, next_face_y):
    planes = range(PLANES)
    face_z = state[7]
    out = []
    for z in planes:
        density, mom_x, mom_y, mom_z, energy, face_x, face_y = (state[f][z] for f in range(7))
        cen_x = 0.5 * (face_x + next_face_x[z])
        cen_y = 0.5 * (face_y + next_face_y[z])
        cen_z = 0.5 * (face_z[z] + face_z[(z + 1) % PLANES])
        inverse = 1.0 / density
        vel_x, vel_y, vel_z = (mom_x * inverse, mom_y * inverse, mom_z * inverse)
        magnetic = 0.5 * (cen_x * cen_x + cen_y * cen_y + cen_z * cen_z)
        kinetic = 0.5 * (mom_x * vel_x + mom_y * vel_y + mom_z * vel_z)
        pressure = (ADIABATIC - 1.0) * (energy - kinetic - magnetic) + magnetic
        vel_dot = vel_x * cen_x + vel_y * cen_y + vel_z * cen_z
        scaled_p = HALF_STEP * pressure
        total = energy + pressure
        sv_x, sv_y, sv_z = (HALF_STEP * vel_x, HALF_STEP * vel_y, HALF_STEP * vel_z)
        sb_x, sb_y, sb_z = (HALF_STEP * cen_x, HALF_STEP * cen_y, HALF_STEP * cen_z)
        xx = mom_x * sv_x - cen_x * sb_x + scaled_p
        yy = mom_y * sv_y - cen_y * sb_y + scaled_p
        zz = mom_z * sv_z - cen_z * sb_z + scaled_p
        xy = mom_x * sv_y - cen_x * sb_y
        xz = mom_x * sv_z - cen_x * sb_z
        yz = mom_y * sv_z - cen_y * sb_z
        diffuse = [DIFFUSE * state[f][z] for f in range(5)]
        flux_x = [HALF_STEP * mom_x, xx, xy, xz, total * sv_x - sb_x * vel_dot]
        flux_y = [HALF_STEP * mom_y, xy, yy, yz, total * sv_y - sb_y * vel_dot]
        flux_z = [HALF_STEP * mom_z, xz, yz, zz, total * sv_z - sb_z * vel_dot]
        e_z = EDGE * (vel_y * cen_x - vel_x * cen_y)
        pair = e_z + radial_prev(e_z)
        out.append(
            dict(
                diffuse=diffuse,
                along_x=[
                    radial_next(f - d) - radial_prev(f + d) for f, d in zip(flux_x, diffuse)
                ],
                low_y=[turn_lanes(f + d, 1) for f, d in zip(flux_y, diffuse)],
                high_y=[turn_lanes(f - d, LANES - 1) for f, d in zip(flux_y, diffuse)],
                flux_z=flux_z,
                shear=xy,
                e_x=EDGE * (vel_z * cen_y - vel_y * cen_z),
                e_y=EDGE * (vel_x * cen_z - vel_z * cen_x),
                pair=pair,
                low_pair=turn_lanes(pair, 1),
                high_pair=turn_lanes(pair, LANES - 1),
            )
        )
    e_x, e_y = (
        [sum((cell[name] for cell in out[1:]), out[0][name]) for name in ("e_x", "e_y")]
    )
    shared = dict(
        e_x=e_x,
        low_e_x=turn_lanes(e_x, 1),
        high_e_x=turn_lanes(e_x, LANES - 1),
        edge_y=[e_y + radial_prev(e_y)] * PLANES,
        along_x=radial_next(e_y) - radial_prev(e_y),
    )
    return out, shared


def tile_step(state, low, here, high):
    lane = lane_index()
    cells_low, shared_low = low
    cells, shared = here
    cells_high, shared_high = high

    def before(turned_low, turned):
        return jnp.where(lane > 0, turned, turned_low)

    def after(turned, turned_high):
        return jnp.where(lane < LANES - 1, turned, turned_high)

    new = [[None] * PLANES for f in range(FIELDS)]
    faces = [
        [
            (cells[z - 1]["flux_z"][f] + cells[z]["flux_z"][f])
            - (cells[z]["diffuse"][f] - cells[z - 1]["diffuse"][f])
            for f in range(5)
        ]
        for z in range(PLANES)
    ]
    low_e_x = before(shared_low["low_e_x"], shared["low_e_x"])
    along_y = after(shared["high_e_x"], shared_high["high_e_x"]) - low_e_x
    edge_x = [shared["e_x"] + low_e_x] * PLANES
    edge_y = shared["edge_y"]
    for z in range(PLANES):
        cell = cells[z]
        up = (z + 1) % PLANES
        for f in range(5):
            high_y = after(cell["high_y"][f], cells_high[z]["high_y"][f])
            low_y = before(cells_low[z]["low_y"][f], cell["low_y"][f])
            along_z = faces[up][f] - faces[z][f]
            kept = state[f][z] - 4.0 * cell["diffuse"][f]
            new[f][z] = kept - (cell["along_x"][f] + (high_y - low_y) + along_z)
        mom_x, mom_y = (state[1][z], state[2][z])
        new[1][z] = new[1][z] + (TIME_STEP * 2.0 * ROTATION) * mom_y
        new[2][z] = new[2][z] - (TIME_STEP * (2.0 - SHEAR_RATE) * ROTATION) * mom_x
        new[4][z] = new[4][z] + (2.0 * SHEAR_RATE * ROTATION) * cell["shear"]
        low_pair = before(cells_low[z]["low_pair"], cell["low_pair"])
        high_pair = after(cell["high_pair"], cells_high[z]["high_pair"])
        edge_z = cell["pair"] + low_pair
        new[5][z] = state[5][z] + ((edge_y[up] - edge_y[z]) - (high_pair - low_pair))
        new[6][z] = state[6][z] + ((radial_next(edge_z) - edge_z) - (edge_x[up] - edge_x[z]))
        new[7][z] = state[7][z] + (along_y - shared["along_x"])
    return new


def step_kernel(
    cells, peers, rows,
    shear_ref, weight_ref, block_ref, up_hbm, up_below_hbm, down_hbm, down_below_hbm,
    out_ref, state_ref, mid_ref, joined_ref, ghost_ref,
    up_ref, up_below_ref, down_ref, down_below_ref, sems,
):
    sources = (up_hbm, up_below_hbm, down_hbm, down_below_hbm)
    ghost_refs = (up_ref, up_below_ref, down_ref, down_below_ref)
    copies = [
        pltpu.make_async_copy(source, ref, sems.at[i])
        for i, (source, ref) in enumerate(zip(sources, ghost_refs))
    ]
    for copy in copies:
        copy.start()
    place = lax.axis_index("gx")
    places = lax.axis_size("gx")
    own, up_start, down_start, _, _ = plan(shear_ref[0], cells, peers)
    up_start = jnp.where(place == 0, up_start, own)
    down_start = jnp.where(place == places - 1, down_start, own)
    lane = lane_index()
    row = row_index()
    window = block_ref.shape[1]
    single = tiles_for(cells)
    pairs = FIELDS // 2

    def ghosts(index, tiles, start):
        def put(i, tile):
            joined_ref[index, i] = tile

        join_tiles(*tiles, cells, put)
        for t, tile in enumerate(cut_window(joined_ref, index, start, window)):
            ghost_ref[index, t] = tile

    for f in range(FIELDS):
        for t in range(window):
            for z in range(PLANES):
                state_ref[t, f, z] = turn_rows(block_ref[f, t], -z * rows)
    for copy in copies:
        copy.wait()
    for pair in range(pairs):
        span = range(pair * single, (pair + 1) * single)
        ghosts(pair, [[ref[i] for i in span] for ref in (up_below_ref, up_ref)], up_start)
        tiles = [[ref[i] for i in span] for ref in (down_below_ref, down_ref)]
        ghosts(pairs + pair, tiles, down_start)
    faces = [ref[pairs * single] for ref in (down_below_ref, down_ref)]
    tiles = [[turn_rows(face, -t * PLANES) for t in range(single)] for face in faces]
    ghosts(2 * pairs, tiles, down_start)

    for f in range(FIELDS):
        pair, second = divmod(f, 2)
        for t in range(window):
            up = ghost_ref[pair, t]
            down = ghost_ref[pairs + pair, t]
            for z in range(PLANES):
                up_at = z * rows + (0 if second else SENT)
                down_at = z * rows + (SENT if second else 0)
                value = state_ref[t, f, z]
                value = jnp.where(row < rows, value, turn_rows(down, rows - down_at))
                value = jnp.where(row < rows + SENT, value, turn_rows(up, rows + SENT - up_at))
                state_ref[t, f, z] = value
    last = rows + SENT - 1

    def faces_beyond(t, face_x):
        beyond = ghost_ref[2 * pairs, t]
        return [
            jnp.where(row == last, turn_rows(beyond, last - z), radial_next(face_x[z]))
            for z in range(PLANES)
        ]

    def terms(ref, t, count, beyond):
        state = [[ref[t, f, z] for z in range(PLANES)] for f in range(FIELDS)]
        if beyond:
            next_face_x = faces_beyond(t, state[FACE_X])
        else:
            next_face_x = [radial_next(face) for face in state[FACE_X]]
        next_face_y = []
        for z in range(PLANES):
            here = turn_lanes(state[6][z], LANES - 1)
            if t + 1 < count:
                there = turn_lanes(ref[t + 1, 6, z], LANES - 1)
                here = jnp.where(lane < LANES - 1, here, there)
            next_face_y.append(here)
        return state, cell_terms(state, next_face_x, next_face_y)

    low = here = terms(state_ref, 0, window, True)
    for t in range(window):
        high = terms(state_ref, t + 1, window, True) if t + 1 < window else here
        new = tile_step(here[0], low[1], here[1], high[1])
        for f in range(FIELDS):
            for z in range(PLANES):
                if t < single or f == 6:
                    mid_ref[t, f, z] = new[f][z]
        low, here = here, high

    weight = weight_ref[...]
    keep = 1.0 - weight
    low = here = terms(mid_ref, 0, window, False)
    low_done = None
    low_moved = None

    def emit(t, moved):
        for f in range(FIELDS):
            out_ref[f, t] = moved[f]

    for t in range(single):
        high = terms(mid_ref, t + 1, window, False) if t + 1 < single else here
        new = tile_step(here[0], low[1], here[1], high[1])
        done = []
        moved = []
        for f in range(FIELDS):
            mixed = []
            turned = []
            for z in range(PLANES):
                value = 0.5 * (state_ref[t, f, z] + new[f][z])
                below = turn_lanes(value, 1)
                turned.append(below)
                if t:
                    below = jnp.where(lane > 0, below, low_done[f][z])
                mixed.append(keep * value + weight * below)
            done.append(turned)
            both = jnp.where(row < rows, mixed[0], turn_rows(mixed[1], rows))
            moved.append(turn_lanes(both, LANES - BELOW))
        if t:
            emit(
                t - 1,
                [jnp.where(lane < LANES - BELOW, a, b) for a, b in zip(low_moved, moved)],
            )
        low_done, low_moved = done, moved
        low, here = here, high
    emit(single - 1, low_moved)


def row_sources(shift, own, cells, peers, target):
    shift = shift - (cells - BELOW - own)
    shift = jnp.where(shift < 0, shift + cells * peers, shift)
    hops, rest = hops_of(shift, cells, peers)
    upper = (target + peers - hops) & (peers - 1)
    lower = (target + peers - 1 - hops) & (peers - 1)
    return upper, lower, rest


def turned_rows(cells, peers, rows, shift_ref, own, part, target, block_ref, out_ref):
    row = row_index()
    lane = lane_index()
    count = out_ref.shape[1]
    spare = count * LANES - cells
    plans = []
    for x in range(rows):
        upper, lower, rest = row_sources(shift_ref[x], own, cells, peers, target)
        first = ((upper ^ part) & 1) == 0
        block = jnp.where(first, upper, lower) >> 1
        amount = jnp.where(first, rest, rest + spare)
        whole = amount >> LANE_BITS
        sources = [t - whole for t in range(count)]
        sources = [jnp.where(t < 0, t + count, t) for t in sources]
        plans.append((block, sources, amount & (LANES - 1)))
    for f in range(FIELDS):
        result = None
        for x, (block, sources, fine) in enumerate(plans):
            tiles = [block_ref[block, f, t] for t in sources]
            tiles = [turn_lanes(tile, fine) for tile in tiles]
            tiles = [jnp.where(lane < fine, tiles[t - 1], tiles[t]) for t in range(count)]
            if x == 0:
                result = tiles
            else:
                result = [jnp.where(row % rows == x, a, b) for a, b in zip(tiles, result)]
        for t in range(count):
            out_ref[f, t] = result[t]


def gather_kernel(cells, peers, rows, shear_ref, shift_ref, *refs):
    in_refs, block_ref, out_ref = (refs[:-2], refs[-2], refs[-1])
    part = lax.axis_index("gy")
    own = plan(shear_ref[0], cells, peers)[0]
    for i, ref in enumerate(reversed(in_refs)):
        block_ref[(part >> 1) ^ i] = ref[...]
    turned_rows(cells, peers, rows, shift_ref, own, part, part ^ 1, block_ref, out_ref)


def keep_kernel(cells, peers, rows, shear_ref, shift_ref, block_ref, out_ref):
    part = lax.axis_index("gy")
    own = plan(shear_ref[0], cells, peers)[0]
    turned_rows(cells, peers, rows, shift_ref, own, part, part, block_ref, out_ref)


def merge_kernel(
    cells, peers, rows, shear_ref, shift_ref, mine_ref, other_ref, out_hbm, out_ref, out_sem
):
    part = lax.axis_index("gy")
    own = plan(shear_ref[0], cells, peers)[0]
    row = row_index() % rows
    lane = lane_index()
    count = mine_ref.shape[1]
    border = jnp.zeros((SUBLANES, LANES), jnp.int32)
    first = jnp.zeros((SUBLANES, LANES), jnp.int32)
    for x in range(rows):
        upper, _, rest = row_sources(shift_ref[x], own, cells, peers, part)
        border = jnp.where(row == x, rest, border)
        first = jnp.where(row == x, ((upper ^ part) & 1) ^ 1, first)
    masks = [(lane + t * LANES >= border) == (first == 1) for t in range(count)]
    for f in range(FIELDS):
        tiles = [jnp.where(masks[t], mine_ref[f, t], other_ref[f, t]) for t in range(count)]
        value = jnp.concatenate(tiles, axis=1)[:, :cells]
        for z in range(PLANES):
            out_ref[f, z] = value[z * rows : (z + 1) * rows]
        pltpu.make_async_copy(out_ref.at[f], out_hbm.at[f], out_sem.at[f]).start()
    for f in range(FIELDS):
        pltpu.make_async_copy(out_ref.at[f], out_hbm.at[f], out_sem.at[f]).wait()


def solution(mesh):
    places, peers = (mesh.shape["gx"], mesh.shape["gy"])
    smem = pl.BlockSpec(memory_space=pltpu.SMEM)
    vmem = pl.BlockSpec(memory_space=pltpu.VMEM)
    hbm = pl.BlockSpec(memory_space=pltpu.HBM)
    params = pltpu.CompilerParams(vmem_limit_bytes=8 * 2**20)
    axes = ("gx", "gy")

    def array(*shape):
        return jax.ShapeDtypeStruct(shape + (SUBLANES, LANES), jnp.float32)

    def scratch(*shape):
        return pltpu.VMEM(shape + (SUBLANES, LANES), jnp.float32)

    def device(x, y):
        return x % places * peers + y % peers

    devices = [(x, y) for x in range(places) for y in range(peers)]

    def ghosts(up_hop, down_hop, up, down):
        out = []
        for message, step, edge, hop in ((up, 1, places - 1, up_hop), (down, -1, 0, -down_hop)):
            for beside in range(2):
                route = [
                    (device(x, y), device(x + step, y + beside + hop * (x == edge)))
                    for x, y in devices
                ]
                out.append(lax.ppermute(message, axes, route))
        return out

    def shards(state, shear_offset, remap_shift, frac_index):
        rows, cells = state.shape[2:]
        single = tiles_for(cells)
        double = tiles_for(2 * cells)
        window = tiles_for(BELOW + cells + ABOVE)
        edge = FIELDS // 2 * single + 1
        below = lax.ppermute(state, "gy", [(i, (i + 1) % peers) for i in range(peers)])
        up, down = pl.pallas_call(
            lambda *refs: edge_kernel(cells, rows, *refs),
            out_shape=[array(edge)] * 2,
            in_specs=[vmem],
            out_specs=[vmem] * 2,
            compiler_params=params,
            name="edge",
        )(state)
        _, _, _, up_hop, down_hop = plan(shear_offset[0], cells, peers)
        branches = [
            lambda u, d, i=i: ghosts(i // 2 + i % 2, i // 2, u, d) for i in range(2 * peers)
        ]
        which = (down_hop + up_hop) & (2 * peers - 1)
        ghost_rows = lax.switch(which, branches, up, down)
        block, weight = pl.pallas_call(
            lambda *refs: join_kernel(cells, peers, *refs),
            out_shape=[array(FIELDS, window), array()],
            in_specs=[smem] * 2 + [vmem] * 2,
            out_specs=[vmem] * 2,
            scratch_shapes=[scratch(FIELDS, double)],
            compiler_params=params,
            name="join",
        )(shear_offset, frac_index, state, below)
        block = pl.pallas_call(
            lambda *refs: step_kernel(cells, peers, rows, *refs),
            out_shape=array(FIELDS, single),
            in_specs=[smem] + [vmem] * 2 + [hbm] * 4,
            out_specs=vmem,
            scratch_shapes=[scratch(window, FIELDS, PLANES)] * 2
            + [scratch(FIELDS + 1, double), scratch(FIELDS + 1, window)]
            + [scratch(edge)] * 4
            + [pltpu.SemaphoreType.DMA((4,))],
            compiler_params=params,
            name="step",
        )(shear_offset, weight, block, *ghost_rows)

        def exchange(value, bits):
            return lax.ppermute(value, "gy", [(i, i ^ bits) for i in range(peers)])

        far = [exchange(block, bits) for bits in range(peers - 2, 0, -2)]
        blocks = far + [block]
        blocks, other = pl.pallas_call(
            lambda *refs: gather_kernel(cells, peers, rows, *refs),
            out_shape=[array(peers // 2, FIELDS, single), array(FIELDS, single)],
            in_specs=[smem] * 2 + [vmem] * (peers // 2),
            out_specs=[vmem] * 2,
            compiler_params=params,
            name="gather",
        )(shear_offset, remap_shift, *blocks)
        other = exchange(other, 1)
        mine = pl.pallas_call(
            lambda *refs: keep_kernel(cells, peers, rows, *refs),
            out_shape=array(FIELDS, single),
            in_specs=[smem] * 2 + [vmem],
            out_specs=vmem,
            compiler_params=params,
            name="keep",
        )(shear_offset, remap_shift, blocks)
        return pl.pallas_call(
            lambda *refs: merge_kernel(cells, peers, rows, *refs),
            out_shape=jax.ShapeDtypeStruct(state.shape, jnp.float32),
            in_specs=[smem] * 2 + [vmem] * 2,
            out_specs=hbm,
            scratch_shapes=[
                pltpu.VMEM(state.shape, jnp.float32),
                pltpu.SemaphoreType.DMA((FIELDS,)),
            ],
            compiler_params=params,
            name="merge",
        )(shear_offset, remap_shift, mine, other)

    placed = (P(None, None, "gx", "gy"), P(), P("gx"), P("gx"))
    return jax.shard_map(
        shards, mesh=mesh, in_specs=placed, out_specs=P(None, None, "gx", "gy"), check_vma=False
    )
```

```python
import jax
import jax.numpy as jnp
from jax import lax
from jax.experimental import pallas as pl
from jax.experimental.pallas import tpu as pltpu
from jax.sharding import PartitionSpec as P

FRAC = 16

ADIABATIC = 5.0 / 3.0
ROTATION = 1.0
SHEAR_RATE = 1.5
MAX_SPEED = 5.0
TIME_STEP = 0.05

LANES = 128
LANE_BITS = 7
SUBLANES = 8
FIELDS = 8
PLANES = 2
FACE_X = 5
BELOW = 3
ABOVE = 3
TAIL = 4
SENT = 2
HALF_STEP = 0.5 * TIME_STEP
DIFFUSE = 0.5 * MAX_SPEED * TIME_STEP
EDGE = 0.25 * TIME_STEP


def lane_index():
    return lax.broadcasted_iota(jnp.int32, (SUBLANES, LANES), 1)


def row_index():
    return lax.broadcasted_iota(jnp.int32, (SUBLANES, LANES), 0)


def turn_lanes(value, amount):
    return pltpu.roll(value, amount, 1)


def turn_rows(value, amount):
    amount %= SUBLANES
    return pltpu.roll(value, amount, 0) if amount else value


def radial_next(value):
    return turn_rows(value, -1)


def radial_prev(value):
    return turn_rows(value, 1)


def tiles_for(columns):
    return -(-columns // LANES)


def hops_of(columns, cells, peers):
    hops = sum(jnp.where(columns >= k * cells, 1, 0) for k in range(1, peers))
    return hops, columns - hops * cells


def plan(shear, cells, peers):
    hops, rest = hops_of(shear, cells, peers)
    middle = cells // 2
    near = (rest >= middle - 5) & (rest <= middle + 5)
    own = jnp.where(near, middle - 12, middle)
    up_hop = jnp.where(rest > own, 1, 0)
    down_hop = jnp.where(rest + own >= cells, 1, 0)
    up = own - rest + up_hop * cells
    down = own + rest - down_hop * cells
    return own, up, down, hops + up_hop, hops + down_hop


def block_tiles(ref, f, cells):
    value = jnp.concatenate([ref[f, z] for z in range(PLANES)], axis=0)
    tiles = []
    for i in range(0, cells, LANES):
        tile = value[:, i : min(i + LANES, cells)]
        spare = LANES - tile.shape[1]
        if spare:
            tile = jnp.concatenate([tile, jnp.zeros((SUBLANES, spare), tile.dtype)], axis=1)
        tiles.append(tile)
    return tiles


def lay_kernel(
    cells, peers, shear_ref, shift_ref, frac_ref, state_ref,
    out_ref, weight_ref, pick_ref, border_ref,
):
    rows = state_ref.shape[2]
    part = lax.axis_index("gy")
    own = plan(shear_ref[0], cells, peers)[0]
    row = row_index()
    spare = tiles_for(cells) * LANES - cells
    blank = jnp.zeros((SUBLANES, LANES), jnp.int32)
    weight = jnp.zeros((SUBLANES, LANES), jnp.float32)
    picks = [[blank, blank], [blank, blank]]
    border = held = blank
    for x in range(rows):
        level = (frac_ref[x].astype(jnp.float32) + 0.5) / FRAC
        weight = jnp.where(row == x, level, weight)
        here = row % rows == x
        for i, target in enumerate((part ^ 1, part)):
            upper, lower, rest = row_sources(shift_ref[x], own, cells, peers, target)
            first = ((upper ^ part) & 1) == 0
            block = (jnp.where(first, upper, lower) ^ part) >> 1
            amount = jnp.where(first, rest, rest + spare)
            picks[i] = [jnp.where(here, a, b) for a, b in zip((block, amount), picks[i])]
            if target is part:
                border = jnp.where(here, rest, border)
                held = jnp.where(here, jnp.where(first, 1, 0), held)
    weight_ref[...] = weight
    for i in range(2):
        for k in range(2):
            pick_ref[i, k] = picks[i][k]
    border_ref[0] = border
    border_ref[1] = held
    for f in range(FIELDS):
        for t, tile in enumerate(block_tiles(state_ref, f, cells)):
            out_ref[f, t] = turn_lanes(tile, cells % LANES)


def pair_kernel(cells, peers, rows, shear_ref, upper_ref, below_ref, joined_ref, up_ref, down_ref):
    place = lax.axis_index("gx")
    places = lax.axis_size("gx")
    own, up, down, _, _ = plan(shear_ref[0], cells, peers)
    up = jnp.where(place == places - 1, up, own)
    down = jnp.where(place == 0, down, own)
    lane = lane_index()
    row = row_index()
    single = tiles_for(cells)
    gap = cells % LANES
    window = single + 1
    for f in range(FIELDS):
        lower = block_tiles(below_ref, f, cells)
        upper = [upper_ref[f, t] for t in range(single)]
        for i in range(single - 1):
            joined_ref[f, i] = lower[i]
        joined_ref[f, single - 1] = jnp.where(lane < gap, lower[-1], upper[0])
        for k in range(single):
            following = upper[min(k + 1, single - 1)]
            joined_ref[f, single + k] = jnp.where(lane < gap, upper[k], following)

    late = row % rows >= SENT
    pairs = FIELDS // 2
    up_tail = down_tail = jnp.zeros((SUBLANES, LANES), jnp.float32)

    def tail(tile, index, so_far):
        return jnp.where(lane // TAIL == index, turn_lanes(tile, index * TAIL), so_far)

    for pair in range(pairs):
        ups = [cut_window(joined_ref, 2 * pair + i, up, window) for i in range(2)]
        downs = [cut_window(joined_ref, 2 * pair + i, down, window) for i in range(2)]
        ups = [jnp.where(late, a, turn_rows(b, -SENT)) for a, b in zip(*ups)]
        downs = [jnp.where(late, turn_rows(b, SENT), a) for a, b in zip(*downs)]
        for t in range(single):
            up_ref[pair * single + t] = ups[t]
            down_ref[pair * single + t] = downs[t]
        up_tail = tail(ups[single], pair, up_tail)
        down_tail = tail(downs[single], pair, down_tail)
    faces = jnp.zeros((SUBLANES, LANES), jnp.float32)
    tiles = cut_window(joined_ref, FACE_X, down, window)
    for t in range(single):
        for z in range(PLANES):
            at = t * PLANES + z
            faces = jnp.where(row == at, turn_rows(tiles[t], at - (z * rows + SENT)), faces)
    down_ref[pairs * single] = faces
    up_ref[pairs * single] = up_tail
    down_ref[pairs * single + 1] = tail(tiles[single], pairs, down_tail)


def cut_window(joined_ref, f, start, count):
    whole = start >> LANE_BITS
    part = start & (LANES - 1)
    last = joined_ref.shape[1] - 1
    tiles = [joined_ref[f, jnp.minimum(whole + t, last)] for t in range(count + 1)]
    turned = [turn_lanes(tile, (LANES - part) & (LANES - 1)) for tile in tiles]
    here = lane_index() < LANES - part
    return [jnp.where(here, turned[t], turned[t + 1]) for t in range(count)]


def cell_terms(state, next_face_x, next_face_y):
    planes = range(PLANES)
    face_z = state[7]
    out = []
    for z in planes:
        density, mom_x, mom_y, mom_z, energy, face_x, face_y = (state[f][z] for f in range(7))
        cen_x = 0.5 * (face_x + next_face_x[z])
        cen_y = 0.5 * (face_y + next_face_y[z])
        cen_z = 0.5 * (face_z[z] + face_z[(z + 1) % PLANES])
        inverse = 1.0 / density
        vel_x, vel_y, vel_z = (mom_x * inverse, mom_y * inverse, mom_z * inverse)
        magnetic = 0.5 * (cen_x * cen_x + cen_y * cen_y + cen_z * cen_z)
        kinetic = 0.5 * (mom_x * vel_x + mom_y * vel_y + mom_z * vel_z)
        pressure = (ADIABATIC - 1.0) * (energy - kinetic - magnetic) + magnetic
        vel_dot = vel_x * cen_x + vel_y * cen_y + vel_z * cen_z
        scaled_p = HALF_STEP * pressure
        total = energy + pressure
        sv_x, sv_y, sv_z = (HALF_STEP * vel_x, HALF_STEP * vel_y, HALF_STEP * vel_z)
        sb_x, sb_y, sb_z = (HALF_STEP * cen_x, HALF_STEP * cen_y, HALF_STEP * cen_z)
        xx = mom_x * sv_x - cen_x * sb_x + scaled_p
        yy = mom_y * sv_y - cen_y * sb_y + scaled_p
        zz = mom_z * sv_z - cen_z * sb_z + scaled_p
        xy = mom_x * sv_y - cen_x * sb_y
        xz = mom_x * sv_z - cen_x * sb_z
        yz = mom_y * sv_z - cen_y * sb_z
        diffuse = [DIFFUSE * state[f][z] for f in range(5)]
        flux_x = [HALF_STEP * mom_x, xx, xy, xz, total * sv_x - sb_x * vel_dot]
        flux_y = [HALF_STEP * mom_y, xy, yy, yz, total * sv_y - sb_y * vel_dot]
        flux_z = [HALF_STEP * mom_z, xz, yz, zz, total * sv_z - sb_z * vel_dot]
        e_z = EDGE * (vel_y * cen_x - vel_x * cen_y)
        pair = e_z + radial_prev(e_z)
        out.append(
            dict(
                diffuse=diffuse,
                along_x=[
                    radial_next(f - d) - radial_prev(f + d) for f, d in zip(flux_x, diffuse)
                ],
                low_y=[turn_lanes(f + d, 1) for f, d in zip(flux_y, diffuse)],
                high_y=[turn_lanes(f - d, LANES - 1) for f, d in zip(flux_y, diffuse)],
                flux_z=flux_z,
                shear=xy,
                e_x=EDGE * (vel_z * cen_y - vel_y * cen_z),
                e_y=EDGE * (vel_x * cen_z - vel_z * cen_x),
                pair=pair,
                low_pair=turn_lanes(pair, 1),
                high_pair=turn_lanes(pair, LANES - 1),
            )
        )
    e_x, e_y = (
        [sum((cell[name] for cell in out[1:]), out[0][name]) for name in ("e_x", "e_y")]
    )
    shared = dict(
        e_x=e_x,
        low_e_x=turn_lanes(e_x, 1),
        high_e_x=turn_lanes(e_x, LANES - 1),
        edge_y=[e_y + radial_prev(e_y)] * PLANES,
        along_x=radial_next(e_y) - radial_prev(e_y),
    )
    return out, shared


def tile_step(state, low, here, high):
    lane = lane_index()
    cells_low, shared_low = low
    cells, shared = here
    cells_high, shared_high = high

    def before(turned_low, turned):
        return jnp.where(lane > 0, turned, turned_low)

    def after(turned, turned_high):
        return jnp.where(lane < LANES - 1, turned, turned_high)

    new = [[None] * PLANES for f in range(FIELDS)]
    faces = [
        [
            (cells[z - 1]["flux_z"][f] + cells[z]["flux_z"][f])
            - (cells[z]["diffuse"][f] - cells[z - 1]["diffuse"][f])
            for f in range(5)
        ]
        for z in range(PLANES)
    ]
    low_e_x = before(shared_low["low_e_x"], shared["low_e_x"])
    along_y = after(shared["high_e_x"], shared_high["high_e_x"]) - low_e_x
    edge_x = [shared["e_x"] + low_e_x] * PLANES
    edge_y = shared["edge_y"]
    for z in range(PLANES):
        cell = cells[z]
        up = (z + 1) % PLANES
        for f in range(5):
            high_y = after(cell["high_y"][f], cells_high[z]["high_y"][f])
            low_y = before(cells_low[z]["low_y"][f], cell["low_y"][f])
            along_z = faces[up][f] - faces[z][f]
            kept = state[f][z] - 4.0 * cell["diffuse"][f]
            new[f][z] = kept - (cell["along_x"][f] + (high_y - low_y) + along_z)
        mom_x, mom_y = (state[1][z], state[2][z])
        new[1][z] = new[1][z] + (TIME_STEP * 2.0 * ROTATION) * mom_y
        new[2][z] = new[2][z] - (TIME_STEP * (2.0 - SHEAR_RATE) * ROTATION) * mom_x
        new[4][z] = new[4][z] + (2.0 * SHEAR_RATE * ROTATION) * cell["shear"]
        low_pair = before(cells_low[z]["low_pair"], cell["low_pair"])
        high_pair = after(cell["high_pair"], cells_high[z]["high_pair"])
        edge_z = cell["pair"] + low_pair
        new[5][z] = state[5][z] + ((edge_y[up] - edge_y[z]) - (high_pair - low_pair))
        new[6][z] = state[6][z] + ((radial_next(edge_z) - edge_z) - (edge_x[up] - edge_x[z]))
        new[7][z] = state[7][z] + (along_y - shared["along_x"])
    return new


def step_kernel(
    cells, peers, rows,
    shear_ref, weight_ref, joined_ref, up_hbm, down_hbm,
    out_ref, state_ref, mid_ref, up_ref, down_ref, up_sem, down_sem,
):
    up_copy = pltpu.make_async_copy(up_hbm, up_ref, up_sem)
    down_copy = pltpu.make_async_copy(down_hbm, down_ref, down_sem)
    up_copy.start()
    down_copy.start()
    own = plan(shear_ref[0], cells, peers)[0]
    lane = lane_index()
    row = row_index()
    single = tiles_for(cells)
    window = single + 1
    pairs = FIELDS // 2

    for f in range(FIELDS):
        for t, tile in enumerate(cut_window(joined_ref, f, own, window)):
            for z in range(PLANES):
                state_ref[t, f, z] = turn_rows(tile, -z * rows)
    up_copy.wait()
    down_copy.wait()
    for f in range(FIELDS):
        pair, second = divmod(f, 2)
        for t in range(window):
            if t < single:
                up = up_ref[pair * single + t]
                down = down_ref[pair * single + t]
            else:
                back = (LANES - pair * TAIL) % LANES
                up = turn_lanes(up_ref[pairs * single], back)
                down = turn_lanes(down_ref[pairs * single + 1], back)
            for z in range(PLANES):
                up_at = z * rows + (0 if second else SENT)
                down_at = z * rows + (SENT if second else 0)
                value = state_ref[t, f, z]
                value = jnp.where(row < rows, value, turn_rows(down, rows - down_at))
                value = jnp.where(row < rows + SENT, value, turn_rows(up, rows + SENT - up_at))
                state_ref[t, f, z] = value
    last = rows + SENT - 1

    def faces_beyond(t, face_x):
        if t < single:
            beyond = [turn_rows(down_ref[pairs * single], last - t * PLANES - z) for z in range(PLANES)]
        else:
            tile = turn_lanes(down_ref[pairs * single + 1], LANES - pairs * TAIL)
            beyond = [turn_rows(tile, last - (z * rows + SENT)) for z in range(PLANES)]
        return [jnp.where(row == last, b, radial_next(face)) for b, face in zip(beyond, face_x)]

    def terms(ref, t, count, beyond):
        state = [[ref[t, f, z] for z in range(PLANES)] for f in range(FIELDS)]
        if beyond:
            next_face_x = faces_beyond(t, state[FACE_X])
        else:
            next_face_x = [radial_next(face) for face in state[FACE_X]]
        next_face_y = []
        for z in range(PLANES):
            here = turn_lanes(state[6][z], LANES - 1)
            if t + 1 < count:
                there = turn_lanes(ref[t + 1, 6, z], LANES - 1)
                here = jnp.where(lane < LANES - 1, here, there)
            next_face_y.append(here)
        return state, cell_terms(state, next_face_x, next_face_y)

    low = here = terms(state_ref, 0, window, True)
    for t in range(window):
        high = terms(state_ref, t + 1, window, True) if t + 1 < window else here
        new = tile_step(here[0], low[1], here[1], high[1])
        for f in range(FIELDS):
            for z in range(PLANES):
                if t < single or f == 6:
                    mid_ref[t, f, z] = new[f][z]
        low, here = here, high

    weight = weight_ref[...]
    keep = 1.0 - weight
    low = here = terms(mid_ref, 0, window, False)
    low_done = None
    low_moved = None

    def emit(t, moved):
        for f in range(FIELDS):
            out_ref[f, t] = moved[f]

    for t in range(single):
        high = terms(mid_ref, t + 1, window, False) if t + 1 < single else here
        new = tile_step(here[0], low[1], here[1], high[1])
        done = []
        moved = []
        for f in range(FIELDS):
            mixed = []
            turned = []
            for z in range(PLANES):
                value = 0.5 * (state_ref[t, f, z] + new[f][z])
                below = turn_lanes(value, 1)
                turned.append(below)
                if t:
                    below = jnp.where(lane > 0, below, low_done[f][z])
                mixed.append(keep * value + weight * below)
            done.append(turned)
            both = jnp.where(row < rows, mixed[0], turn_rows(mixed[1], rows))
            moved.append(turn_lanes(both, LANES - BELOW))
        if t:
            emit(
                t - 1,
                [jnp.where(lane < LANES - BELOW, a, b) for a, b in zip(low_moved, moved)],
            )
        low_done, low_moved = done, moved
        low, here = here, high
    emit(single - 1, low_moved)


def row_sources(shift, own, cells, peers, target):
    shift = shift - (cells - BELOW - own)
    shift = jnp.where(shift < 0, shift + cells * peers, shift)
    hops, rest = hops_of(shift, cells, peers)
    upper = (target + peers - hops) & (peers - 1)
    lower = (target + peers - 1 - hops) & (peers - 1)
    return upper, lower, rest


def pick_kernel(target, pick_ref, *refs):
    in_refs, out_ref = (refs[:-1], refs[-1])
    count = out_ref.shape[1]
    block = pick_ref[target, 0]
    amount = pick_ref[target, 1]
    lane = lane_index()
    fine = amount & (LANES - 1)
    source = (lane - fine) & (LANES - 1)
    chosen = [block == i for i in range(len(in_refs))]
    for f in range(FIELDS):
        tiles = [in_refs[0][f, t] for t in range(count)]
        for mask, ref in zip(chosen[1:], in_refs[1:]):
            tiles = [jnp.where(mask, ref[f, t], tiles[t]) for t in range(count)]
        step = 1
        while step < count:
            moves = (amount & (step * LANES)) != 0
            tiles = [jnp.where(moves, tiles[(t - step) % count], tiles[t]) for t in range(count)]
            step *= 2
        tiles = [
            jnp.take_along_axis(tile, source, axis=1, mode="promise_in_bounds") for tile in tiles
        ]
        for t in range(count):
            out_ref[f, t] = jnp.where(lane < fine, tiles[t - 1], tiles[t])


def merge_kernel(cells, rows, border_ref, mine_ref, other_ref, out_hbm, out_ref, out_sem):
    count = mine_ref.shape[1]
    border = border_ref[0]
    held = border_ref[1] == 1
    masks = [(lane_index() + t * LANES >= border) == held for t in range(count)]
    for f in range(FIELDS):
        tiles = [jnp.where(masks[t], mine_ref[f, t], other_ref[f, t]) for t in range(count)]
        value = jnp.concatenate(tiles, axis=1)[:, :cells]
        for z in range(PLANES):
            out_ref[f, z] = value[z * rows : (z + 1) * rows]
        pltpu.make_async_copy(out_ref.at[f], out_hbm.at[f], out_sem.at[f]).start()
    for f in range(FIELDS):
        pltpu.make_async_copy(out_ref.at[f], out_hbm.at[f], out_sem.at[f]).wait()


def solution(mesh):
    places, peers = (mesh.shape["gx"], mesh.shape["gy"])
    smem = pl.BlockSpec(memory_space=pltpu.SMEM)
    vmem = pl.BlockSpec(memory_space=pltpu.VMEM)
    hbm = pl.BlockSpec(memory_space=pltpu.HBM)
    params = pltpu.CompilerParams(vmem_limit_bytes=8 * 2**20)
    axes = ("gx", "gy")

    def array(*shape):
        return jax.ShapeDtypeStruct(shape + (SUBLANES, LANES), jnp.float32)

    def scratch(*shape):
        return pltpu.VMEM(shape + (SUBLANES, LANES), jnp.float32)

    def device(x, y):
        return x % places * peers + y % peers

    devices = [(x, y) for x in range(places) for y in range(peers)]

    def ghosts(up_hop, down_hop, up, down):
        rise = [(device(x, y), device(x + 1, y + up_hop * (x == places - 1))) for x, y in devices]
        fall = [(device(x, y), device(x - 1, y - down_hop * (x == 0))) for x, y in devices]
        up = lax.ppermute(up, axes, rise)
        return up, lax.ppermute(down, axes, fall)

    def shards(state, shear_offset, remap_shift, frac_index):
        rows, cells = state.shape[2:]
        single = tiles_for(cells)
        double = tiles_for(2 * cells)
        window = tiles_for(BELOW + cells + ABOVE)
        below = lax.ppermute(state, "gy", [(i, (i + 1) % peers) for i in range(peers)])
        numbers = lambda *shape: jax.ShapeDtypeStruct(shape + (SUBLANES, LANES), jnp.int32)
        upper, weight, pick, border = pl.pallas_call(
            lambda *refs: lay_kernel(cells, peers, *refs),
            out_shape=[array(FIELDS, single), array(), numbers(2, 2), numbers(2)],
            in_specs=[smem] * 3 + [vmem],
            out_specs=[vmem] * 4,
            compiler_params=params,
            name="lay",
        )(shear_offset, remap_shift, frac_index, state)
        edge = FIELDS // 2 * single + 2
        joined, up, down = pl.pallas_call(
            lambda *refs: pair_kernel(cells, peers, rows, *refs),
            out_shape=[array(FIELDS, double), array(edge), array(edge)],
            in_specs=[smem, vmem, vmem],
            out_specs=[vmem] * 3,
            compiler_params=params,
            name="pair",
        )(shear_offset, upper, below)
        _, _, _, up_hop, down_hop = plan(shear_offset[0], cells, peers)
        branches = [
            lambda u, d, i=i: ghosts(i // 2 + i % 2, i // 2, u, d) for i in range(2 * peers)
        ]
        which = (down_hop + up_hop) & (2 * peers - 1)
        up, down = lax.switch(which, branches, up, down)
        block = pl.pallas_call(
            lambda *refs: step_kernel(cells, peers, rows, *refs),
            out_shape=array(FIELDS, single),
            in_specs=[smem] + [vmem] * 2 + [hbm] * 2,
            out_specs=vmem,
            scratch_shapes=[scratch(window, FIELDS, PLANES)] * 2
            + [scratch(edge), scratch(edge)]
            + [pltpu.SemaphoreType.DMA] * 2,
            compiler_params=params,
            name="step",
        )(shear_offset, weight, joined, up, down)

        def exchange(value, bits):
            return lax.ppermute(value, "gy", [(i, i ^ bits) for i in range(peers)])

        far = [exchange(block, bits) for bits in range(peers - 2, 0, -2)]

        def picked(target, name):
            return pl.pallas_call(
                lambda pick_ref, *refs: pick_kernel(target, pick_ref, *refs[-2::-1], refs[-1]),
                out_shape=array(FIELDS, single),
                in_specs=[vmem] * (1 + peers // 2),
                out_specs=vmem,
                compiler_params=params,
                name=name,
            )(pick, *far, block)

        other = exchange(picked(0, "gather"), 1)
        mine = picked(1, "keep")
        return pl.pallas_call(
            lambda *refs: merge_kernel(cells, rows, *refs),
            out_shape=jax.ShapeDtypeStruct(state.shape, jnp.float32),
            in_specs=[vmem] * 3,
            out_specs=hbm,
            scratch_shapes=[
                pltpu.VMEM(state.shape, jnp.float32),
                pltpu.SemaphoreType.DMA((FIELDS,)),
            ],
            compiler_params=params,
            name="merge",
        )(border, mine, other)

    placed = (P(None, None, "gx", "gy"), P(), P("gx"), P("gx"))
    return jax.shard_map(
        shards, mesh=mesh, in_specs=placed, out_specs=P(None, None, "gx", "gy"), check_vma=False
    )
```

```python
import jax
import jax.numpy as jnp
from jax import lax
from jax.experimental import pallas as pl
from jax.experimental.pallas import tpu as pltpu
from jax.sharding import PartitionSpec as P

FRAC = 16

ADIABATIC = 5.0 / 3.0
ROTATION = 1.0
SHEAR_RATE = 1.5
MAX_SPEED = 5.0
TIME_STEP = 0.05

LANES = 128
LANE_BITS = 7
SUBLANES = 8
FIELDS = 8
PLANES = 2
FACE_X = 5
BELOW = 3
ABOVE = 3
TAIL = 4
SENT = 2
HALF_STEP = 0.5 * TIME_STEP
DIFFUSE = 0.5 * MAX_SPEED * TIME_STEP
EDGE = 0.25 * TIME_STEP


def lane_index():
    return lax.broadcasted_iota(jnp.int32, (SUBLANES, LANES), 1)


def row_index():
    return lax.broadcasted_iota(jnp.int32, (SUBLANES, LANES), 0)


def turn_lanes(value, amount):
    return pltpu.roll(value, amount, 1)


def turn_rows(value, amount):
    amount %= SUBLANES
    return pltpu.roll(value, amount, 0) if amount else value


def radial_next(value):
    return turn_rows(value, -1)


def radial_prev(value):
    return turn_rows(value, 1)


def tiles_for(columns):
    return -(-columns // LANES)


def hops_of(columns, cells, peers):
    hops = sum(jnp.where(columns >= k * cells, 1, 0) for k in range(1, peers))
    return hops, columns - hops * cells


def plan(shear, cells, peers):
    hops, rest = hops_of(shear, cells, peers)
    middle = cells // 2
    near = (rest >= middle - 5) & (rest <= middle + 5)
    own = jnp.where(near, middle - 12, middle)
    up_hop = jnp.where(rest > own, 1, 0)
    down_hop = jnp.where(rest + own >= cells, 1, 0)
    up = own - rest + up_hop * cells
    down = own + rest - down_hop * cells
    return own, up, down, hops + up_hop, hops + down_hop


def block_tiles(ref, f, cells):
    value = jnp.concatenate([ref[f, z] for z in range(PLANES)], axis=0)
    tiles = []
    for i in range(0, cells, LANES):
        tile = value[:, i : min(i + LANES, cells)]
        spare = LANES - tile.shape[1]
        if spare:
            tile = jnp.concatenate([tile, jnp.zeros((SUBLANES, spare), tile.dtype)], axis=1)
        tiles.append(tile)
    return tiles


def lay_kernel(cells, state_ref, out_ref):
    for f in range(FIELDS):
        for t, tile in enumerate(block_tiles(state_ref, f, cells)):
            out_ref[f, t] = tile


def remap_kernel(
    cells, peers, rows, shear_ref, shift_ref, frac_ref, weight_ref, pick_ref, border_ref
):
    part = lax.axis_index("gy")
    own = plan(shear_ref[0], cells, peers)[0]
    row = row_index()
    spare = tiles_for(cells) * LANES - cells
    blank = jnp.zeros((SUBLANES, LANES), jnp.int32)
    weight = jnp.zeros((SUBLANES, LANES), jnp.float32)
    picks = [[blank, blank], [blank, blank]]
    border = held = blank
    for x in range(rows):
        level = (frac_ref[x].astype(jnp.float32) + 0.5) / FRAC
        weight = jnp.where(row == x, level, weight)
        here = row % rows == x
        for i, target in enumerate((part ^ 1, part)):
            upper, lower, rest = row_sources(shift_ref[x], own, cells, peers, target)
            first = ((upper ^ part) & 1) == 0
            block = (jnp.where(first, upper, lower) ^ part) >> 1
            amount = jnp.where(first, rest, rest + spare)
            picks[i] = [jnp.where(here, a, b) for a, b in zip((block, amount), picks[i])]
            if target is part:
                border = jnp.where(here, rest, border)
                held = jnp.where(here, jnp.where(first, 1, 0), held)
    weight_ref[...] = weight
    for i in range(2):
        for k in range(2):
            pick_ref[i, k] = picks[i][k]
    border_ref[0] = border
    border_ref[1] = held


def pair_kernel(cells, peers, rows, shear_ref, upper_ref, below_ref, joined_ref, up_ref, down_ref):
    place = lax.axis_index("gx")
    places = lax.axis_size("gx")
    own, up, down, _, _ = plan(shear_ref[0], cells, peers)
    up = jnp.where(place == places - 1, up, own)
    down = jnp.where(place == 0, down, own)
    lane = lane_index()
    row = row_index()
    single = tiles_for(cells)
    gap = cells % LANES
    window = single + 1
    for f in range(FIELDS):
        lower = [below_ref[f, t] for t in range(single)]
        upper = [turn_lanes(upper_ref[f, t], gap) for t in range(single)]
        for i in range(single - 1):
            joined_ref[f, i] = lower[i]
        joined_ref[f, single - 1] = jnp.where(lane < gap, lower[-1], upper[0])
        for k in range(single):
            following = upper[min(k + 1, single - 1)]
            joined_ref[f, single + k] = jnp.where(lane < gap, upper[k], following)

    late = row % rows >= SENT
    pairs = FIELDS // 2
    up_tail = down_tail = jnp.zeros((SUBLANES, LANES), jnp.float32)

    def tail(tile, index, so_far):
        return jnp.where(lane // TAIL == index, turn_lanes(tile, index * TAIL), so_far)

    for pair in range(pairs):
        ups = [cut_window(joined_ref, 2 * pair + i, up, window) for i in range(2)]
        downs = [cut_window(joined_ref, 2 * pair + i, down, window) for i in range(2)]
        ups = [jnp.where(late, a, turn_rows(b, -SENT)) for a, b in zip(*ups)]
        downs = [jnp.where(late, turn_rows(b, SENT), a) for a, b in zip(*downs)]
        for t in range(single):
            up_ref[pair * single + t] = ups[t]
            down_ref[pair * single + t] = downs[t]
        up_tail = tail(ups[single], pair, up_tail)
        down_tail = tail(downs[single], pair, down_tail)
    faces = jnp.zeros((SUBLANES, LANES), jnp.float32)
    tiles = cut_window(joined_ref, FACE_X, down, window)
    for t in range(single):
        for z in range(PLANES):
            at = t * PLANES + z
            faces = jnp.where(row == at, turn_rows(tiles[t], at - (z * rows + SENT)), faces)
    down_ref[pairs * single] = faces
    up_ref[pairs * single] = up_tail
    down_ref[pairs * single + 1] = tail(tiles[single], pairs, down_tail)


def cut_window(joined_ref, f, start, count):
    whole = start >> LANE_BITS
    part = start & (LANES - 1)
    last = joined_ref.shape[1] - 1
    tiles = [joined_ref[f, jnp.minimum(whole + t, last)] for t in range(count + 1)]
    turned = [turn_lanes(tile, (LANES - part) & (LANES - 1)) for tile in tiles]
    here = lane_index() < LANES - part
    return [jnp.where(here, turned[t], turned[t + 1]) for t in range(count)]


def cell_terms(state, next_face_x, next_face_y):
    planes = range(PLANES)
    face_z = state[7]
    out = []
    for z in planes:
        density, mom_x, mom_y, mom_z, energy, face_x, face_y = (state[f][z] for f in range(7))
        cen_x = 0.5 * (face_x + next_face_x[z])
        cen_y = 0.5 * (face_y + next_face_y[z])
        cen_z = 0.5 * (face_z[z] + face_z[(z + 1) % PLANES])
        inverse = 1.0 / density
        vel_x, vel_y, vel_z = (mom_x * inverse, mom_y * inverse, mom_z * inverse)
        magnetic = 0.5 * (cen_x * cen_x + cen_y * cen_y + cen_z * cen_z)
        kinetic = 0.5 * (mom_x * vel_x + mom_y * vel_y + mom_z * vel_z)
        pressure = (ADIABATIC - 1.0) * (energy - kinetic - magnetic) + magnetic
        vel_dot = vel_x * cen_x + vel_y * cen_y + vel_z * cen_z
        scaled_p = HALF_STEP * pressure
        total = energy + pressure
        sv_x, sv_y, sv_z = (HALF_STEP * vel_x, HALF_STEP * vel_y, HALF_STEP * vel_z)
        sb_x, sb_y, sb_z = (HALF_STEP * cen_x, HALF_STEP * cen_y, HALF_STEP * cen_z)
        xx = mom_x * sv_x - cen_x * sb_x + scaled_p
        yy = mom_y * sv_y - cen_y * sb_y + scaled_p
        zz = mom_z * sv_z - cen_z * sb_z + scaled_p
        xy = mom_x * sv_y - cen_x * sb_y
        xz = mom_x * sv_z - cen_x * sb_z
        yz = mom_y * sv_z - cen_y * sb_z
        diffuse = [DIFFUSE * state[f][z] for f in range(5)]
        flux_x = [HALF_STEP * mom_x, xx, xy, xz, total * sv_x - sb_x * vel_dot]
        flux_y = [HALF_STEP * mom_y, xy, yy, yz, total * sv_y - sb_y * vel_dot]
        flux_z = [HALF_STEP * mom_z, xz, yz, zz, total * sv_z - sb_z * vel_dot]
        e_z = EDGE * (vel_y * cen_x - vel_x * cen_y)
        pair = e_z + radial_prev(e_z)
        out.append(
            dict(
                diffuse=diffuse,
                along_x=[
                    radial_next(f - d) - radial_prev(f + d) for f, d in zip(flux_x, diffuse)
                ],
                low_y=[turn_lanes(f + d, 1) for f, d in zip(flux_y, diffuse)],
                high_y=[turn_lanes(f - d, LANES - 1) for f, d in zip(flux_y, diffuse)],
                flux_z=flux_z,
                shear=xy,
                e_x=EDGE * (vel_z * cen_y - vel_y * cen_z),
                e_y=EDGE * (vel_x * cen_z - vel_z * cen_x),
                pair=pair,
                low_pair=turn_lanes(pair, 1),
                high_pair=turn_lanes(pair, LANES - 1),
            )
        )
    e_x, e_y = (
        [sum((cell[name] for cell in out[1:]), out[0][name]) for name in ("e_x", "e_y")]
    )
    shared = dict(
        e_x=e_x,
        low_e_x=turn_lanes(e_x, 1),
        high_e_x=turn_lanes(e_x, LANES - 1),
        edge_y=[e_y + radial_prev(e_y)] * PLANES,
        along_x=radial_next(e_y) - radial_prev(e_y),
    )
    return out, shared


def tile_step(state, low, here, high):
    lane = lane_index()
    cells_low, shared_low = low
    cells, shared = here
    cells_high, shared_high = high

    def before(turned_low, turned):
        return jnp.where(lane > 0, turned, turned_low)

    def after(turned, turned_high):
        return jnp.where(lane < LANES - 1, turned, turned_high)

    new = [[None] * PLANES for f in range(FIELDS)]
    faces = [
        [
            (cells[z - 1]["flux_z"][f] + cells[z]["flux_z"][f])
            - (cells[z]["diffuse"][f] - cells[z - 1]["diffuse"][f])
            for f in range(5)
        ]
        for z in range(PLANES)
    ]
    low_e_x = before(shared_low["low_e_x"], shared["low_e_x"])
    along_y = after(shared["high_e_x"], shared_high["high_e_x"]) - low_e_x
    edge_x = [shared["e_x"] + low_e_x] * PLANES
    edge_y = shared["edge_y"]
    for z in range(PLANES):
        cell = cells[z]
        up = (z + 1) % PLANES
        for f in range(5):
            high_y = after(cell["high_y"][f], cells_high[z]["high_y"][f])
            low_y = before(cells_low[z]["low_y"][f], cell["low_y"][f])
            along_z = faces[up][f] - faces[z][f]
            kept = state[f][z] - 4.0 * cell["diffuse"][f]
            new[f][z] = kept - (cell["along_x"][f] + (high_y - low_y) + along_z)
        mom_x, mom_y = (state[1][z], state[2][z])
        new[1][z] = new[1][z] + (TIME_STEP * 2.0 * ROTATION) * mom_y
        new[2][z] = new[2][z] - (TIME_STEP * (2.0 - SHEAR_RATE) * ROTATION) * mom_x
        new[4][z] = new[4][z] + (2.0 * SHEAR_RATE * ROTATION) * cell["shear"]
        low_pair = before(cells_low[z]["low_pair"], cell["low_pair"])
        high_pair = after(cell["high_pair"], cells_high[z]["high_pair"])
        edge_z = cell["pair"] + low_pair
        new[5][z] = state[5][z] + ((edge_y[up] - edge_y[z]) - (high_pair - low_pair))
        new[6][z] = state[6][z] + ((radial_next(edge_z) - edge_z) - (edge_x[up] - edge_x[z]))
        new[7][z] = state[7][z] + (along_y - shared["along_x"])
    return new


def step_kernel(
    cells, peers, rows,
    shear_ref, weight_ref, joined_ref, up_hbm, down_hbm,
    out_ref, state_ref, mid_ref, up_ref, down_ref, up_sem, down_sem,
):
    up_copy = pltpu.make_async_copy(up_hbm, up_ref, up_sem)
    down_copy = pltpu.make_async_copy(down_hbm, down_ref, down_sem)
    up_copy.start()
    down_copy.start()
    own = plan(shear_ref[0], cells, peers)[0]
    lane = lane_index()
    row = row_index()
    single = tiles_for(cells)
    window = single + 1
    pairs = FIELDS // 2

    for f in range(FIELDS):
        for t, tile in enumerate(cut_window(joined_ref, f, own, window)):
            for z in range(PLANES):
                state_ref[t, f, z] = turn_rows(tile, -z * rows)
    up_copy.wait()
    down_copy.wait()
    for f in range(FIELDS):
        pair, second = divmod(f, 2)
        for t in range(window):
            if t < single:
                up = up_ref[pair * single + t]
                down = down_ref[pair * single + t]
            else:
                back = (LANES - pair * TAIL) % LANES
                up = turn_lanes(up_ref[pairs * single], back)
                down = turn_lanes(down_ref[pairs * single + 1], back)
            for z in range(PLANES):
                up_at = z * rows + (0 if second else SENT)
                down_at = z * rows + (SENT if second else 0)
                value = state_ref[t, f, z]
                value = jnp.where(row < rows, value, turn_rows(down, rows - down_at))
                value = jnp.where(row < rows + SENT, value, turn_rows(up, rows + SENT - up_at))
                state_ref[t, f, z] = value
    last = rows + SENT - 1

    def faces_beyond(t, face_x):
        if t < single:
            beyond = [turn_rows(down_ref[pairs * single], last - t * PLANES - z) for z in range(PLANES)]
        else:
            tile = turn_lanes(down_ref[pairs * single + 1], LANES - pairs * TAIL)
            beyond = [turn_rows(tile, last - (z * rows + SENT)) for z in range(PLANES)]
        return [jnp.where(row == last, b, radial_next(face)) for b, face in zip(beyond, face_x)]

    def terms(ref, t, count, beyond):
        state = [[ref[t, f, z] for z in range(PLANES)] for f in range(FIELDS)]
        if beyond:
            next_face_x = faces_beyond(t, state[FACE_X])
        else:
            next_face_x = [radial_next(face) for face in state[FACE_X]]
        next_face_y = []
        for z in range(PLANES):
            here = turn_lanes(state[6][z], LANES - 1)
            if t + 1 < count:
                there = turn_lanes(ref[t + 1, 6, z], LANES - 1)
                here = jnp.where(lane < LANES - 1, here, there)
            next_face_y.append(here)
        return state, cell_terms(state, next_face_x, next_face_y)

    low = here = terms(state_ref, 0, window, True)
    for t in range(window):
        high = terms(state_ref, t + 1, window, True) if t + 1 < window else here
        new = tile_step(here[0], low[1], here[1], high[1])
        for f in range(FIELDS):
            for z in range(PLANES):
                if t < single or f == 6:
                    mid_ref[t, f, z] = new[f][z]
        low, here = here, high

    weight = weight_ref[...]
    keep = 1.0 - weight
    low = here = terms(mid_ref, 0, window, False)
    low_done = None
    low_moved = None

    def emit(t, moved):
        for f in range(FIELDS):
            out_ref[f, t] = moved[f]

    for t in range(single):
        high = terms(mid_ref, t + 1, window, False) if t + 1 < single else here
        new = tile_step(here[0], low[1], here[1], high[1])
        done = []
        moved = []
        for f in range(FIELDS):
            mixed = []
            turned = []
            for z in range(PLANES):
                value = 0.5 * (state_ref[t, f, z] + new[f][z])
                below = turn_lanes(value, 1)
                turned.append(below)
                if t:
                    below = jnp.where(lane > 0, below, low_done[f][z])
                mixed.append(keep * value + weight * below)
            done.append(turned)
            both = jnp.where(row < rows, mixed[0], turn_rows(mixed[1], rows))
            moved.append(turn_lanes(both, LANES - BELOW))
        if t:
            emit(
                t - 1,
                [jnp.where(lane < LANES - BELOW, a, b) for a, b in zip(low_moved, moved)],
            )
        low_done, low_moved = done, moved
        low, here = here, high
    emit(single - 1, low_moved)


def row_sources(shift, own, cells, peers, target):
    shift = shift - (cells - BELOW - own)
    shift = jnp.where(shift < 0, shift + cells * peers, shift)
    hops, rest = hops_of(shift, cells, peers)
    upper = (target + peers - hops) & (peers - 1)
    lower = (target + peers - 1 - hops) & (peers - 1)
    return upper, lower, rest


def pick_kernel(target, pick_ref, *refs):
    in_refs, out_ref = (refs[:-1], refs[-1])
    count = out_ref.shape[1]
    block = pick_ref[target, 0]
    amount = pick_ref[target, 1]
    lane = lane_index()
    fine = amount & (LANES - 1)
    source = (lane - fine) & (LANES - 1)
    chosen = [block == i for i in range(len(in_refs))]
    for f in range(FIELDS):
        tiles = [in_refs[0][f, t] for t in range(count)]
        for mask, ref in zip(chosen[1:], in_refs[1:]):
            tiles = [jnp.where(mask, ref[f, t], tiles[t]) for t in range(count)]
        step = 1
        while step < count:
            moves = (amount & (step * LANES)) != 0
            tiles = [jnp.where(moves, tiles[(t - step) % count], tiles[t]) for t in range(count)]
            step *= 2
        tiles = [
            jnp.take_along_axis(tile, source, axis=1, mode="promise_in_bounds") for tile in tiles
        ]
        for t in range(count):
            out_ref[f, t] = jnp.where(lane < fine, tiles[t - 1], tiles[t])


def merge_kernel(cells, rows, border_ref, mine_ref, other_ref, out_hbm, out_ref, out_sem):
    count = mine_ref.shape[1]
    border = border_ref[0]
    held = border_ref[1] == 1
    masks = [(lane_index() + t * LANES >= border) == held for t in range(count)]
    for f in range(FIELDS):
        tiles = [jnp.where(masks[t], mine_ref[f, t], other_ref[f, t]) for t in range(count)]
        value = jnp.concatenate(tiles, axis=1)[:, :cells]
        for z in range(PLANES):
            out_ref[f, z] = value[z * rows : (z + 1) * rows]
        pltpu.make_async_copy(out_ref.at[f], out_hbm.at[f], out_sem.at[f]).start()
    for f in range(FIELDS):
        pltpu.make_async_copy(out_ref.at[f], out_hbm.at[f], out_sem.at[f]).wait()


def solution(mesh):
    places, peers = (mesh.shape["gx"], mesh.shape["gy"])
    smem = pl.BlockSpec(memory_space=pltpu.SMEM)
    vmem = pl.BlockSpec(memory_space=pltpu.VMEM)
    hbm = pl.BlockSpec(memory_space=pltpu.HBM)
    params = pltpu.CompilerParams(vmem_limit_bytes=8 * 2**20)
    axes = ("gx", "gy")

    def array(*shape):
        return jax.ShapeDtypeStruct(shape + (SUBLANES, LANES), jnp.float32)

    def scratch(*shape):
        return pltpu.VMEM(shape + (SUBLANES, LANES), jnp.float32)

    def device(x, y):
        return x % places * peers + y % peers

    devices = [(x, y) for x in range(places) for y in range(peers)]

    def ghosts(up_hop, down_hop, up, down):
        rise = [(device(x, y), device(x + 1, y + up_hop * (x == places - 1))) for x, y in devices]
        fall = [(device(x, y), device(x - 1, y - down_hop * (x == 0))) for x, y in devices]
        up = lax.ppermute(up, axes, rise)
        return up, lax.ppermute(down, axes, fall)

    def shards(state, shear_offset, remap_shift, frac_index):
        rows, cells = state.shape[2:]
        single = tiles_for(cells)
        double = tiles_for(2 * cells)
        window = tiles_for(BELOW + cells + ABOVE)
        numbers = lambda *shape: jax.ShapeDtypeStruct(shape + (SUBLANES, LANES), jnp.int32)
        upper = pl.pallas_call(
            lambda *refs: lay_kernel(cells, *refs),
            out_shape=array(FIELDS, single),
            in_specs=[vmem],
            out_specs=vmem,
            compiler_params=params,
            name="lay",
        )(state)
        below = lax.ppermute(upper, "gy", [(i, (i + 1) % peers) for i in range(peers)])
        weight, pick, border = pl.pallas_call(
            lambda *refs: remap_kernel(cells, peers, rows, *refs),
            out_shape=[array(), numbers(2, 2), numbers(2)],
            in_specs=[smem] * 3,
            out_specs=[vmem] * 3,
            compiler_params=params,
            name="remap",
        )(shear_offset, remap_shift, frac_index)
        edge = FIELDS // 2 * single + 2
        joined, up, down = pl.pallas_call(
            lambda *refs: pair_kernel(cells, peers, rows, *refs),
            out_shape=[array(FIELDS, double), array(edge), array(edge)],
            in_specs=[smem, vmem, vmem],
            out_specs=[vmem] * 3,
            compiler_params=params,
            name="pair",
        )(shear_offset, upper, below)
        _, _, _, up_hop, down_hop = plan(shear_offset[0], cells, peers)
        branches = [
            lambda u, d, i=i: ghosts(i // 2 + i % 2, i // 2, u, d) for i in range(2 * peers)
        ]
        which = (down_hop + up_hop) & (2 * peers - 1)
        up, down = lax.switch(which, branches, up, down)
        block = pl.pallas_call(
            lambda *refs: step_kernel(cells, peers, rows, *refs),
            out_shape=array(FIELDS, single),
            in_specs=[smem] + [vmem] * 2 + [hbm] * 2,
            out_specs=vmem,
            scratch_shapes=[scratch(window, FIELDS, PLANES)] * 2
            + [scratch(edge), scratch(edge)]
            + [pltpu.SemaphoreType.DMA] * 2,
            compiler_params=params,
            name="step",
        )(shear_offset, weight, joined, up, down)

        def exchange(value, bits):
            return lax.ppermute(value, "gy", [(i, i ^ bits) for i in range(peers)])

        far = [exchange(block, bits) for bits in range(peers - 2, 0, -2)]

        def picked(target, name):
            return pl.pallas_call(
                lambda pick_ref, *refs: pick_kernel(target, pick_ref, *refs[-2::-1], refs[-1]),
                out_shape=array(FIELDS, single),
                in_specs=[vmem] * (1 + peers // 2),
                out_specs=vmem,
                compiler_params=params,
                name=name,
            )(pick, *far, block)

        other = exchange(picked(0, "gather"), 1)
        mine = picked(1, "keep")
        return pl.pallas_call(
            lambda *refs: merge_kernel(cells, rows, *refs),
            out_shape=jax.ShapeDtypeStruct(state.shape, jnp.float32),
            in_specs=[vmem] * 3,
            out_specs=hbm,
            scratch_shapes=[
                pltpu.VMEM(state.shape, jnp.float32),
                pltpu.SemaphoreType.DMA((FIELDS,)),
            ],
            compiler_params=params,
            name="merge",
        )(border, mine, other)

    placed = (P(None, None, "gx", "gy"), P(), P("gx"), P("gx"))
    return jax.shard_map(
        shards, mesh=mesh, in_specs=placed, out_specs=P(None, None, "gx", "gy"), check_vma=False
    )
```

```python
import jax
import jax.numpy as jnp
from jax import lax
from jax.experimental import pallas as pl
from jax.experimental.pallas import tpu as pltpu
from jax.sharding import PartitionSpec as P

FRAC = 16

ADIABATIC = 5.0 / 3.0
ROTATION = 1.0
SHEAR_RATE = 1.5
MAX_SPEED = 5.0
TIME_STEP = 0.05

LANES = 128
LANE_BITS = 7
SUBLANES = 8
FIELDS = 8
PLANES = 2
FACE_X = 5
BELOW = 3
ABOVE = 3
TAIL = 4
SENT = 2
HALF_STEP = 0.5 * TIME_STEP
DIFFUSE = 0.5 * MAX_SPEED * TIME_STEP
EDGE = 0.25 * TIME_STEP


def lane_index():
    return lax.broadcasted_iota(jnp.int32, (SUBLANES, LANES), 1)


def row_index():
    return lax.broadcasted_iota(jnp.int32, (SUBLANES, LANES), 0)


def turn_lanes(value, amount):
    return pltpu.roll(value, amount, 1)


def turn_rows(value, amount):
    amount %= SUBLANES
    return pltpu.roll(value, amount, 0) if amount else value


def radial_next(value):
    return turn_rows(value, -1)


def radial_prev(value):
    return turn_rows(value, 1)


def tiles_for(columns):
    return -(-columns // LANES)


def hops_of(columns, cells, peers):
    hops = sum(jnp.where(columns >= k * cells, 1, 0) for k in range(1, peers))
    return hops, columns - hops * cells


def plan(shear, cells, peers):
    hops, rest = hops_of(shear, cells, peers)
    middle = cells // 2
    near = (rest >= middle - 5) & (rest <= middle + 5)
    own = jnp.where(near, middle - 12, middle)
    up_hop = jnp.where(rest > own, 1, 0)
    down_hop = jnp.where(rest + own >= cells, 1, 0)
    up = own - rest + up_hop * cells
    down = own + rest - down_hop * cells
    return own, up, down, hops + up_hop, hops + down_hop


def block_tiles(ref, f, cells):
    value = jnp.concatenate([ref[f, z] for z in range(PLANES)], axis=0)
    tiles = []
    for i in range(0, cells, LANES):
        tile = value[:, i : min(i + LANES, cells)]
        spare = LANES - tile.shape[1]
        if spare:
            tile = jnp.concatenate([tile, jnp.zeros((SUBLANES, spare), tile.dtype)], axis=1)
        tiles.append(tile)
    return tiles


def lay_kernel(
    cells, peers, shear_ref, shift_ref, frac_ref, state_ref,
    out_ref, weight_ref, pick_ref, border_ref,
):
    rows = state_ref.shape[2]
    part = lax.axis_index("gy")
    own = plan(shear_ref[0], cells, peers)[0]
    row = row_index()
    spare = tiles_for(cells) * LANES - cells
    blank = jnp.zeros((SUBLANES, LANES), jnp.int32)
    weight = jnp.zeros((SUBLANES, LANES), jnp.float32)
    picks = [[blank, blank], [blank, blank]]
    border = held = blank
    for x in range(rows):
        level = (frac_ref[x].astype(jnp.float32) + 0.5) / FRAC
        weight = jnp.where(row == x, level, weight)
        here = row % rows == x
        for i, target in enumerate((part ^ 1, part)):
            upper, lower, rest = row_sources(shift_ref[x], own, cells, peers, target)
            first = ((upper ^ part) & 1) == 0
            block = (jnp.where(first, upper, lower) ^ part) >> 1
            block = jnp.where((part & 1) == 1, partner_order(block, peers // 2), block)
            amount = jnp.where(first, rest, rest + spare)
            picks[i] = [jnp.where(here, a, b) for a, b in zip((block, amount), picks[i])]
            if target is part:
                border = jnp.where(here, rest, border)
                held = jnp.where(here, jnp.where(first, 1, 0), held)
    weight_ref[...] = weight
    for i in range(2):
        for k in range(2):
            pick_ref[i, k] = picks[i][k]
    border_ref[0] = border
    border_ref[1] = held
    for f in range(FIELDS):
        for t, tile in enumerate(block_tiles(state_ref, f, cells)):
            out_ref[f, t] = turn_lanes(tile, cells % LANES)


def pair_kernel(cells, peers, rows, shear_ref, upper_ref, below_ref, joined_ref, up_ref, down_ref):
    place = lax.axis_index("gx")
    places = lax.axis_size("gx")
    own, up, down, _, _ = plan(shear_ref[0], cells, peers)
    up = jnp.where(place == places - 1, up, own)
    down = jnp.where(place == 0, down, own)
    lane = lane_index()
    row = row_index()
    single = tiles_for(cells)
    gap = cells % LANES
    window = single + 1
    for f in range(FIELDS):
        lower = block_tiles(below_ref, f, cells)
        upper = [upper_ref[f, t] for t in range(single)]
        for i in range(single - 1):
            joined_ref[f, i] = lower[i]
        joined_ref[f, single - 1] = jnp.where(lane < gap, lower[-1], upper[0])
        for k in range(single):
            following = upper[min(k + 1, single - 1)]
            joined_ref[f, single + k] = jnp.where(lane < gap, upper[k], following)

    late = row % rows >= SENT
    pairs = FIELDS // 2
    up_tail = down_tail = jnp.zeros((SUBLANES, LANES), jnp.float32)

    def tail(tile, index, so_far):
        return jnp.where(lane // TAIL == index, turn_lanes(tile, index * TAIL), so_far)

    for pair in range(pairs):
        ups = [cut_window(joined_ref, 2 * pair + i, up, window) for i in range(2)]
        downs = [cut_window(joined_ref, 2 * pair + i, down, window) for i in range(2)]
        ups = [jnp.where(late, a, turn_rows(b, -SENT)) for a, b in zip(*ups)]
        downs = [jnp.where(late, turn_rows(b, SENT), a) for a, b in zip(*downs)]
        for t in range(single):
            up_ref[pair * single + t] = ups[t]
            down_ref[pair * single + t] = downs[t]
        up_tail = tail(ups[single], pair, up_tail)
        down_tail = tail(downs[single], pair, down_tail)
    faces = jnp.zeros((SUBLANES, LANES), jnp.float32)
    tiles = cut_window(joined_ref, FACE_X, down, window)
    for t in range(single):
        for z in range(PLANES):
            at = t * PLANES + z
            faces = jnp.where(row == at, turn_rows(tiles[t], at - (z * rows + SENT)), faces)
    down_ref[pairs * single] = faces
    up_ref[pairs * single] = up_tail
    down_ref[pairs * single + 1] = tail(tiles[single], pairs, down_tail)


def cut_window(joined_ref, f, start, count):
    whole = start >> LANE_BITS
    part = start & (LANES - 1)
    last = joined_ref.shape[1] - 1
    tiles = [joined_ref[f, jnp.minimum(whole + t, last)] for t in range(count + 1)]
    turned = [turn_lanes(tile, (LANES - part) & (LANES - 1)) for tile in tiles]
    here = lane_index() < LANES - part
    return [jnp.where(here, turned[t], turned[t + 1]) for t in range(count)]


def cell_terms(state, next_face_x, next_face_y):
    planes = range(PLANES)
    face_z = state[7]
    out = []
    for z in planes:
        density, mom_x, mom_y, mom_z, energy, face_x, face_y = (state[f][z] for f in range(7))
        cen_x = 0.5 * (face_x + next_face_x[z])
        cen_y = 0.5 * (face_y + next_face_y[z])
        cen_z = 0.5 * (face_z[z] + face_z[(z + 1) % PLANES])
        inverse = 1.0 / density
        vel_x, vel_y, vel_z = (mom_x * inverse, mom_y * inverse, mom_z * inverse)
        magnetic = 0.5 * (cen_x * cen_x + cen_y * cen_y + cen_z * cen_z)
        kinetic = 0.5 * (mom_x * vel_x + mom_y * vel_y + mom_z * vel_z)
        pressure = (ADIABATIC - 1.0) * (energy - kinetic - magnetic) + magnetic
        vel_dot = vel_x * cen_x + vel_y * cen_y + vel_z * cen_z
        scaled_p = HALF_STEP * pressure
        total = energy + pressure
        sv_x, sv_y, sv_z = (HALF_STEP * vel_x, HALF_STEP * vel_y, HALF_STEP * vel_z)
        sb_x, sb_y, sb_z = (HALF_STEP * cen_x, HALF_STEP * cen_y, HALF_STEP * cen_z)
        xx = mom_x * sv_x - cen_x * sb_x + scaled_p
        yy = mom_y * sv_y - cen_y * sb_y + scaled_p
        zz = mom_z * sv_z - cen_z * sb_z + scaled_p
        xy = mom_x * sv_y - cen_x * sb_y
        xz = mom_x * sv_z - cen_x * sb_z
        yz = mom_y * sv_z - cen_y * sb_z
        diffuse = [DIFFUSE * state[f][z] for f in range(5)]
        flux_x = [HALF_STEP * mom_x, xx, xy, xz, total * sv_x - sb_x * vel_dot]
        flux_y = [HALF_STEP * mom_y, xy, yy, yz, total * sv_y - sb_y * vel_dot]
        flux_z = [HALF_STEP * mom_z, xz, yz, zz, total * sv_z - sb_z * vel_dot]
        e_z = EDGE * (vel_y * cen_x - vel_x * cen_y)
        pair = e_z + radial_prev(e_z)
        out.append(
            dict(
                diffuse=diffuse,
                along_x=[
                    radial_next(f - d) - radial_prev(f + d) for f, d in zip(flux_x, diffuse)
                ],
                low_y=[turn_lanes(f + d, 1) for f, d in zip(flux_y, diffuse)],
                high_y=[turn_lanes(f - d, LANES - 1) for f, d in zip(flux_y, diffuse)],
                flux_z=flux_z,
                shear=xy,
                e_x=EDGE * (vel_z * cen_y - vel_y * cen_z),
                e_y=EDGE * (vel_x * cen_z - vel_z * cen_x),
                pair=pair,
                low_pair=turn_lanes(pair, 1),
                high_pair=turn_lanes(pair, LANES - 1),
            )
        )
    e_x, e_y = (
        [sum((cell[name] for cell in out[1:]), out[0][name]) for name in ("e_x", "e_y")]
    )
    shared = dict(
        e_x=e_x,
        low_e_x=turn_lanes(e_x, 1),
        high_e_x=turn_lanes(e_x, LANES - 1),
        edge_y=[e_y + radial_prev(e_y)] * PLANES,
        along_x=radial_next(e_y) - radial_prev(e_y),
    )
    return out, shared


def tile_step(state, low, here, high):
    lane = lane_index()
    cells_low, shared_low = low
    cells, shared = here
    cells_high, shared_high = high

    def before(turned_low, turned):
        return jnp.where(lane > 0, turned, turned_low)

    def after(turned, turned_high):
        return jnp.where(lane < LANES - 1, turned, turned_high)

    new = [[None] * PLANES for f in range(FIELDS)]
    faces = [
        [
            (cells[z - 1]["flux_z"][f] + cells[z]["flux_z"][f])
            - (cells[z]["diffuse"][f] - cells[z - 1]["diffuse"][f])
            for f in range(5)
        ]
        for z in range(PLANES)
    ]
    low_e_x = before(shared_low["low_e_x"], shared["low_e_x"])
    along_y = after(shared["high_e_x"], shared_high["high_e_x"]) - low_e_x
    edge_x = [shared["e_x"] + low_e_x] * PLANES
    edge_y = shared["edge_y"]
    for z in range(PLANES):
        cell = cells[z]
        up = (z + 1) % PLANES
        for f in range(5):
            high_y = after(cell["high_y"][f], cells_high[z]["high_y"][f])
            low_y = before(cells_low[z]["low_y"][f], cell["low_y"][f])
            along_z = faces[up][f] - faces[z][f]
            kept = state[f][z] - 4.0 * cell["diffuse"][f]
            new[f][z] = kept - (cell["along_x"][f] + (high_y - low_y) + along_z)
        mom_x, mom_y = (state[1][z], state[2][z])
        new[1][z] = new[1][z] + (TIME_STEP * 2.0 * ROTATION) * mom_y
        new[2][z] = new[2][z] - (TIME_STEP * (2.0 - SHEAR_RATE) * ROTATION) * mom_x
        new[4][z] = new[4][z] + (2.0 * SHEAR_RATE * ROTATION) * cell["shear"]
        low_pair = before(cells_low[z]["low_pair"], cell["low_pair"])
        high_pair = after(cell["high_pair"], cells_high[z]["high_pair"])
        edge_z = cell["pair"] + low_pair
        new[5][z] = state[5][z] + ((edge_y[up] - edge_y[z]) - (high_pair - low_pair))
        new[6][z] = state[6][z] + ((radial_next(edge_z) - edge_z) - (edge_x[up] - edge_x[z]))
        new[7][z] = state[7][z] + (along_y - shared["along_x"])
    return new


def step_kernel(
    cells, peers, rows,
    shear_ref, weight_ref, joined_ref, up_hbm, down_hbm,
    out_ref, state_ref, mid_ref, up_ref, down_ref, up_sem, down_sem,
):
    up_copy = pltpu.make_async_copy(up_hbm, up_ref, up_sem)
    down_copy = pltpu.make_async_copy(down_hbm, down_ref, down_sem)
    up_copy.start()
    down_copy.start()
    own = plan(shear_ref[0], cells, peers)[0]
    lane = lane_index()
    row = row_index()
    single = tiles_for(cells)
    window = single + 1
    pairs = FIELDS // 2

    for f in range(FIELDS):
        for t, tile in enumerate(cut_window(joined_ref, f, own, window)):
            for z in range(PLANES):
                state_ref[t, f, z] = turn_rows(tile, -z * rows)
    up_copy.wait()
    down_copy.wait()
    for f in range(FIELDS):
        pair, second = divmod(f, 2)
        for t in range(window):
            if t < single:
                up = up_ref[pair * single + t]
                down = down_ref[pair * single + t]
            else:
                back = (LANES - pair * TAIL) % LANES
                up = turn_lanes(up_ref[pairs * single], back)
                down = turn_lanes(down_ref[pairs * single + 1], back)
            for z in range(PLANES):
                up_at = z * rows + (0 if second else SENT)
                down_at = z * rows + (SENT if second else 0)
                value = state_ref[t, f, z]
                value = jnp.where(row < rows, value, turn_rows(down, rows - down_at))
                value = jnp.where(row < rows + SENT, value, turn_rows(up, rows + SENT - up_at))
                state_ref[t, f, z] = value
    last = rows + SENT - 1

    def faces_beyond(t, face_x):
        if t < single:
            beyond = [turn_rows(down_ref[pairs * single], last - t * PLANES - z) for z in range(PLANES)]
        else:
            tile = turn_lanes(down_ref[pairs * single + 1], LANES - pairs * TAIL)
            beyond = [turn_rows(tile, last - (z * rows + SENT)) for z in range(PLANES)]
        return [jnp.where(row == last, b, radial_next(face)) for b, face in zip(beyond, face_x)]

    def terms(ref, t, count, beyond):
        state = [[ref[t, f, z] for z in range(PLANES)] for f in range(FIELDS)]
        if beyond:
            next_face_x = faces_beyond(t, state[FACE_X])
        else:
            next_face_x = [radial_next(face) for face in state[FACE_X]]
        next_face_y = []
        for z in range(PLANES):
            here = turn_lanes(state[6][z], LANES - 1)
            if t + 1 < count:
                there = turn_lanes(ref[t + 1, 6, z], LANES - 1)
                here = jnp.where(lane < LANES - 1, here, there)
            next_face_y.append(here)
        return state, cell_terms(state, next_face_x, next_face_y)

    low = here = terms(state_ref, 0, window, True)
    for t in range(window):
        high = terms(state_ref, t + 1, window, True) if t + 1 < window else here
        new = tile_step(here[0], low[1], here[1], high[1])
        for f in range(FIELDS):
            for z in range(PLANES):
                if t < single or f == 6:
                    mid_ref[t, f, z] = new[f][z]
        low, here = here, high

    weight = weight_ref[...]
    keep = 1.0 - weight
    low = here = terms(mid_ref, 0, window, False)
    low_done = None
    low_moved = None

    def emit(t, moved):
        for f in range(FIELDS):
            out_ref[f, t] = moved[f]

    for t in range(single):
        high = terms(mid_ref, t + 1, window, False) if t + 1 < single else here
        new = tile_step(here[0], low[1], here[1], high[1])
        done = []
        moved = []
        for f in range(FIELDS):
            mixed = []
            turned = []
            for z in range(PLANES):
                value = 0.5 * (state_ref[t, f, z] + new[f][z])
                below = turn_lanes(value, 1)
                turned.append(below)
                if t:
                    below = jnp.where(lane > 0, below, low_done[f][z])
                mixed.append(keep * value + weight * below)
            done.append(turned)
            both = jnp.where(row < rows, mixed[0], turn_rows(mixed[1], rows))
            moved.append(turn_lanes(both, LANES - BELOW))
        if t:
            emit(
                t - 1,
                [jnp.where(lane < LANES - BELOW, a, b) for a, b in zip(low_moved, moved)],
            )
        low_done, low_moved = done, moved
        low, here = here, high
    emit(single - 1, low_moved)


def partner_order(offset, chips):
    bits = chips.bit_length() - 1
    return sum(((offset >> b) & 1) << (bits - 1 - b) for b in range(bits))


def row_sources(shift, own, cells, peers, target):
    shift = shift - (cells - BELOW - own)
    shift = jnp.where(shift < 0, shift + cells * peers, shift)
    hops, rest = hops_of(shift, cells, peers)
    upper = (target + peers - hops) & (peers - 1)
    lower = (target + peers - 1 - hops) & (peers - 1)
    return upper, lower, rest


def pick_kernel(target, pick_ref, *refs):
    in_refs, out_ref = (refs[:-1], refs[-1])
    count = out_ref.shape[1]
    block = pick_ref[target, 0]
    amount = pick_ref[target, 1]
    lane = lane_index()
    fine = amount & (LANES - 1)
    source = (lane - fine) & (LANES - 1)
    chosen = [block == i for i in range(len(in_refs))]
    for f in range(FIELDS):
        tiles = [in_refs[0][f, t] for t in range(count)]
        for mask, ref in zip(chosen[1:], in_refs[1:]):
            tiles = [jnp.where(mask, ref[f, t], tiles[t]) for t in range(count)]
        step = 1
        while step < count:
            moves = (amount & (step * LANES)) != 0
            tiles = [jnp.where(moves, tiles[(t - step) % count], tiles[t]) for t in range(count)]
            step *= 2
        tiles = [
            jnp.take_along_axis(tile, source, axis=1, mode="promise_in_bounds") for tile in tiles
        ]
        for t in range(count):
            out_ref[f, t] = jnp.where(lane < fine, tiles[t - 1], tiles[t])


def merge_kernel(cells, rows, border_ref, mine_ref, other_ref, out_hbm, out_ref, out_sem):
    count = mine_ref.shape[1]
    border = border_ref[0]
    held = border_ref[1] == 1
    masks = [(lane_index() + t * LANES >= border) == held for t in range(count)]
    for f in range(FIELDS):
        tiles = [jnp.where(masks[t], mine_ref[f, t], other_ref[f, t]) for t in range(count)]
        value = jnp.concatenate(tiles, axis=1)[:, :cells]
        for z in range(PLANES):
            out_ref[f, z] = value[z * rows : (z + 1) * rows]
        pltpu.make_async_copy(out_ref.at[f], out_hbm.at[f], out_sem.at[f]).start()
    for f in range(FIELDS):
        pltpu.make_async_copy(out_ref.at[f], out_hbm.at[f], out_sem.at[f]).wait()


def solution(mesh):
    places, peers = (mesh.shape["gx"], mesh.shape["gy"])
    smem = pl.BlockSpec(memory_space=pltpu.SMEM)
    vmem = pl.BlockSpec(memory_space=pltpu.VMEM)
    hbm = pl.BlockSpec(memory_space=pltpu.HBM)
    params = pltpu.CompilerParams(vmem_limit_bytes=8 * 2**20)
    axes = ("gx", "gy")

    def array(*shape):
        return jax.ShapeDtypeStruct(shape + (SUBLANES, LANES), jnp.float32)

    def scratch(*shape):
        return pltpu.VMEM(shape + (SUBLANES, LANES), jnp.float32)

    def device(x, y):
        return x % places * peers + y % peers

    devices = [(x, y) for x in range(places) for y in range(peers)]

    def ghosts(up_hop, down_hop, up, down):
        rise = [(device(x, y), device(x + 1, y + up_hop * (x == places - 1))) for x, y in devices]
        fall = [(device(x, y), device(x - 1, y - down_hop * (x == 0))) for x, y in devices]
        up = lax.ppermute(up, axes, rise)
        return up, lax.ppermute(down, axes, fall)

    def shards(state, shear_offset, remap_shift, frac_index):
        rows, cells = state.shape[2:]
        single = tiles_for(cells)
        double = tiles_for(2 * cells)
        window = tiles_for(BELOW + cells + ABOVE)
        below = lax.ppermute(state, "gy", [(i, (i + 1) % peers) for i in range(peers)])
        numbers = lambda *shape: jax.ShapeDtypeStruct(shape + (SUBLANES, LANES), jnp.int32)
        upper, weight, pick, border = pl.pallas_call(
            lambda *refs: lay_kernel(cells, peers, *refs),
            out_shape=[array(FIELDS, single), array(), numbers(2, 2), numbers(2)],
            in_specs=[smem] * 3 + [vmem],
            out_specs=[vmem] * 4,
            compiler_params=params,
            name="lay",
        )(shear_offset, remap_shift, frac_index, state)
        edge = FIELDS // 2 * single + 2
        joined, up, down = pl.pallas_call(
            lambda *refs: pair_kernel(cells, peers, rows, *refs),
            out_shape=[array(FIELDS, double), array(edge), array(edge)],
            in_specs=[smem, vmem, vmem],
            out_specs=[vmem] * 3,
            compiler_params=params,
            name="pair",
        )(shear_offset, upper, below)
        _, _, _, up_hop, down_hop = plan(shear_offset[0], cells, peers)
        branches = [
            lambda u, d, i=i: ghosts(i // 2 + i % 2, i // 2, u, d) for i in range(2 * peers)
        ]
        which = (down_hop + up_hop) & (2 * peers - 1)
        up, down = lax.switch(which, branches, up, down)
        block = pl.pallas_call(
            lambda *refs: step_kernel(cells, peers, rows, *refs),
            out_shape=array(FIELDS, single),
            in_specs=[smem] + [vmem] * 2 + [hbm] * 2,
            out_specs=vmem,
            scratch_shapes=[scratch(window, FIELDS, PLANES)] * 2
            + [scratch(edge), scratch(edge)]
            + [pltpu.SemaphoreType.DMA] * 2,
            compiler_params=params,
            name="step",
        )(shear_offset, weight, joined, up, down)

        def exchange(value, bits):
            return lax.ppermute(value, "gy", [(i, i ^ bits) for i in range(peers)])

        def across(offset):
            offsets = (offset, partner_order(offset, peers // 2))
            return lax.ppermute(block, "gy", [(i, i ^ (2 * offsets[i % 2])) for i in range(peers)])

        far = [across(offset) for offset in range(peers // 2 - 1, 0, -1)]

        def picked(target, name):
            return pl.pallas_call(
                lambda pick_ref, *refs: pick_kernel(target, pick_ref, *refs[-2::-1], refs[-1]),
                out_shape=array(FIELDS, single),
                in_specs=[vmem] * (1 + peers // 2),
                out_specs=vmem,
                compiler_params=params,
                name=name,
            )(pick, *far, block)

        other = exchange(picked(0, "gather"), 1)
        mine = picked(1, "keep")
        return pl.pallas_call(
            lambda *refs: merge_kernel(cells, rows, *refs),
            out_shape=jax.ShapeDtypeStruct(state.shape, jnp.float32),
            in_specs=[vmem] * 3,
            out_specs=hbm,
            scratch_shapes=[
                pltpu.VMEM(state.shape, jnp.float32),
                pltpu.SemaphoreType.DMA((FIELDS,)),
            ],
            compiler_params=params,
            name="merge",
        )(border, mine, other)

    placed = (P(None, None, "gx", "gy"), P(), P("gx"), P("gx"))
    return jax.shard_map(
        shards, mesh=mesh, in_specs=placed, out_specs=P(None, None, "gx", "gy"), check_vma=False
    )
```

```python
import jax
import jax.numpy as jnp
from jax import lax
from jax.experimental import pallas as pl
from jax.experimental.pallas import tpu as pltpu
from jax.sharding import PartitionSpec as P

FRAC = 16

ADIABATIC = 5.0 / 3.0
ROTATION = 1.0
SHEAR_RATE = 1.5
MAX_SPEED = 5.0
TIME_STEP = 0.05

LANES = 128
LANE_BITS = 7
SUBLANES = 8
FIELDS = 8
PLANES = 2
FACE_X = 5
BELOW = 3
ABOVE = 3
TAIL = 4
SENT = 2
HALF_STEP = 0.5 * TIME_STEP
DIFFUSE = 0.5 * MAX_SPEED * TIME_STEP
EDGE = 0.25 * TIME_STEP


def lane_index():
    return lax.broadcasted_iota(jnp.int32, (SUBLANES, LANES), 1)


def row_index():
    return lax.broadcasted_iota(jnp.int32, (SUBLANES, LANES), 0)


def turn_lanes(value, amount):
    return pltpu.roll(value, amount, 1)


def turn_rows(value, amount):
    amount %= SUBLANES
    return pltpu.roll(value, amount, 0) if amount else value


def radial_next(value):
    return turn_rows(value, -1)


def radial_prev(value):
    return turn_rows(value, 1)


def tiles_for(columns):
    return -(-columns // LANES)


def hops_of(columns, cells, peers):
    hops = sum(jnp.where(columns >= k * cells, 1, 0) for k in range(1, peers))
    return hops, columns - hops * cells


def plan(shear, cells, peers):
    hops, rest = hops_of(shear, cells, peers)
    middle = cells // 2
    near = (rest >= middle - 5) & (rest <= middle + 5)
    own = jnp.where(near, middle - 12, middle)
    up_hop = jnp.where(rest > own, 1, 0)
    down_hop = jnp.where(rest + own >= cells, 1, 0)
    up = own - rest + up_hop * cells
    down = own + rest - down_hop * cells
    return own, up, down, hops + up_hop, hops + down_hop


def block_tiles(ref, f, cells):
    value = jnp.concatenate([ref[f, z] for z in range(PLANES)], axis=0)
    tiles = []
    for i in range(0, cells, LANES):
        tile = value[:, i : min(i + LANES, cells)]
        spare = LANES - tile.shape[1]
        if spare:
            tile = jnp.concatenate([tile, jnp.zeros((SUBLANES, spare), tile.dtype)], axis=1)
        tiles.append(tile)
    return tiles


def lay_kernel(
    cells, peers, shear_ref, shift_ref, frac_ref, state_ref,
    out_ref, weight_ref, pick_ref, border_ref,
):
    rows = state_ref.shape[2]
    part = lax.axis_index("gy")
    own = plan(shear_ref[0], cells, peers)[0]
    row = row_index()
    spare = tiles_for(cells) * LANES - cells
    blank = jnp.zeros((SUBLANES, LANES), jnp.int32)
    weight = jnp.zeros((SUBLANES, LANES), jnp.float32)
    picks = [[blank, blank], [blank, blank]]
    border = held = blank
    for x in range(rows):
        level = (frac_ref[x].astype(jnp.float32) + 0.5) / FRAC
        weight = jnp.where(row == x, level, weight)
        here = row % rows == x
        for i, target in enumerate((part ^ 1, part)):
            upper, lower, rest = row_sources(shift_ref[x], own, cells, peers, target)
            first = ((upper ^ part) & 1) == 0
            block = (jnp.where(first, upper, lower) ^ part) >> 1
            amount = jnp.where(first, rest, rest + spare)
            picks[i] = [jnp.where(here, a, b) for a, b in zip((block, amount), picks[i])]
            if target is part:
                border = jnp.where(here, rest, border)
                held = jnp.where(here, jnp.where(first, 1, 0), held)
    weight_ref[...] = weight
    for i in range(2):
        for k in range(2):
            pick_ref[i, k] = picks[i][k]
    border_ref[0] = border
    border_ref[1] = held
    for f in range(FIELDS):
        for t, tile in enumerate(block_tiles(state_ref, f, cells)):
            out_ref[f, t] = turn_lanes(tile, cells % LANES)


def pair_kernel(cells, peers, rows, shear_ref, upper_ref, below_ref, joined_ref, up_ref, down_ref):
    place = lax.axis_index("gx")
    places = lax.axis_size("gx")
    own, up, down, _, _ = plan(shear_ref[0], cells, peers)
    up = jnp.where(place == places - 1, up, own)
    down = jnp.where(place == 0, down, own)
    lane = lane_index()
    row = row_index()
    single = tiles_for(cells)
    gap = cells % LANES
    window = single + 1
    for f in range(FIELDS):
        lower = block_tiles(below_ref, f, cells)
        upper = [upper_ref[f, t] for t in range(single)]
        for i in range(single - 1):
            joined_ref[f, i] = lower[i]
        joined_ref[f, single - 1] = jnp.where(lane < gap, lower[-1], upper[0])
        for k in range(single):
            following = upper[min(k + 1, single - 1)]
            joined_ref[f, single + k] = jnp.where(lane < gap, upper[k], following)

    late = row % rows >= SENT
    pairs = FIELDS // 2
    up_tail = down_tail = jnp.zeros((SUBLANES, LANES), jnp.float32)

    def tail(tile, index, so_far):
        return jnp.where(lane // TAIL == index, turn_lanes(tile, index * TAIL), so_far)

    for pair in range(pairs):
        ups = [cut_window(joined_ref, 2 * pair + i, up, window) for i in range(2)]
        downs = [cut_window(joined_ref, 2 * pair + i, down, window) for i in range(2)]
        ups = [jnp.where(late, a, turn_rows(b, -SENT)) for a, b in zip(*ups)]
        downs = [jnp.where(late, turn_rows(b, SENT), a) for a, b in zip(*downs)]
        for t in range(single):
            up_ref[pair * single + t] = ups[t]
            down_ref[pair * single + t] = downs[t]
        up_tail = tail(ups[single], pair, up_tail)
        down_tail = tail(downs[single], pair, down_tail)
    faces = jnp.zeros((SUBLANES, LANES), jnp.float32)
    tiles = cut_window(joined_ref, FACE_X, down, window)
    for t in range(single):
        for z in range(PLANES):
            at = t * PLANES + z
            faces = jnp.where(row == at, turn_rows(tiles[t], at - (z * rows + SENT)), faces)
    down_ref[pairs * single] = faces
    up_ref[pairs * single] = up_tail
    down_ref[pairs * single + 1] = tail(tiles[single], pairs, down_tail)


def cut_window(joined_ref, f, start, count):
    whole = start >> LANE_BITS
    part = start & (LANES - 1)
    last = joined_ref.shape[1] - 1
    tiles = [joined_ref[f, jnp.minimum(whole + t, last)] for t in range(count + 1)]
    turned = [turn_lanes(tile, (LANES - part) & (LANES - 1)) for tile in tiles]
    here = lane_index() < LANES - part
    return [jnp.where(here, turned[t], turned[t + 1]) for t in range(count)]


def cell_terms(state, next_face_x, next_face_y):
    planes = range(PLANES)
    face_z = state[7]
    out = []
    for z in planes:
        density, mom_x, mom_y, mom_z, energy, face_x, face_y = (state[f][z] for f in range(7))
        cen_x = 0.5 * (face_x + next_face_x[z])
        cen_y = 0.5 * (face_y + next_face_y[z])
        cen_z = 0.5 * (face_z[z] + face_z[(z + 1) % PLANES])
        inverse = 1.0 / density
        vel_x, vel_y, vel_z = (mom_x * inverse, mom_y * inverse, mom_z * inverse)
        magnetic = 0.5 * (cen_x * cen_x + cen_y * cen_y + cen_z * cen_z)
        kinetic = 0.5 * (mom_x * vel_x + mom_y * vel_y + mom_z * vel_z)
        pressure = (ADIABATIC - 1.0) * (energy - kinetic - magnetic) + magnetic
        vel_dot = vel_x * cen_x + vel_y * cen_y + vel_z * cen_z
        scaled_p = HALF_STEP * pressure
        total = energy + pressure
        sv_x, sv_y, sv_z = (HALF_STEP * vel_x, HALF_STEP * vel_y, HALF_STEP * vel_z)
        sb_x, sb_y, sb_z = (HALF_STEP * cen_x, HALF_STEP * cen_y, HALF_STEP * cen_z)
        xx = mom_x * sv_x - cen_x * sb_x + scaled_p
        yy = mom_y * sv_y - cen_y * sb_y + scaled_p
        zz = mom_z * sv_z - cen_z * sb_z + scaled_p
        xy = mom_x * sv_y - cen_x * sb_y
        xz = mom_x * sv_z - cen_x * sb_z
        yz = mom_y * sv_z - cen_y * sb_z
        diffuse = [DIFFUSE * state[f][z] for f in range(5)]
        flux_x = [HALF_STEP * mom_x, xx, xy, xz, total * sv_x - sb_x * vel_dot]
        flux_y = [HALF_STEP * mom_y, xy, yy, yz, total * sv_y - sb_y * vel_dot]
        flux_z = [HALF_STEP * mom_z, xz, yz, zz, total * sv_z - sb_z * vel_dot]
        e_z = EDGE * (vel_y * cen_x - vel_x * cen_y)
        pair = e_z + radial_prev(e_z)
        out.append(
            dict(
                diffuse=diffuse,
                along_x=[
                    radial_next(f - d) - radial_prev(f + d) for f, d in zip(flux_x, diffuse)
                ],
                low_y=[turn_lanes(f + d, 1) for f, d in zip(flux_y, diffuse)],
                high_y=[turn_lanes(f - d, LANES - 1) for f, d in zip(flux_y, diffuse)],
                flux_z=flux_z,
                shear=xy,
                e_x=EDGE * (vel_z * cen_y - vel_y * cen_z),
                e_y=EDGE * (vel_x * cen_z - vel_z * cen_x),
                pair=pair,
                low_pair=turn_lanes(pair, 1),
                high_pair=turn_lanes(pair, LANES - 1),
            )
        )
    e_x, e_y = (
        [sum((cell[name] for cell in out[1:]), out[0][name]) for name in ("e_x", "e_y")]
    )
    shared = dict(
        e_x=e_x,
        low_e_x=turn_lanes(e_x, 1),
        high_e_x=turn_lanes(e_x, LANES - 1),
        edge_y=[e_y + radial_prev(e_y)] * PLANES,
        along_x=radial_next(e_y) - radial_prev(e_y),
    )
    return out, shared


def tile_step(state, low, here, high):
    lane = lane_index()
    cells_low, shared_low = low
    cells, shared = here
    cells_high, shared_high = high

    def before(turned_low, turned):
        return jnp.where(lane > 0, turned, turned_low)

    def after(turned, turned_high):
        return jnp.where(lane < LANES - 1, turned, turned_high)

    new = [[None] * PLANES for f in range(FIELDS)]
    faces = [
        [
            (cells[z - 1]["flux_z"][f] + cells[z]["flux_z"][f])
            - (cells[z]["diffuse"][f] - cells[z - 1]["diffuse"][f])
            for f in range(5)
        ]
        for z in range(PLANES)
    ]
    low_e_x = before(shared_low["low_e_x"], shared["low_e_x"])
    along_y = after(shared["high_e_x"], shared_high["high_e_x"]) - low_e_x
    edge_x = [shared["e_x"] + low_e_x] * PLANES
    edge_y = shared["edge_y"]
    for z in range(PLANES):
        cell = cells[z]
        up = (z + 1) % PLANES
        for f in range(5):
            high_y = after(cell["high_y"][f], cells_high[z]["high_y"][f])
            low_y = before(cells_low[z]["low_y"][f], cell["low_y"][f])
            along_z = faces[up][f] - faces[z][f]
            kept = state[f][z] - 4.0 * cell["diffuse"][f]
            new[f][z] = kept - (cell["along_x"][f] + (high_y - low_y) + along_z)
        mom_x, mom_y = (state[1][z], state[2][z])
        new[1][z] = new[1][z] + (TIME_STEP * 2.0 * ROTATION) * mom_y
        new[2][z] = new[2][z] - (TIME_STEP * (2.0 - SHEAR_RATE) * ROTATION) * mom_x
        new[4][z] = new[4][z] + (2.0 * SHEAR_RATE * ROTATION) * cell["shear"]
        low_pair = before(cells_low[z]["low_pair"], cell["low_pair"])
        high_pair = after(cell["high_pair"], cells_high[z]["high_pair"])
        edge_z = cell["pair"] + low_pair
        new[5][z] = state[5][z] + ((edge_y[up] - edge_y[z]) - (high_pair - low_pair))
        new[6][z] = state[6][z] + ((radial_next(edge_z) - edge_z) - (edge_x[up] - edge_x[z]))
        new[7][z] = state[7][z] + (along_y - shared["along_x"])
    return new


def step_kernel(
    cells, peers, rows,
    shear_ref, weight_ref, joined_ref, up_ref, down_ref, out_ref, state_ref, mid_ref
):
    own = plan(shear_ref[0], cells, peers)[0]
    lane = lane_index()
    row = row_index()
    single = tiles_for(cells)
    window = single + 1
    pairs = FIELDS // 2

    for f in range(FIELDS):
        for t, tile in enumerate(cut_window(joined_ref, f, own, window)):
            for z in range(PLANES):
                state_ref[t, f, z] = turn_rows(tile, -z * rows)
    for f in range(FIELDS):
        pair, second = divmod(f, 2)
        for t in range(window):
            if t < single:
                up = up_ref[pair * single + t]
                down = down_ref[pair * single + t]
            else:
                back = (LANES - pair * TAIL) % LANES
                up = turn_lanes(up_ref[pairs * single], back)
                down = turn_lanes(down_ref[pairs * single + 1], back)
            for z in range(PLANES):
                up_at = z * rows + (0 if second else SENT)
                down_at = z * rows + (SENT if second else 0)
                value = state_ref[t, f, z]
                value = jnp.where(row < rows, value, turn_rows(down, rows - down_at))
                value = jnp.where(row < rows + SENT, value, turn_rows(up, rows + SENT - up_at))
                state_ref[t, f, z] = value
    last = rows + SENT - 1

    def faces_beyond(t, face_x):
        if t < single:
            beyond = [turn_rows(down_ref[pairs * single], last - t * PLANES - z) for z in range(PLANES)]
        else:
            tile = turn_lanes(down_ref[pairs * single + 1], LANES - pairs * TAIL)
            beyond = [turn_rows(tile, last - (z * rows + SENT)) for z in range(PLANES)]
        return [jnp.where(row == last, b, radial_next(face)) for b, face in zip(beyond, face_x)]

    def terms(ref, t, count, beyond):
        state = [[ref[t, f, z] for z in range(PLANES)] for f in range(FIELDS)]
        if beyond:
            next_face_x = faces_beyond(t, state[FACE_X])
        else:
            next_face_x = [radial_next(face) for face in state[FACE_X]]
        next_face_y = []
        for z in range(PLANES):
            here = turn_lanes(state[6][z], LANES - 1)
            if t + 1 < count:
                there = turn_lanes(ref[t + 1, 6, z], LANES - 1)
                here = jnp.where(lane < LANES - 1, here, there)
            next_face_y.append(here)
        return state, cell_terms(state, next_face_x, next_face_y)

    low = here = terms(state_ref, 0, window, True)
    for t in range(window):
        high = terms(state_ref, t + 1, window, True) if t + 1 < window else here
        new = tile_step(here[0], low[1], here[1], high[1])
        for f in range(FIELDS):
            for z in range(PLANES):
                if t < single or f == 6:
                    mid_ref[t, f, z] = new[f][z]
        low, here = here, high

    weight = weight_ref[...]
    keep = 1.0 - weight
    low = here = terms(mid_ref, 0, window, False)
    low_done = None
    low_moved = None

    def emit(t, moved):
        for f in range(FIELDS):
            out_ref[f, t] = moved[f]

    for t in range(single):
        high = terms(mid_ref, t + 1, window, False) if t + 1 < single else here
        new = tile_step(here[0], low[1], here[1], high[1])
        done = []
        moved = []
        for f in range(FIELDS):
            mixed = []
            turned = []
            for z in range(PLANES):
                value = 0.5 * (state_ref[t, f, z] + new[f][z])
                below = turn_lanes(value, 1)
                turned.append(below)
                if t:
                    below = jnp.where(lane > 0, below, low_done[f][z])
                mixed.append(keep * value + weight * below)
            done.append(turned)
            both = jnp.where(row < rows, mixed[0], turn_rows(mixed[1], rows))
            moved.append(turn_lanes(both, LANES - BELOW))
        if t:
            emit(
                t - 1,
                [jnp.where(lane < LANES - BELOW, a, b) for a, b in zip(low_moved, moved)],
            )
        low_done, low_moved = done, moved
        low, here = here, high
    emit(single - 1, low_moved)


def row_sources(shift, own, cells, peers, target):
    shift = shift - (cells - BELOW - own)
    shift = jnp.where(shift < 0, shift + cells * peers, shift)
    hops, rest = hops_of(shift, cells, peers)
    upper = (target + peers - hops) & (peers - 1)
    lower = (target + peers - 1 - hops) & (peers - 1)
    return upper, lower, rest


def pick_kernel(target, pick_ref, *refs):
    in_refs, out_ref = (refs[:-1], refs[-1])
    count = out_ref.shape[1]
    block = pick_ref[target, 0]
    amount = pick_ref[target, 1]
    lane = lane_index()
    fine = amount & (LANES - 1)
    source = (lane - fine) & (LANES - 1)
    chosen = [block == i for i in range(len(in_refs))]
    for f in range(FIELDS):
        tiles = [in_refs[0][f, t] for t in range(count)]
        for mask, ref in zip(chosen[1:], in_refs[1:]):
            tiles = [jnp.where(mask, ref[f, t], tiles[t]) for t in range(count)]
        step = 1
        while step < count:
            moves = (amount & (step * LANES)) != 0
            tiles = [jnp.where(moves, tiles[(t - step) % count], tiles[t]) for t in range(count)]
            step *= 2
        tiles = [
            jnp.take_along_axis(tile, source, axis=1, mode="promise_in_bounds") for tile in tiles
        ]
        for t in range(count):
            out_ref[f, t] = jnp.where(lane < fine, tiles[t - 1], tiles[t])


def merge_kernel(cells, rows, border_ref, mine_ref, other_ref, out_hbm, out_ref, out_sem):
    count = mine_ref.shape[1]
    border = border_ref[0]
    held = border_ref[1] == 1
    masks = [(lane_index() + t * LANES >= border) == held for t in range(count)]
    for f in range(FIELDS):
        tiles = [jnp.where(masks[t], mine_ref[f, t], other_ref[f, t]) for t in range(count)]
        value = jnp.concatenate(tiles, axis=1)[:, :cells]
        for z in range(PLANES):
            out_ref[f, z] = value[z * rows : (z + 1) * rows]
        pltpu.make_async_copy(out_ref.at[f], out_hbm.at[f], out_sem.at[f]).start()
    for f in range(FIELDS):
        pltpu.make_async_copy(out_ref.at[f], out_hbm.at[f], out_sem.at[f]).wait()


def solution(mesh):
    places, peers = (mesh.shape["gx"], mesh.shape["gy"])
    smem = pl.BlockSpec(memory_space=pltpu.SMEM)
    vmem = pl.BlockSpec(memory_space=pltpu.VMEM)
    hbm = pl.BlockSpec(memory_space=pltpu.HBM)
    params = pltpu.CompilerParams(vmem_limit_bytes=8 * 2**20)
    axes = ("gx", "gy")

    def array(*shape):
        return jax.ShapeDtypeStruct(shape + (SUBLANES, LANES), jnp.float32)

    def scratch(*shape):
        return pltpu.VMEM(shape + (SUBLANES, LANES), jnp.float32)

    def device(x, y):
        return x % places * peers + y % peers

    devices = [(x, y) for x in range(places) for y in range(peers)]

    def ghosts(up_hop, down_hop, up, down):
        rise = [(device(x, y), device(x + 1, y + up_hop * (x == places - 1))) for x, y in devices]
        fall = [(device(x, y), device(x - 1, y - down_hop * (x == 0))) for x, y in devices]
        up = lax.ppermute(up, axes, rise)
        return up, lax.ppermute(down, axes, fall)

    def shards(state, shear_offset, remap_shift, frac_index):
        rows, cells = state.shape[2:]
        single = tiles_for(cells)
        double = tiles_for(2 * cells)
        window = tiles_for(BELOW + cells + ABOVE)
        below = lax.ppermute(state, "gy", [(i, (i + 1) % peers) for i in range(peers)])
        numbers = lambda *shape: jax.ShapeDtypeStruct(shape + (SUBLANES, LANES), jnp.int32)
        upper, weight, pick, border = pl.pallas_call(
            lambda *refs: lay_kernel(cells, peers, *refs),
            out_shape=[array(FIELDS, single), array(), numbers(2, 2), numbers(2)],
            in_specs=[smem] * 3 + [vmem],
            out_specs=[vmem] * 4,
            compiler_params=params,
            name="lay",
        )(shear_offset, remap_shift, frac_index, state)
        edge = FIELDS // 2 * single + 2
        joined, up, down = pl.pallas_call(
            lambda *refs: pair_kernel(cells, peers, rows, *refs),
            out_shape=[array(FIELDS, double), array(edge), array(edge)],
            in_specs=[smem, vmem, vmem],
            out_specs=[vmem] * 3,
            compiler_params=params,
            name="pair",
        )(shear_offset, upper, below)
        def finish(up_hop, down_hop, up, down):
            up, down = ghosts(up_hop, down_hop, up, down)
            return pl.pallas_call(
                lambda *refs: step_kernel(cells, peers, rows, *refs),
                out_shape=array(FIELDS, single),
                in_specs=[smem] + [vmem] * 4,
                out_specs=vmem,
                scratch_shapes=[scratch(window, FIELDS, PLANES)] * 2,
                compiler_params=params,
                name="step",
            )(shear_offset, weight, joined, up, down)

        _, _, _, up_hop, down_hop = plan(shear_offset[0], cells, peers)
        branches = [
            lambda u, d, i=i: finish(i // 2 + i % 2, i // 2, u, d) for i in range(2 * peers)
        ]
        which = (down_hop + up_hop) & (2 * peers - 1)
        block = lax.switch(which, branches, up, down)

        def exchange(value, bits):
            return lax.ppermute(value, "gy", [(i, i ^ bits) for i in range(peers)])

        far = [exchange(block, bits) for bits in range(peers - 2, 0, -2)]

        def picked(target, name):
            return pl.pallas_call(
                lambda pick_ref, *refs: pick_kernel(target, pick_ref, *refs[-2::-1], refs[-1]),
                out_shape=array(FIELDS, single),
                in_specs=[vmem] * (1 + peers // 2),
                out_specs=vmem,
                compiler_params=params,
                name=name,
            )(pick, *far, block)

        other = exchange(picked(0, "gather"), 1)
        mine = picked(1, "keep")
        return pl.pallas_call(
            lambda *refs: merge_kernel(cells, rows, *refs),
            out_shape=jax.ShapeDtypeStruct(state.shape, jnp.float32),
            in_specs=[vmem] * 3,
            out_specs=hbm,
            scratch_shapes=[
                pltpu.VMEM(state.shape, jnp.float32),
                pltpu.SemaphoreType.DMA((FIELDS,)),
            ],
            compiler_params=params,
            name="merge",
        )(border, mine, other)

    placed = (P(None, None, "gx", "gy"), P(), P("gx"), P("gx"))
    return jax.shard_map(
        shards, mesh=mesh, in_specs=placed, out_specs=P(None, None, "gx", "gy"), check_vma=False
    )
```

```python
import jax
import jax.numpy as jnp
from jax import lax
from jax.experimental import pallas as pl
from jax.experimental.pallas import tpu as pltpu
from jax.sharding import PartitionSpec as P

FRAC = 16

ADIABATIC = 5.0 / 3.0
ROTATION = 1.0
SHEAR_RATE = 1.5
MAX_SPEED = 5.0
TIME_STEP = 0.05

LANES = 128
LANE_BITS = 7
SUBLANES = 8
FIELDS = 8
PLANES = 2
FACE_X = 5
BELOW = 3
ABOVE = 3
TAIL = 4
SENT = 2
HALF_STEP = 0.5 * TIME_STEP
DIFFUSE = 0.5 * MAX_SPEED * TIME_STEP
EDGE = 0.25 * TIME_STEP


def lane_index():
    return lax.broadcasted_iota(jnp.int32, (SUBLANES, LANES), 1)


def row_index():
    return lax.broadcasted_iota(jnp.int32, (SUBLANES, LANES), 0)


def turn_lanes(value, amount):
    return pltpu.roll(value, amount, 1)


def turn_rows(value, amount):
    amount %= SUBLANES
    return pltpu.roll(value, amount, 0) if amount else value


def radial_next(value):
    return turn_rows(value, -1)


def radial_prev(value):
    return turn_rows(value, 1)


def tiles_for(columns):
    return -(-columns // LANES)


def hops_of(columns, cells, peers):
    hops = sum(jnp.where(columns >= k * cells, 1, 0) for k in range(1, peers))
    return hops, columns - hops * cells


def plan(shear, cells, peers):
    hops, rest = hops_of(shear, cells, peers)
    middle = cells // 2
    near = (rest >= middle - 5) & (rest <= middle + 5)
    own = jnp.where(near, middle - 12, middle)
    up_hop = jnp.where(rest > own, 1, 0)
    down_hop = jnp.where(rest + own >= cells, 1, 0)
    up = own - rest + up_hop * cells
    down = own + rest - down_hop * cells
    return own, up, down, hops + up_hop, hops + down_hop


def block_tiles(ref, f, cells):
    value = jnp.concatenate([ref[f, z] for z in range(PLANES)], axis=0)
    tiles = []
    for i in range(0, cells, LANES):
        tile = value[:, i : min(i + LANES, cells)]
        spare = LANES - tile.shape[1]
        if spare:
            tile = jnp.concatenate([tile, jnp.zeros((SUBLANES, spare), tile.dtype)], axis=1)
        tiles.append(tile)
    return tiles


def lay_kernel(
    cells, peers, shear_ref, shift_ref, frac_ref, state_ref,
    out_ref, weight_ref, pick_ref, border_ref,
):
    rows = state_ref.shape[2]
    part = lax.axis_index("gy")
    own = plan(shear_ref[0], cells, peers)[0]
    row = row_index()
    spare = tiles_for(cells) * LANES - cells
    blank = jnp.zeros((SUBLANES, LANES), jnp.int32)
    weight = jnp.zeros((SUBLANES, LANES), jnp.float32)
    picks = [[blank, blank], [blank, blank]]
    border = held = blank
    for x in range(rows):
        level = (frac_ref[x].astype(jnp.float32) + 0.5) / FRAC
        weight = jnp.where(row == x, level, weight)
        here = row % rows == x
        for i, target in enumerate((part ^ 1, part)):
            upper, lower, rest = row_sources(shift_ref[x], own, cells, peers, target)
            first = ((upper ^ part) & 1) == 0
            block = (jnp.where(first, upper, lower) ^ part) >> 1
            amount = jnp.where(first, rest, rest + spare)
            picks[i] = [jnp.where(here, a, b) for a, b in zip((block, amount), picks[i])]
            if target is part:
                border = jnp.where(here, rest, border)
                held = jnp.where(here, jnp.where(first, 1, 0), held)
    weight_ref[...] = weight
    for i in range(2):
        for k in range(2):
            pick_ref[i, k] = picks[i][k]
    border_ref[0] = border
    border_ref[1] = held
    for f in range(FIELDS):
        for t, tile in enumerate(block_tiles(state_ref, f, cells)):
            out_ref[f, t] = turn_lanes(tile, cells % LANES)


def pair_kernel(cells, peers, rows, shear_ref, upper_ref, below_ref, joined_ref, up_ref, down_ref):
    place = lax.axis_index("gx")
    places = lax.axis_size("gx")
    own, up, down, _, _ = plan(shear_ref[0], cells, peers)
    up = jnp.where(place == places - 1, up, own)
    down = jnp.where(place == 0, down, own)
    lane = lane_index()
    row = row_index()
    single = tiles_for(cells)
    gap = cells % LANES
    window = single + 1
    for f in range(FIELDS):
        lower = block_tiles(below_ref, f, cells)
        upper = [upper_ref[f, t] for t in range(single)]
        for i in range(single - 1):
            joined_ref[f, i] = lower[i]
        joined_ref[f, single - 1] = jnp.where(lane < gap, lower[-1], upper[0])
        for k in range(single):
            following = upper[min(k + 1, single - 1)]
            joined_ref[f, single + k] = jnp.where(lane < gap, upper[k], following)

    late = row % rows >= SENT
    pairs = FIELDS // 2
    up_tail = down_tail = jnp.zeros((SUBLANES, LANES), jnp.float32)

    def tail(tile, index, so_far):
        return jnp.where(lane // TAIL == index, turn_lanes(tile, index * TAIL), so_far)

    for pair in range(pairs):
        ups = [cut_window(joined_ref, 2 * pair + i, up, window) for i in range(2)]
        downs = [cut_window(joined_ref, 2 * pair + i, down, window) for i in range(2)]
        ups = [jnp.where(late, a, turn_rows(b, -SENT)) for a, b in zip(*ups)]
        downs = [jnp.where(late, turn_rows(b, SENT), a) for a, b in zip(*downs)]
        for t in range(single):
            up_ref[pair * single + t] = ups[t]
            down_ref[pair * single + t] = downs[t]
        up_tail = tail(ups[single], pair, up_tail)
        down_tail = tail(downs[single], pair, down_tail)
    faces = jnp.zeros((SUBLANES, LANES), jnp.float32)
    tiles = cut_window(joined_ref, FACE_X, down, window)
    for t in range(single):
        for z in range(PLANES):
            at = t * PLANES + z
            faces = jnp.where(row == at, turn_rows(tiles[t], at - (z * rows + SENT)), faces)
    down_ref[pairs * single] = faces
    up_ref[pairs * single] = up_tail
    down_ref[pairs * single + 1] = tail(tiles[single], pairs, down_tail)


def cut_window(joined_ref, f, start, count):
    whole = start >> LANE_BITS
    part = start & (LANES - 1)
    last = joined_ref.shape[1] - 1
    tiles = [joined_ref[f, jnp.minimum(whole + t, last)] for t in range(count + 1)]
    turned = [turn_lanes(tile, (LANES - part) & (LANES - 1)) for tile in tiles]
    here = lane_index() < LANES - part
    return [jnp.where(here, turned[t], turned[t + 1]) for t in range(count)]


def cell_terms(state, next_face_x, next_face_y):
    planes = range(PLANES)
    face_z = state[7]
    out = []
    for z in planes:
        density, mom_x, mom_y, mom_z, energy, face_x, face_y = (state[f][z] for f in range(7))
        cen_x = 0.5 * (face_x + next_face_x[z])
        cen_y = 0.5 * (face_y + next_face_y[z])
        cen_z = 0.5 * (face_z[z] + face_z[(z + 1) % PLANES])
        inverse = 1.0 / density
        vel_x, vel_y, vel_z = (mom_x * inverse, mom_y * inverse, mom_z * inverse)
        magnetic = 0.5 * (cen_x * cen_x + cen_y * cen_y + cen_z * cen_z)
        kinetic = 0.5 * (mom_x * vel_x + mom_y * vel_y + mom_z * vel_z)
        pressure = (ADIABATIC - 1.0) * (energy - kinetic - magnetic) + magnetic
        vel_dot = vel_x * cen_x + vel_y * cen_y + vel_z * cen_z
        scaled_p = HALF_STEP * pressure
        total = energy + pressure
        sv_x, sv_y, sv_z = (HALF_STEP * vel_x, HALF_STEP * vel_y, HALF_STEP * vel_z)
        sb_x, sb_y, sb_z = (HALF_STEP * cen_x, HALF_STEP * cen_y, HALF_STEP * cen_z)
        xx = mom_x * sv_x - cen_x * sb_x + scaled_p
        yy = mom_y * sv_y - cen_y * sb_y + scaled_p
        zz = mom_z * sv_z - cen_z * sb_z + scaled_p
        xy = mom_x * sv_y - cen_x * sb_y
        xz = mom_x * sv_z - cen_x * sb_z
        yz = mom_y * sv_z - cen_y * sb_z
        diffuse = [DIFFUSE * state[f][z] for f in range(5)]
        flux_x = [HALF_STEP * mom_x, xx, xy, xz, total * sv_x - sb_x * vel_dot]
        flux_y = [HALF_STEP * mom_y, xy, yy, yz, total * sv_y - sb_y * vel_dot]
        flux_z = [HALF_STEP * mom_z, xz, yz, zz, total * sv_z - sb_z * vel_dot]
        e_z = EDGE * (vel_y * cen_x - vel_x * cen_y)
        pair = e_z + radial_prev(e_z)
        out.append(
            dict(
                diffuse=diffuse,
                along_x=[
                    radial_next(f - d) - radial_prev(f + d) for f, d in zip(flux_x, diffuse)
                ],
                low_y=[turn_lanes(f + d, 1) for f, d in zip(flux_y, diffuse)],
                high_y=[turn_lanes(f - d, LANES - 1) for f, d in zip(flux_y, diffuse)],
                flux_z=flux_z,
                shear=xy,
                e_x=EDGE * (vel_z * cen_y - vel_y * cen_z),
                e_y=EDGE * (vel_x * cen_z - vel_z * cen_x),
                pair=pair,
                low_pair=turn_lanes(pair, 1),
                high_pair=turn_lanes(pair, LANES - 1),
            )
        )
    e_x, e_y = (
        [sum((cell[name] for cell in out[1:]), out[0][name]) for name in ("e_x", "e_y")]
    )
    shared = dict(
        e_x=e_x,
        low_e_x=turn_lanes(e_x, 1),
        high_e_x=turn_lanes(e_x, LANES - 1),
        edge_y=[e_y + radial_prev(e_y)] * PLANES,
        along_x=radial_next(e_y) - radial_prev(e_y),
    )
    return out, shared


def tile_step(state, low, here, high):
    lane = lane_index()
    cells_low, shared_low = low
    cells, shared = here
    cells_high, shared_high = high

    def before(turned_low, turned):
        return jnp.where(lane > 0, turned, turned_low)

    def after(turned, turned_high):
        return jnp.where(lane < LANES - 1, turned, turned_high)

    new = [[None] * PLANES for f in range(FIELDS)]
    faces = [
        [
            (cells[z - 1]["flux_z"][f] + cells[z]["flux_z"][f])
            - (cells[z]["diffuse"][f] - cells[z - 1]["diffuse"][f])
            for f in range(5)
        ]
        for z in range(PLANES)
    ]
    low_e_x = before(shared_low["low_e_x"], shared["low_e_x"])
    along_y = after(shared["high_e_x"], shared_high["high_e_x"]) - low_e_x
    edge_x = [shared["e_x"] + low_e_x] * PLANES
    edge_y = shared["edge_y"]
    for z in range(PLANES):
        cell = cells[z]
        up = (z + 1) % PLANES
        for f in range(5):
            high_y = after(cell["high_y"][f], cells_high[z]["high_y"][f])
            low_y = before(cells_low[z]["low_y"][f], cell["low_y"][f])
            along_z = faces[up][f] - faces[z][f]
            kept = state[f][z] - 4.0 * cell["diffuse"][f]
            new[f][z] = kept - (cell["along_x"][f] + (high_y - low_y) + along_z)
        mom_x, mom_y = (state[1][z], state[2][z])
        new[1][z] = new[1][z] + (TIME_STEP * 2.0 * ROTATION) * mom_y
        new[2][z] = new[2][z] - (TIME_STEP * (2.0 - SHEAR_RATE) * ROTATION) * mom_x
        new[4][z] = new[4][z] + (2.0 * SHEAR_RATE * ROTATION) * cell["shear"]
        low_pair = before(cells_low[z]["low_pair"], cell["low_pair"])
        high_pair = after(cell["high_pair"], cells_high[z]["high_pair"])
        edge_z = cell["pair"] + low_pair
        new[5][z] = state[5][z] + ((edge_y[up] - edge_y[z]) - (high_pair - low_pair))
        new[6][z] = state[6][z] + ((radial_next(edge_z) - edge_z) - (edge_x[up] - edge_x[z]))
        new[7][z] = state[7][z] + (along_y - shared["along_x"])
    return new


def step_kernel(
    cells, peers, rows,
    shear_ref, weight_ref, joined_ref, up_hbm, down_hbm,
    out_ref, state_ref, mid_ref, up_ref, down_ref, up_sem, down_sem,
):
    up_copy = pltpu.make_async_copy(up_hbm, up_ref, up_sem)
    down_copy = pltpu.make_async_copy(down_hbm, down_ref, down_sem)
    up_copy.start()
    down_copy.start()
    own = plan(shear_ref[0], cells, peers)[0]
    lane = lane_index()
    row = row_index()
    single = tiles_for(cells)
    window = single + 1
    pairs = FIELDS // 2

    for f in range(FIELDS):
        for t, tile in enumerate(cut_window(joined_ref, f, own, window)):
            for z in range(PLANES):
                state_ref[t, f, z] = turn_rows(tile, -z * rows)
    up_copy.wait()
    down_copy.wait()
    for f in range(FIELDS):
        pair, second = divmod(f, 2)
        for t in range(window):
            if t < single:
                up = up_ref[pair * single + t]
                down = down_ref[pair * single + t]
            else:
                back = (LANES - pair * TAIL) % LANES
                up = turn_lanes(up_ref[pairs * single], back)
                down = turn_lanes(down_ref[pairs * single + 1], back)
            for z in range(PLANES):
                up_at = z * rows + (0 if second else SENT)
                down_at = z * rows + (SENT if second else 0)
                value = state_ref[t, f, z]
                value = jnp.where(row < rows, value, turn_rows(down, rows - down_at))
                value = jnp.where(row < rows + SENT, value, turn_rows(up, rows + SENT - up_at))
                state_ref[t, f, z] = value
    last = rows + SENT - 1

    def faces_beyond(t, face_x):
        if t < single:
            beyond = [turn_rows(down_ref[pairs * single], last - t * PLANES - z) for z in range(PLANES)]
        else:
            tile = turn_lanes(down_ref[pairs * single + 1], LANES - pairs * TAIL)
            beyond = [turn_rows(tile, last - (z * rows + SENT)) for z in range(PLANES)]
        return [jnp.where(row == last, b, radial_next(face)) for b, face in zip(beyond, face_x)]

    def terms(ref, t, count, beyond):
        state = [[ref[t, f, z] for z in range(PLANES)] for f in range(FIELDS)]
        if beyond:
            next_face_x = faces_beyond(t, state[FACE_X])
        else:
            next_face_x = [radial_next(face) for face in state[FACE_X]]
        next_face_y = []
        for z in range(PLANES):
            here = turn_lanes(state[6][z], LANES - 1)
            if t + 1 < count:
                there = turn_lanes(ref[t + 1, 6, z], LANES - 1)
                here = jnp.where(lane < LANES - 1, here, there)
            next_face_y.append(here)
        return state, cell_terms(state, next_face_x, next_face_y)

    low = here = terms(state_ref, 0, window, True)
    for t in range(window):
        high = terms(state_ref, t + 1, window, True) if t + 1 < window else here
        new = tile_step(here[0], low[1], here[1], high[1])
        for f in range(FIELDS):
            for z in range(PLANES):
                if t < single or f == 6:
                    mid_ref[t, f, z] = new[f][z]
        low, here = here, high

    weight = weight_ref[...]
    keep = 1.0 - weight
    low = here = terms(mid_ref, 0, window, False)
    low_done = None
    low_moved = None

    def emit(t, moved):
        for f in range(FIELDS):
            out_ref[f, t] = moved[f]

    for t in range(single):
        high = terms(mid_ref, t + 1, window, False) if t + 1 < single else here
        new = tile_step(here[0], low[1], here[1], high[1])
        done = []
        moved = []
        for f in range(FIELDS):
            mixed = []
            turned = []
            for z in range(PLANES):
                value = 0.5 * (state_ref[t, f, z] + new[f][z])
                below = turn_lanes(value, 1)
                turned.append(below)
                if t:
                    below = jnp.where(lane > 0, below, low_done[f][z])
                mixed.append(keep * value + weight * below)
            done.append(turned)
            both = jnp.where(row < rows, mixed[0], turn_rows(mixed[1], rows))
            moved.append(turn_lanes(both, LANES - BELOW))
        if t:
            emit(
                t - 1,
                [jnp.where(lane < LANES - BELOW, a, b) for a, b in zip(low_moved, moved)],
            )
        low_done, low_moved = done, moved
        low, here = here, high
    emit(single - 1, low_moved)


def row_sources(shift, own, cells, peers, target):
    shift = shift - (cells - BELOW - own)
    shift = jnp.where(shift < 0, shift + cells * peers, shift)
    hops, rest = hops_of(shift, cells, peers)
    upper = (target + peers - hops) & (peers - 1)
    lower = (target + peers - 1 - hops) & (peers - 1)
    return upper, lower, rest


def pick_kernel(target, pick_ref, *refs):
    in_refs, out_ref = (refs[:-1], refs[-1])
    count = out_ref.shape[1]
    block = pick_ref[target, 0]
    amount = pick_ref[target, 1]
    lane = lane_index()
    fine = amount & (LANES - 1)
    source = (lane - fine) & (LANES - 1)
    chosen = [block == i for i in range(len(in_refs))]
    for f in range(FIELDS):
        tiles = [in_refs[0][f, t] for t in range(count)]
        for mask, ref in zip(chosen[1:], in_refs[1:]):
            tiles = [jnp.where(mask, ref[f, t], tiles[t]) for t in range(count)]
        step = 1
        while step < count:
            moves = (amount & (step * LANES)) != 0
            tiles = [jnp.where(moves, tiles[(t - step) % count], tiles[t]) for t in range(count)]
            step *= 2
        tiles = [
            jnp.take_along_axis(tile, source, axis=1, mode="promise_in_bounds") for tile in tiles
        ]
        for t in range(count):
            out_ref[f, t] = jnp.where(lane < fine, tiles[t - 1], tiles[t])


def merge_kernel(cells, rows, border_ref, mine_ref, other_ref, out_hbm, out_ref, out_sem):
    count = mine_ref.shape[1]
    border = border_ref[0]
    held = border_ref[1] == 1
    masks = [(lane_index() + t * LANES >= border) == held for t in range(count)]
    for f in range(FIELDS):
        tiles = [jnp.where(masks[t], mine_ref[f, t], other_ref[f, t]) for t in range(count)]
        value = jnp.concatenate(tiles, axis=1)[:, :cells]
        for z in range(PLANES):
            out_ref[f, z] = value[z * rows : (z + 1) * rows]
        pltpu.make_async_copy(out_ref.at[f], out_hbm.at[f], out_sem.at[f]).start()
    for f in range(FIELDS):
        pltpu.make_async_copy(out_ref.at[f], out_hbm.at[f], out_sem.at[f]).wait()


def solution(mesh):
    places, peers = (mesh.shape["gx"], mesh.shape["gy"])
    smem = pl.BlockSpec(memory_space=pltpu.SMEM)
    vmem = pl.BlockSpec(memory_space=pltpu.VMEM)
    hbm = pl.BlockSpec(memory_space=pltpu.HBM)
    params = pltpu.CompilerParams(vmem_limit_bytes=8 * 2**20)
    axes = ("gx", "gy")

    def array(*shape):
        return jax.ShapeDtypeStruct(shape + (SUBLANES, LANES), jnp.float32)

    def scratch(*shape):
        return pltpu.VMEM(shape + (SUBLANES, LANES), jnp.float32)

    def device(x, y):
        return x % places * peers + y % peers

    devices = [(x, y) for x in range(places) for y in range(peers)]

    def ghosts(up_hop, down_hop, up, down):
        rise = [(device(x, y), device(x + 1, y + up_hop * (x == places - 1))) for x, y in devices]
        fall = [(device(x, y), device(x - 1, y - down_hop * (x == 0))) for x, y in devices]
        up = lax.ppermute(up, axes, rise)
        return up, lax.ppermute(down, axes, fall)

    def shards(state, shear_offset, remap_shift, frac_index):
        rows, cells = state.shape[2:]
        single = tiles_for(cells)
        double = tiles_for(2 * cells)
        window = tiles_for(BELOW + cells + ABOVE)
        below = lax.ppermute(state, "gy", [(i, (i + 1) % peers) for i in range(peers)])
        numbers = lambda *shape: jax.ShapeDtypeStruct(shape + (SUBLANES, LANES), jnp.int32)
        upper, weight, pick, border = pl.pallas_call(
            lambda *refs: lay_kernel(cells, peers, *refs),
            out_shape=[array(FIELDS, single), array(), numbers(2, 2), numbers(2)],
            in_specs=[smem] * 3 + [vmem],
            out_specs=[vmem] * 4,
            compiler_params=params,
            name="lay",
        )(shear_offset, remap_shift, frac_index, state)
        edge = FIELDS // 2 * single + 2
        joined, up, down = pl.pallas_call(
            lambda *refs: pair_kernel(cells, peers, rows, *refs),
            out_shape=[array(FIELDS, double), array(edge), array(edge)],
            in_specs=[smem, vmem, vmem],
            out_specs=[vmem] * 3,
            compiler_params=params,
            name="pair",
        )(shear_offset, upper, below)
        _, _, _, up_hop, down_hop = plan(shear_offset[0], cells, peers)
        branches = [
            lambda u, d, i=i: ghosts(i // 2 + i % 2, i // 2, u, d) for i in range(2 * peers)
        ]
        which = (down_hop + up_hop) & (2 * peers - 1)
        up, down = lax.switch(which, branches, up, down)
        block = pl.pallas_call(
            lambda *refs: step_kernel(cells, peers, rows, *refs),
            out_shape=array(FIELDS, single),
            in_specs=[smem] + [vmem] * 2 + [hbm] * 2,
            out_specs=vmem,
            scratch_shapes=[scratch(window, FIELDS, PLANES)] * 2
            + [scratch(edge), scratch(edge)]
            + [pltpu.SemaphoreType.DMA] * 2,
            compiler_params=params,
            name="step",
        )(shear_offset, weight, joined, up, down)

        def exchange(value, bits):
            return lax.ppermute(value, "gy", [(i, i ^ bits) for i in range(peers)])

        blocks = [block] + [exchange(block, bits) for bits in range(2, peers, 2)]

        def picked(target, name):
            return pl.pallas_call(
                lambda *refs: pick_kernel(target, *refs),
                out_shape=array(FIELDS, single),
                in_specs=[vmem] * (1 + peers // 2),
                out_specs=vmem,
                compiler_params=params,
                name=name,
            )(pick, *blocks)

        other = exchange(picked(0, "gather"), 1)
        mine = picked(1, "keep")
        return pl.pallas_call(
            lambda *refs: merge_kernel(cells, rows, *refs),
            out_shape=jax.ShapeDtypeStruct(state.shape, jnp.float32),
            in_specs=[vmem] * 3,
            out_specs=hbm,
            scratch_shapes=[
                pltpu.VMEM(state.shape, jnp.float32),
                pltpu.SemaphoreType.DMA((FIELDS,)),
            ],
            compiler_params=params,
            name="merge",
        )(border, mine, other)

    placed = (P(None, None, "gx", "gy"), P(), P("gx"), P("gx"))
    return jax.shard_map(
        shards, mesh=mesh, in_specs=placed, out_specs=P(None, None, "gx", "gy"), check_vma=False
    )
```

```python
import jax
import jax.numpy as jnp
from jax import lax
from jax.experimental import pallas as pl
from jax.experimental.pallas import tpu as pltpu
from jax.sharding import PartitionSpec as P

FRAC = 16

ADIABATIC = 5.0 / 3.0
ROTATION = 1.0
SHEAR_RATE = 1.5
MAX_SPEED = 5.0
TIME_STEP = 0.05

LANES = 128
LANE_BITS = 7
SUBLANES = 8
FIELDS = 8
PLANES = 2
FACE_X = 5
BELOW = 3
ABOVE = 3
TAIL = 4
SENT = 2
HALF_STEP = 0.5 * TIME_STEP
DIFFUSE = 0.5 * MAX_SPEED * TIME_STEP
EDGE = 0.25 * TIME_STEP


def lane_index():
    return lax.broadcasted_iota(jnp.int32, (SUBLANES, LANES), 1)


def row_index():
    return lax.broadcasted_iota(jnp.int32, (SUBLANES, LANES), 0)


def turn_lanes(value, amount):
    return pltpu.roll(value, amount, 1)


def turn_rows(value, amount):
    amount %= SUBLANES
    return pltpu.roll(value, amount, 0) if amount else value


def radial_next(value):
    return turn_rows(value, -1)


def radial_prev(value):
    return turn_rows(value, 1)


def tiles_for(columns):
    return -(-columns // LANES)


def hops_of(columns, cells, peers):
    hops = sum(jnp.where(columns >= k * cells, 1, 0) for k in range(1, peers))
    return hops, columns - hops * cells


def plan(shear, cells, peers):
    hops, rest = hops_of(shear, cells, peers)
    middle = cells // 2
    near = (rest >= middle - 5) & (rest <= middle + 5)
    own = jnp.where(near, middle - 12, middle)
    up_hop = jnp.where(rest > own, 1, 0)
    down_hop = jnp.where(rest + own >= cells, 1, 0)
    up = own - rest + up_hop * cells
    down = own + rest - down_hop * cells
    return own, up, down, hops + up_hop, hops + down_hop


def block_tiles(ref, f, cells):
    value = jnp.concatenate([ref[f, z] for z in range(PLANES)], axis=0)
    tiles = []
    for i in range(0, cells, LANES):
        tile = value[:, i : min(i + LANES, cells)]
        spare = LANES - tile.shape[1]
        if spare:
            tile = jnp.concatenate([tile, jnp.zeros((SUBLANES, spare), tile.dtype)], axis=1)
        tiles.append(tile)
    return tiles


def lay_kernel(
    cells, peers, shear_ref, shift_ref, frac_ref, state_ref,
    out_ref, weight_ref, pick_ref, border_ref,
):
    rows = state_ref.shape[2]
    part = lax.axis_index("gy")
    own = plan(shear_ref[0], cells, peers)[0]
    row = row_index()
    spare = tiles_for(cells) * LANES - cells
    blank = jnp.zeros((SUBLANES, LANES), jnp.int32)
    weight = jnp.zeros((SUBLANES, LANES), jnp.float32)
    picks = [[blank, blank], [blank, blank]]
    border = held = blank
    for x in range(rows):
        level = (frac_ref[x].astype(jnp.float32) + 0.5) / FRAC
        weight = jnp.where(row == x, level, weight)
        here = row % rows == x
        for i, target in enumerate((part ^ 1, part)):
            upper, lower, rest = row_sources(shift_ref[x], own, cells, peers, target)
            first = ((upper ^ part) & 1) == 0
            block = (jnp.where(first, upper, lower) ^ part) >> 1
            block = jnp.where((part & 1) == 1, partner_order(block, peers // 2), block)
            amount = jnp.where(first, rest, rest + spare)
            picks[i] = [jnp.where(here, a, b) for a, b in zip((block, amount), picks[i])]
            if target is part:
                border = jnp.where(here, rest, border)
                held = jnp.where(here, jnp.where(first, 1, 0), held)
    weight_ref[...] = weight
    for i in range(2):
        for k in range(2):
            pick_ref[i, k] = picks[i][k]
    border_ref[0] = border
    border_ref[1] = held
    for f in range(FIELDS):
        for t, tile in enumerate(block_tiles(state_ref, f, cells)):
            out_ref[f, t] = turn_lanes(tile, cells % LANES)


def pair_kernel(cells, peers, rows, shear_ref, upper_ref, below_ref, joined_ref, up_ref, down_ref):
    place = lax.axis_index("gx")
    places = lax.axis_size("gx")
    own, up, down, _, _ = plan(shear_ref[0], cells, peers)
    up = jnp.where(place == places - 1, up, own)
    down = jnp.where(place == 0, down, own)
    lane = lane_index()
    row = row_index()
    single = tiles_for(cells)
    gap = cells % LANES
    window = single + 1
    for f in range(FIELDS):
        lower = block_tiles(below_ref, f, cells)
        upper = [upper_ref[f, t] for t in range(single)]
        for i in range(single - 1):
            joined_ref[f, i] = lower[i]
        joined_ref[f, single - 1] = jnp.where(lane < gap, lower[-1], upper[0])
        for k in range(single):
            following = upper[min(k + 1, single - 1)]
            joined_ref[f, single + k] = jnp.where(lane < gap, upper[k], following)

    late = row % rows >= SENT
    pairs = FIELDS // 2
    up_tail = down_tail = jnp.zeros((SUBLANES, LANES), jnp.float32)

    def tail(tile, index, so_far):
        return jnp.where(lane // TAIL == index, turn_lanes(tile, index * TAIL), so_far)

    for pair in range(pairs):
        ups = [cut_window(joined_ref, 2 * pair + i, up, window) for i in range(2)]
        downs = [cut_window(joined_ref, 2 * pair + i, down, window) for i in range(2)]
        ups = [jnp.where(late, a, turn_rows(b, -SENT)) for a, b in zip(*ups)]
        downs = [jnp.where(late, turn_rows(b, SENT), a) for a, b in zip(*downs)]
        for t in range(single):
            up_ref[pair * single + t] = ups[t]
            down_ref[pair * single + t] = downs[t]
        up_tail = tail(ups[single], pair, up_tail)
        down_tail = tail(downs[single], pair, down_tail)
    faces = jnp.zeros((SUBLANES, LANES), jnp.float32)
    tiles = cut_window(joined_ref, FACE_X, down, window)
    for t in range(single):
        for z in range(PLANES):
            at = t * PLANES + z
            faces = jnp.where(row == at, turn_rows(tiles[t], at - (z * rows + SENT)), faces)
    down_ref[pairs * single] = faces
    up_ref[pairs * single] = up_tail
    down_ref[pairs * single + 1] = tail(tiles[single], pairs, down_tail)


def cut_window(joined_ref, f, start, count):
    whole = start >> LANE_BITS
    part = start & (LANES - 1)
    last = joined_ref.shape[1] - 1
    tiles = [joined_ref[f, jnp.minimum(whole + t, last)] for t in range(count + 1)]
    turned = [turn_lanes(tile, (LANES - part) & (LANES - 1)) for tile in tiles]
    here = lane_index() < LANES - part
    return [jnp.where(here, turned[t], turned[t + 1]) for t in range(count)]


def cell_terms(state, next_face_x, next_face_y):
    planes = range(PLANES)
    face_z = state[7]
    out = []
    for z in planes:
        density, mom_x, mom_y, mom_z, energy, face_x, face_y = (state[f][z] for f in range(7))
        cen_x = 0.5 * (face_x + next_face_x[z])
        cen_y = 0.5 * (face_y + next_face_y[z])
        cen_z = 0.5 * (face_z[z] + face_z[(z + 1) % PLANES])
        inverse = 1.0 / density
        vel_x, vel_y, vel_z = (mom_x * inverse, mom_y * inverse, mom_z * inverse)
        magnetic = 0.5 * (cen_x * cen_x + cen_y * cen_y + cen_z * cen_z)
        kinetic = 0.5 * (mom_x * vel_x + mom_y * vel_y + mom_z * vel_z)
        pressure = (ADIABATIC - 1.0) * (energy - kinetic - magnetic) + magnetic
        vel_dot = vel_x * cen_x + vel_y * cen_y + vel_z * cen_z
        scaled_p = HALF_STEP * pressure
        total = energy + pressure
        sv_x, sv_y, sv_z = (HALF_STEP * vel_x, HALF_STEP * vel_y, HALF_STEP * vel_z)
        sb_x, sb_y, sb_z = (HALF_STEP * cen_x, HALF_STEP * cen_y, HALF_STEP * cen_z)
        xx = mom_x * sv_x - cen_x * sb_x + scaled_p
        yy = mom_y * sv_y - cen_y * sb_y + scaled_p
        zz = mom_z * sv_z - cen_z * sb_z + scaled_p
        xy = mom_x * sv_y - cen_x * sb_y
        xz = mom_x * sv_z - cen_x * sb_z
        yz = mom_y * sv_z - cen_y * sb_z
        diffuse = [DIFFUSE * state[f][z] for f in range(5)]
        flux_x = [HALF_STEP * mom_x, xx, xy, xz, total * sv_x - sb_x * vel_dot]
        flux_y = [HALF_STEP * mom_y, xy, yy, yz, total * sv_y - sb_y * vel_dot]
        flux_z = [HALF_STEP * mom_z, xz, yz, zz, total * sv_z - sb_z * vel_dot]
        e_z = EDGE * (vel_y * cen_x - vel_x * cen_y)
        pair = e_z + radial_prev(e_z)
        out.append(
            dict(
                diffuse=diffuse,
                along_x=[
                    radial_next(f - d) - radial_prev(f + d) for f, d in zip(flux_x, diffuse)
                ],
                low_y=[turn_lanes(f + d, 1) for f, d in zip(flux_y, diffuse)],
                high_y=[turn_lanes(f - d, LANES - 1) for f, d in zip(flux_y, diffuse)],
                flux_z=flux_z,
                shear=xy,
                e_x=EDGE * (vel_z * cen_y - vel_y * cen_z),
                e_y=EDGE * (vel_x * cen_z - vel_z * cen_x),
                pair=pair,
                low_pair=turn_lanes(pair, 1),
                high_pair=turn_lanes(pair, LANES - 1),
            )
        )
    e_x, e_y = (
        [sum((cell[name] for cell in out[1:]), out[0][name]) for name in ("e_x", "e_y")]
    )
    shared = dict(
        e_x=e_x,
        low_e_x=turn_lanes(e_x, 1),
        high_e_x=turn_lanes(e_x, LANES - 1),
        edge_y=[e_y + radial_prev(e_y)] * PLANES,
        along_x=radial_next(e_y) - radial_prev(e_y),
    )
    return out, shared


def tile_step(state, low, here, high):
    lane = lane_index()
    cells_low, shared_low = low
    cells, shared = here
    cells_high, shared_high = high

    def before(turned_low, turned):
        return jnp.where(lane > 0, turned, turned_low)

    def after(turned, turned_high):
        return jnp.where(lane < LANES - 1, turned, turned_high)

    new = [[None] * PLANES for f in range(FIELDS)]
    faces = [[], []]
    for f in range(5):
        both = cells[0]["flux_z"][f] + cells[1]["flux_z"][f]
        jump = cells[1]["diffuse"][f] - cells[0]["diffuse"][f]
        faces[0].append(both + jump)
        faces[1].append(both - jump)
    low_e_x = before(shared_low["low_e_x"], shared["low_e_x"])
    along_y = after(shared["high_e_x"], shared_high["high_e_x"]) - low_e_x
    edge_x = [shared["e_x"] + low_e_x] * PLANES
    edge_y = shared["edge_y"]
    for z in range(PLANES):
        cell = cells[z]
        up = (z + 1) % PLANES
        for f in range(5):
            high_y = after(cell["high_y"][f], cells_high[z]["high_y"][f])
            low_y = before(cells_low[z]["low_y"][f], cell["low_y"][f])
            along_z = faces[up][f] - faces[z][f]
            kept = (1.0 - 4.0 * DIFFUSE) * state[f][z]
            new[f][z] = kept - (cell["along_x"][f] + (high_y - low_y) + along_z)
        mom_x, mom_y = (state[1][z], state[2][z])
        new[1][z] = new[1][z] + (TIME_STEP * 2.0 * ROTATION) * mom_y
        new[2][z] = new[2][z] - (TIME_STEP * (2.0 - SHEAR_RATE) * ROTATION) * mom_x
        new[4][z] = new[4][z] + (2.0 * SHEAR_RATE * ROTATION) * cell["shear"]
        low_pair = before(cells_low[z]["low_pair"], cell["low_pair"])
        high_pair = after(cell["high_pair"], cells_high[z]["high_pair"])
        edge_z = cell["pair"] + low_pair
        new[5][z] = state[5][z] + ((edge_y[up] - edge_y[z]) - (high_pair - low_pair))
        new[6][z] = state[6][z] + ((radial_next(edge_z) - edge_z) - (edge_x[up] - edge_x[z]))
        new[7][z] = state[7][z] + (along_y - shared["along_x"])
    return new


def step_kernel(
    cells, peers, rows,
    shear_ref, weight_ref, joined_ref, up_hbm, down_hbm,
    out_ref, state_ref, mid_ref, up_ref, down_ref, up_sem, down_sem,
):
    up_copy = pltpu.make_async_copy(up_hbm, up_ref, up_sem)
    down_copy = pltpu.make_async_copy(down_hbm, down_ref, down_sem)
    up_copy.start()
    down_copy.start()
    own = plan(shear_ref[0], cells, peers)[0]
    lane = lane_index()
    row = row_index()
    single = tiles_for(cells)
    window = single + 1
    pairs = FIELDS // 2

    for f in range(FIELDS):
        for t, tile in enumerate(cut_window(joined_ref, f, own, window)):
            for z in range(PLANES):
                state_ref[t, f, z] = turn_rows(tile, -z * rows)
    up_copy.wait()
    down_copy.wait()
    for f in range(FIELDS):
        pair, second = divmod(f, 2)
        for t in range(window):
            if t < single:
                up = up_ref[pair * single + t]
                down = down_ref[pair * single + t]
            else:
                back = (LANES - pair * TAIL) % LANES
                up = turn_lanes(up_ref[pairs * single], back)
                down = turn_lanes(down_ref[pairs * single + 1], back)
            for z in range(PLANES):
                up_at = z * rows + (0 if second else SENT)
                down_at = z * rows + (SENT if second else 0)
                value = state_ref[t, f, z]
                value = jnp.where(row < rows, value, turn_rows(down, rows - down_at))
                value = jnp.where(row < rows + SENT, value, turn_rows(up, rows + SENT - up_at))
                state_ref[t, f, z] = value
    last = rows + SENT - 1

    def faces_beyond(t, face_x):
        if t < single:
            beyond = [turn_rows(down_ref[pairs * single], last - t * PLANES - z) for z in range(PLANES)]
        else:
            tile = turn_lanes(down_ref[pairs * single + 1], LANES - pairs * TAIL)
            beyond = [turn_rows(tile, last - (z * rows + SENT)) for z in range(PLANES)]
        return [jnp.where(row == last, b, radial_next(face)) for b, face in zip(beyond, face_x)]

    def terms(ref, t, count, beyond):
        state = [[ref[t, f, z] for z in range(PLANES)] for f in range(FIELDS)]
        if beyond:
            next_face_x = faces_beyond(t, state[FACE_X])
        else:
            next_face_x = [radial_next(face) for face in state[FACE_X]]
        next_face_y = []
        for z in range(PLANES):
            here = turn_lanes(state[6][z], LANES - 1)
            if t + 1 < count:
                there = turn_lanes(ref[t + 1, 6, z], LANES - 1)
                here = jnp.where(lane < LANES - 1, here, there)
            next_face_y.append(here)
        return state, cell_terms(state, next_face_x, next_face_y)

    low = here = terms(state_ref, 0, window, True)
    for t in range(window):
        high = terms(state_ref, t + 1, window, True) if t + 1 < window else here
        new = tile_step(here[0], low[1], here[1], high[1])
        for f in range(FIELDS):
            for z in range(PLANES):
                if t < single or f == 6:
                    mid_ref[t, f, z] = new[f][z]
        low, here = here, high

    weight = weight_ref[...]
    keep = 1.0 - weight
    low = here = terms(mid_ref, 0, window, False)
    low_done = None
    low_moved = None

    def emit(t, moved):
        for f in range(FIELDS):
            out_ref[f, t] = moved[f]

    for t in range(single):
        high = terms(mid_ref, t + 1, window, False) if t + 1 < single else here
        new = tile_step(here[0], low[1], here[1], high[1])
        done = []
        moved = []
        for f in range(FIELDS):
            mixed = []
            turned = []
            for z in range(PLANES):
                value = 0.5 * (state_ref[t, f, z] + new[f][z])
                below = turn_lanes(value, 1)
                turned.append(below)
                if t:
                    below = jnp.where(lane > 0, below, low_done[f][z])
                mixed.append(keep * value + weight * below)
            done.append(turned)
            both = jnp.where(row < rows, mixed[0], turn_rows(mixed[1], rows))
            moved.append(turn_lanes(both, LANES - BELOW))
        if t:
            emit(
                t - 1,
                [jnp.where(lane < LANES - BELOW, a, b) for a, b in zip(low_moved, moved)],
            )
        low_done, low_moved = done, moved
        low, here = here, high
    emit(single - 1, low_moved)


def partner_order(offset, chips):
    bits = chips.bit_length() - 1
    return sum(((offset >> b) & 1) << (bits - 1 - b) for b in range(bits))


def row_sources(shift, own, cells, peers, target):
    shift = shift - (cells - BELOW - own)
    shift = jnp.where(shift < 0, shift + cells * peers, shift)
    hops, rest = hops_of(shift, cells, peers)
    upper = (target + peers - hops) & (peers - 1)
    lower = (target + peers - 1 - hops) & (peers - 1)
    return upper, lower, rest


def pick_kernel(target, pick_ref, *refs):
    in_refs, out_ref = (refs[:-1], refs[-1])
    count = out_ref.shape[1]
    block = pick_ref[target, 0]
    amount = pick_ref[target, 1]
    lane = lane_index()
    fine = amount & (LANES - 1)
    source = (lane - fine) & (LANES - 1)
    chosen = [block == i for i in range(len(in_refs))]
    for f in range(FIELDS):
        tiles = [in_refs[0][f, t] for t in range(count)]
        for mask, ref in zip(chosen[1:], in_refs[1:]):
            tiles = [jnp.where(mask, ref[f, t], tiles[t]) for t in range(count)]
        step = 1
        while step < count:
            moves = (amount & (step * LANES)) != 0
            tiles = [jnp.where(moves, tiles[(t - step) % count], tiles[t]) for t in range(count)]
            step *= 2
        tiles = [
            jnp.take_along_axis(tile, source, axis=1, mode="promise_in_bounds") for tile in tiles
        ]
        for t in range(count):
            out_ref[f, t] = jnp.where(lane < fine, tiles[t - 1], tiles[t])


def merge_kernel(cells, rows, border_ref, mine_ref, other_ref, out_hbm, out_ref, out_sem):
    count = mine_ref.shape[1]
    border = border_ref[0]
    held = border_ref[1] == 1
    masks = [(lane_index() + t * LANES >= border) == held for t in range(count)]
    for f in range(FIELDS):
        tiles = [jnp.where(masks[t], mine_ref[f, t], other_ref[f, t]) for t in range(count)]
        value = jnp.concatenate(tiles, axis=1)[:, :cells]
        for z in range(PLANES):
            out_ref[f, z] = value[z * rows : (z + 1) * rows]
        pltpu.make_async_copy(out_ref.at[f], out_hbm.at[f], out_sem.at[f]).start()
    for f in range(FIELDS):
        pltpu.make_async_copy(out_ref.at[f], out_hbm.at[f], out_sem.at[f]).wait()


def solution(mesh):
    places, peers = (mesh.shape["gx"], mesh.shape["gy"])
    smem = pl.BlockSpec(memory_space=pltpu.SMEM)
    vmem = pl.BlockSpec(memory_space=pltpu.VMEM)
    hbm = pl.BlockSpec(memory_space=pltpu.HBM)
    params = pltpu.CompilerParams(vmem_limit_bytes=8 * 2**20)
    axes = ("gx", "gy")

    def array(*shape):
        return jax.ShapeDtypeStruct(shape + (SUBLANES, LANES), jnp.float32)

    def scratch(*shape):
        return pltpu.VMEM(shape + (SUBLANES, LANES), jnp.float32)

    def device(x, y):
        return x % places * peers + y % peers

    devices = [(x, y) for x in range(places) for y in range(peers)]

    def ghosts(up_hop, down_hop, up, down):
        rise = [(device(x, y), device(x + 1, y + up_hop * (x == places - 1))) for x, y in devices]
        fall = [(device(x, y), device(x - 1, y - down_hop * (x == 0))) for x, y in devices]
        up = lax.ppermute(up, axes, rise)
        return up, lax.ppermute(down, axes, fall)

    def shards(state, shear_offset, remap_shift, frac_index):
        rows, cells = state.shape[2:]
        single = tiles_for(cells)
        double = tiles_for(2 * cells)
        window = tiles_for(BELOW + cells + ABOVE)
        below = lax.ppermute(state, "gy", [(i, (i + 1) % peers) for i in range(peers)])
        numbers = lambda *shape: jax.ShapeDtypeStruct(shape + (SUBLANES, LANES), jnp.int32)
        upper, weight, pick, border = pl.pallas_call(
            lambda *refs: lay_kernel(cells, peers, *refs),
            out_shape=[array(FIELDS, single), array(), numbers(2, 2), numbers(2)],
            in_specs=[smem] * 3 + [vmem],
            out_specs=[vmem] * 4,
            compiler_params=params,
            name="lay",
        )(shear_offset, remap_shift, frac_index, state)
        edge = FIELDS // 2 * single + 2
        joined, up, down = pl.pallas_call(
            lambda *refs: pair_kernel(cells, peers, rows, *refs),
            out_shape=[array(FIELDS, double), array(edge), array(edge)],
            in_specs=[smem, vmem, vmem],
            out_specs=[vmem] * 3,
            compiler_params=params,
            name="pair",
        )(shear_offset, upper, below)
        _, _, _, up_hop, down_hop = plan(shear_offset[0], cells, peers)
        branches = [
            lambda u, d, i=i: ghosts(i // 2 + i % 2, i // 2, u, d) for i in range(2 * peers)
        ]
        which = (down_hop + up_hop) & (2 * peers - 1)
        up, down = lax.switch(which, branches, up, down)
        block = pl.pallas_call(
            lambda *refs: step_kernel(cells, peers, rows, *refs),
            out_shape=array(FIELDS, single),
            in_specs=[smem] + [vmem] * 2 + [hbm] * 2,
            out_specs=vmem,
            scratch_shapes=[scratch(window, FIELDS, PLANES)] * 2
            + [scratch(edge), scratch(edge)]
            + [pltpu.SemaphoreType.DMA] * 2,
            compiler_params=params,
            name="step",
        )(shear_offset, weight, joined, up, down)

        def exchange(value, bits):
            return lax.ppermute(value, "gy", [(i, i ^ bits) for i in range(peers)])

        def across(offset):
            offsets = (offset, partner_order(offset, peers // 2))
            return lax.ppermute(block, "gy", [(i, i ^ (2 * offsets[i % 2])) for i in range(peers)])

        far = [across(offset) for offset in range(peers // 2 - 1, 0, -1)]

        def picked(target, name):
            return pl.pallas_call(
                lambda pick_ref, *refs: pick_kernel(target, pick_ref, *refs[-2::-1], refs[-1]),
                out_shape=array(FIELDS, single),
                in_specs=[vmem] * (1 + peers // 2),
                out_specs=vmem,
                compiler_params=params,
                name=name,
            )(pick, *far, block)

        other = exchange(picked(0, "gather"), 1)
        mine = picked(1, "keep")
        return pl.pallas_call(
            lambda *refs: merge_kernel(cells, rows, *refs),
            out_shape=jax.ShapeDtypeStruct(state.shape, jnp.float32),
            in_specs=[vmem] * 3,
            out_specs=hbm,
            scratch_shapes=[
                pltpu.VMEM(state.shape, jnp.float32),
                pltpu.SemaphoreType.DMA((FIELDS,)),
            ],
            compiler_params=params,
            name="merge",
        )(border, mine, other)

    placed = (P(None, None, "gx", "gy"), P(), P("gx"), P("gx"))
    return jax.shard_map(
        shards, mesh=mesh, in_specs=placed, out_specs=P(None, None, "gx", "gy"), check_vma=False
    )
```

```python
import jax
import jax.numpy as jnp
from jax import lax
from jax.experimental import pallas as pl
from jax.experimental.pallas import tpu as pltpu
from jax.sharding import PartitionSpec as P

FRAC = 16

ADIABATIC = 5.0 / 3.0
ROTATION = 1.0
SHEAR_RATE = 1.5
MAX_SPEED = 5.0
TIME_STEP = 0.05

LANES = 128
LANE_BITS = 7
SUBLANES = 8
FIELDS = 8
PLANES = 2
FACE_X = 5
BELOW = 3
ABOVE = 3
TAIL = 4
SENT = 2
HALF_STEP = 0.5 * TIME_STEP
DIFFUSE = 0.5 * MAX_SPEED * TIME_STEP
EDGE = 0.25 * TIME_STEP


def lane_index():
    return lax.broadcasted_iota(jnp.int32, (SUBLANES, LANES), 1)


def row_index():
    return lax.broadcasted_iota(jnp.int32, (SUBLANES, LANES), 0)


def turn_lanes(value, amount):
    return pltpu.roll(value, amount, 1)


def turn_rows(value, amount):
    amount %= SUBLANES
    return pltpu.roll(value, amount, 0) if amount else value


def radial_next(value):
    return turn_rows(value, -1)


def radial_prev(value):
    return turn_rows(value, 1)


def tiles_for(columns):
    return -(-columns // LANES)


def hops_of(columns, cells, peers):
    hops = sum(jnp.where(columns >= k * cells, 1, 0) for k in range(1, peers))
    return hops, columns - hops * cells


def plan(shear, cells, peers):
    hops, rest = hops_of(shear, cells, peers)
    middle = cells // 2
    near = (rest >= middle - 5) & (rest <= middle + 5)
    own = jnp.where(near, middle - 12, middle)
    up_hop = jnp.where(rest > own, 1, 0)
    down_hop = jnp.where(rest + own >= cells, 1, 0)
    up = own - rest + up_hop * cells
    down = own + rest - down_hop * cells
    return own, up, down, hops + up_hop, hops + down_hop


def block_tiles(ref, f, cells):
    value = jnp.concatenate([ref[f, z] for z in range(PLANES)], axis=0)
    tiles = []
    for i in range(0, cells, LANES):
        tile = value[:, i : min(i + LANES, cells)]
        spare = LANES - tile.shape[1]
        if spare:
            tile = jnp.concatenate([tile, jnp.zeros((SUBLANES, spare), tile.dtype)], axis=1)
        tiles.append(tile)
    return tiles


def lay_kernel(
    cells, peers, shear_ref, shift_ref, frac_ref, state_ref,
    out_ref, weight_ref, pick_ref, border_ref,
):
    rows = state_ref.shape[2]
    part = lax.axis_index("gy")
    own = plan(shear_ref[0], cells, peers)[0]
    row = row_index()
    spare = tiles_for(cells) * LANES - cells
    blank = jnp.zeros((SUBLANES, LANES), jnp.int32)
    weight = jnp.zeros((SUBLANES, LANES), jnp.float32)
    picks = [[blank, blank], [blank, blank]]
    border = held = blank
    for x in range(rows):
        level = (frac_ref[x].astype(jnp.float32) + 0.5) / FRAC
        weight = jnp.where(row == x, level, weight)
        here = row % rows == x
        for i, target in enumerate((part ^ 1, part)):
            upper, lower, rest = row_sources(shift_ref[x], own, cells, peers, target)
            first = ((upper ^ part) & 1) == 0
            block = (jnp.where(first, upper, lower) ^ part) >> 1
            block = jnp.where((part & 1) == 1, partner_order(block, peers // 2), block)
            amount = jnp.where(first, rest, rest + spare)
            picks[i] = [jnp.where(here, a, b) for a, b in zip((block, amount), picks[i])]
            if target is part:
                border = jnp.where(here, rest, border)
                held = jnp.where(here, jnp.where(first, 1, 0), held)
    weight_ref[...] = weight
    for i in range(2):
        for k in range(2):
            pick_ref[i, k] = picks[i][k]
    border_ref[0] = border
    border_ref[1] = held
    for f in range(FIELDS):
        for t, tile in enumerate(block_tiles(state_ref, f, cells)):
            out_ref[f, t] = turn_lanes(tile, cells % LANES)


def pair_kernel(cells, peers, rows, shear_ref, upper_ref, below_ref, joined_ref, up_ref, down_ref):
    place = lax.axis_index("gx")
    places = lax.axis_size("gx")
    own, up, down, _, _ = plan(shear_ref[0], cells, peers)
    up = jnp.where(place == places - 1, up, own)
    down = jnp.where(place == 0, down, own)
    lane = lane_index()
    row = row_index()
    single = tiles_for(cells)
    gap = cells % LANES
    window = single + 1
    for f in range(FIELDS):
        lower = block_tiles(below_ref, f, cells)
        upper = [upper_ref[f, t] for t in range(single)]
        for i in range(single - 1):
            joined_ref[f, i] = lower[i]
        joined_ref[f, single - 1] = jnp.where(lane < gap, lower[-1], upper[0])
        for k in range(single):
            following = upper[min(k + 1, single - 1)]
            joined_ref[f, single + k] = jnp.where(lane < gap, upper[k], following)

    late = row % rows >= SENT
    pairs = FIELDS // 2
    up_tail = down_tail = jnp.zeros((SUBLANES, LANES), jnp.float32)

    def tail(tile, index, so_far):
        return jnp.where(lane // TAIL == index, turn_lanes(tile, index * TAIL), so_far)

    for pair in range(pairs):
        ups = [cut_window(joined_ref, 2 * pair + i, up, window) for i in range(2)]
        downs = [cut_window(joined_ref, 2 * pair + i, down, window) for i in range(2)]
        ups = [jnp.where(late, a, turn_rows(b, -SENT)) for a, b in zip(*ups)]
        downs = [jnp.where(late, turn_rows(b, SENT), a) for a, b in zip(*downs)]
        for t in range(single):
            up_ref[pair * single + t] = ups[t]
            down_ref[pair * single + t] = downs[t]
        up_tail = tail(ups[single], pair, up_tail)
        down_tail = tail(downs[single], pair, down_tail)
    faces = jnp.zeros((SUBLANES, LANES), jnp.float32)
    tiles = cut_window(joined_ref, FACE_X, down, window)
    for t in range(single):
        for z in range(PLANES):
            at = t * PLANES + z
            faces = jnp.where(row == at, turn_rows(tiles[t], at - (z * rows + SENT)), faces)
    down_ref[pairs * single] = faces
    up_ref[pairs * single] = up_tail
    down_ref[pairs * single + 1] = tail(tiles[single], pairs, down_tail)


def cut_window(joined_ref, f, start, count):
    whole = start >> LANE_BITS
    part = start & (LANES - 1)
    last = joined_ref.shape[1] - 1
    tiles = [joined_ref[f, jnp.minimum(whole + t, last)] for t in range(count + 1)]
    turned = [turn_lanes(tile, (LANES - part) & (LANES - 1)) for tile in tiles]
    here = lane_index() < LANES - part
    return [jnp.where(here, turned[t], turned[t + 1]) for t in range(count)]


def cell_terms(state, next_face_x, next_face_y):
    planes = range(PLANES)
    face_z = state[7]
    out = []
    for z in planes:
        density, mom_x, mom_y, mom_z, energy, face_x, face_y = (state[f][z] for f in range(7))
        cen_x = 0.5 * (face_x + next_face_x[z])
        cen_y = 0.5 * (face_y + next_face_y[z])
        cen_z = 0.5 * (face_z[z] + face_z[(z + 1) % PLANES])
        inverse = 1.0 / density
        vel_x, vel_y, vel_z = (mom_x * inverse, mom_y * inverse, mom_z * inverse)
        magnetic = 0.5 * (cen_x * cen_x + cen_y * cen_y + cen_z * cen_z)
        kinetic = 0.5 * (mom_x * vel_x + mom_y * vel_y + mom_z * vel_z)
        pressure = (ADIABATIC - 1.0) * (energy - kinetic - magnetic) + magnetic
        vel_dot = vel_x * cen_x + vel_y * cen_y + vel_z * cen_z
        scaled_p = HALF_STEP * pressure
        total = energy + pressure
        sv_x, sv_y, sv_z = (HALF_STEP * vel_x, HALF_STEP * vel_y, HALF_STEP * vel_z)
        sb_x, sb_y, sb_z = (HALF_STEP * cen_x, HALF_STEP * cen_y, HALF_STEP * cen_z)
        xx = mom_x * sv_x - cen_x * sb_x + scaled_p
        yy = mom_y * sv_y - cen_y * sb_y + scaled_p
        zz = mom_z * sv_z - cen_z * sb_z + scaled_p
        xy = mom_x * sv_y - cen_x * sb_y
        xz = mom_x * sv_z - cen_x * sb_z
        yz = mom_y * sv_z - cen_y * sb_z
        diffuse = [DIFFUSE * state[f][z] for f in range(5)]
        flux_x = [HALF_STEP * mom_x, xx, xy, xz, total * sv_x - sb_x * vel_dot]
        flux_y = [HALF_STEP * mom_y, xy, yy, yz, total * sv_y - sb_y * vel_dot]
        flux_z = [HALF_STEP * mom_z, xz, yz, zz, total * sv_z - sb_z * vel_dot]
        e_z = EDGE * (vel_y * cen_x - vel_x * cen_y)
        pair = e_z + radial_prev(e_z)
        out.append(
            dict(
                diffuse=diffuse,
                along_x=[
                    radial_next(f - d) - radial_prev(f + d) for f, d in zip(flux_x, diffuse)
                ],
                low_y=[turn_lanes(f + d, 1) for f, d in zip(flux_y, diffuse)],
                high_y=[turn_lanes(f - d, LANES - 1) for f, d in zip(flux_y, diffuse)],
                flux_z=flux_z,
                shear=xy,
                e_x=EDGE * (vel_z * cen_y - vel_y * cen_z),
                e_y=EDGE * (vel_x * cen_z - vel_z * cen_x),
                pair=pair,
                low_pair=turn_lanes(pair, 1),
                high_pair=turn_lanes(pair, LANES - 1),
            )
        )
    e_x, e_y = (
        [sum((cell[name] for cell in out[1:]), out[0][name]) for name in ("e_x", "e_y")]
    )
    shared = dict(
        e_x=e_x,
        low_e_x=turn_lanes(e_x, 1),
        high_e_x=turn_lanes(e_x, LANES - 1),
        edge_y=[e_y + radial_prev(e_y)] * PLANES,
        along_x=radial_next(e_y) - radial_prev(e_y),
    )
    return out, shared


def tile_step(state, low, here, high):
    lane = lane_index()
    cells_low, shared_low = low
    cells, shared = here
    cells_high, shared_high = high

    def before(turned_low, turned):
        return jnp.where(lane > 0, turned, turned_low)

    def after(turned, turned_high):
        return jnp.where(lane < LANES - 1, turned, turned_high)

    new = [[None] * PLANES for f in range(FIELDS)]
    faces = [
        [
            (cells[z - 1]["flux_z"][f] + cells[z]["flux_z"][f])
            - (cells[z]["diffuse"][f] - cells[z - 1]["diffuse"][f])
            for f in range(5)
        ]
        for z in range(PLANES)
    ]
    low_e_x = before(shared_low["low_e_x"], shared["low_e_x"])
    along_y = after(shared["high_e_x"], shared_high["high_e_x"]) - low_e_x
    edge_x = [shared["e_x"] + low_e_x] * PLANES
    edge_y = shared["edge_y"]
    for z in range(PLANES):
        cell = cells[z]
        up = (z + 1) % PLANES
        for f in range(5):
            high_y = after(cell["high_y"][f], cells_high[z]["high_y"][f])
            low_y = before(cells_low[z]["low_y"][f], cell["low_y"][f])
            along_z = faces[up][f] - faces[z][f]
            kept = state[f][z] - 4.0 * cell["diffuse"][f]
            new[f][z] = kept - (cell["along_x"][f] + (high_y - low_y) + along_z)
        mom_x, mom_y = (state[1][z], state[2][z])
        new[1][z] = new[1][z] + (TIME_STEP * 2.0 * ROTATION) * mom_y
        new[2][z] = new[2][z] - (TIME_STEP * (2.0 - SHEAR_RATE) * ROTATION) * mom_x
        new[4][z] = new[4][z] + (2.0 * SHEAR_RATE * ROTATION) * cell["shear"]
        low_pair = before(cells_low[z]["low_pair"], cell["low_pair"])
        high_pair = after(cell["high_pair"], cells_high[z]["high_pair"])
        edge_z = cell["pair"] + low_pair
        new[5][z] = state[5][z] + ((edge_y[up] - edge_y[z]) - (high_pair - low_pair))
        new[6][z] = state[6][z] + ((radial_next(edge_z) - edge_z) - (edge_x[up] - edge_x[z]))
        new[7][z] = state[7][z] + (along_y - shared["along_x"])
    return new


def step_kernel(
    cells, peers, rows,
    shear_ref, weight_ref, joined_ref, up_hbm, down_hbm,
    out_ref, state_ref, mid_ref, up_ref, down_ref, up_sem, down_sem,
):
    up_copy = pltpu.make_async_copy(up_hbm, up_ref, up_sem)
    down_copy = pltpu.make_async_copy(down_hbm, down_ref, down_sem)
    up_copy.start()
    down_copy.start()
    own = plan(shear_ref[0], cells, peers)[0]
    lane = lane_index()
    row = row_index()
    single = tiles_for(cells)
    window = single + 1
    pairs = FIELDS // 2

    for f in range(FIELDS):
        for t, tile in enumerate(cut_window(joined_ref, f, own, window)):
            for z in range(PLANES):
                state_ref[t, f, z] = turn_rows(tile, -z * rows)
    up_copy.wait()
    down_copy.wait()
    for f in range(FIELDS):
        pair, second = divmod(f, 2)
        for t in range(window):
            if t < single:
                up = up_ref[pair * single + t]
                down = down_ref[pair * single + t]
            else:
                back = (LANES - pair * TAIL) % LANES
                up = turn_lanes(up_ref[pairs * single], back)
                down = turn_lanes(down_ref[pairs * single + 1], back)
            for z in range(PLANES):
                up_at = z * rows + (0 if second else SENT)
                down_at = z * rows + (SENT if second else 0)
                value = state_ref[t, f, z]
                value = jnp.where(row < rows, value, turn_rows(down, rows - down_at))
                value = jnp.where(row < rows + SENT, value, turn_rows(up, rows + SENT - up_at))
                state_ref[t, f, z] = value
    last = rows + SENT - 1

    def faces_beyond(t, face_x):
        if t < single:
            beyond = [turn_rows(down_ref[pairs * single], last - t * PLANES - z) for z in range(PLANES)]
        else:
            tile = turn_lanes(down_ref[pairs * single + 1], LANES - pairs * TAIL)
            beyond = [turn_rows(tile, last - (z * rows + SENT)) for z in range(PLANES)]
        return [jnp.where(row == last, b, radial_next(face)) for b, face in zip(beyond, face_x)]

    def terms(ref, t, count, beyond):
        state = [[ref[t, f, z] for z in range(PLANES)] for f in range(FIELDS)]
        if beyond:
            next_face_x = faces_beyond(t, state[FACE_X])
        else:
            next_face_x = [radial_next(face) for face in state[FACE_X]]
        next_face_y = []
        for z in range(PLANES):
            here = turn_lanes(state[6][z], LANES - 1)
            if t + 1 < count:
                there = turn_lanes(ref[t + 1, 6, z], LANES - 1)
                here = jnp.where(lane < LANES - 1, here, there)
            next_face_y.append(here)
        return state, cell_terms(state, next_face_x, next_face_y)

    low = here = terms(state_ref, 0, window, True)
    for t in range(window):
        high = terms(state_ref, t + 1, window, True) if t + 1 < window else here
        new = tile_step(here[0], low[1], here[1], high[1])
        for f in range(FIELDS):
            for z in range(PLANES):
                if t < single or f == 6:
                    mid_ref[t, f, z] = new[f][z]
        low, here = here, high

    weight = weight_ref[...]
    keep = 1.0 - weight
    low = here = terms(mid_ref, 0, window, False)
    low_done = None
    low_moved = None

    def emit(t, moved):
        for f in range(FIELDS):
            out_ref[f, t] = moved[f]

    for t in range(single):
        high = terms(mid_ref, t + 1, window, False) if t + 1 < single else here
        new = tile_step(here[0], low[1], here[1], high[1])
        done = []
        moved = []
        for f in range(FIELDS):
            mixed = []
            turned = []
            for z in range(PLANES):
                value = 0.5 * (state_ref[t, f, z] + new[f][z])
                below = turn_lanes(value, 1)
                turned.append(below)
                if t:
                    below = jnp.where(lane > 0, below, low_done[f][z])
                mixed.append(keep * value + weight * below)
            done.append(turned)
            both = jnp.where(row < rows, mixed[0], turn_rows(mixed[1], rows))
            moved.append(turn_lanes(both, LANES - BELOW))
        if t:
            emit(
                t - 1,
                [jnp.where(lane < LANES - BELOW, a, b) for a, b in zip(low_moved, moved)],
            )
        low_done, low_moved = done, moved
        low, here = here, high
    emit(single - 1, low_moved)


def partner_order(offset, chips):
    bits = chips.bit_length() - 1
    return sum(((offset >> b) & 1) << (bits - 1 - b) for b in range(bits))


def row_sources(shift, own, cells, peers, target):
    shift = shift - (cells - BELOW - own)
    shift = jnp.where(shift < 0, shift + cells * peers, shift)
    hops, rest = hops_of(shift, cells, peers)
    upper = (target + peers - hops) & (peers - 1)
    lower = (target + peers - 1 - hops) & (peers - 1)
    return upper, lower, rest


def pick_kernel(target, pick_ref, *refs):
    in_refs, out_ref = (refs[:-1], refs[-1])
    count = out_ref.shape[1]
    block = pick_ref[target, 0]
    amount = pick_ref[target, 1]
    lane = lane_index()
    fine = amount & (LANES - 1)
    source = (lane - fine) & (LANES - 1)
    chosen = [block == i for i in range(len(in_refs))]
    for f in range(FIELDS):
        tiles = [in_refs[0][f, t] for t in range(count)]
        for mask, ref in zip(chosen[1:], in_refs[1:]):
            tiles = [jnp.where(mask, ref[f, t], tiles[t]) for t in range(count)]
        step = 1
        while step < count:
            moves = (amount & (step * LANES)) != 0
            tiles = [jnp.where(moves, tiles[(t - step) % count], tiles[t]) for t in range(count)]
            step *= 2
        tiles = [
            jnp.take_along_axis(tile, source, axis=1, mode="promise_in_bounds") for tile in tiles
        ]
        for t in range(count):
            out_ref[f, t] = jnp.where(lane < fine, tiles[t - 1], tiles[t])


def merge_kernel(cells, rows, border_ref, mine_ref, other_ref, out_hbm, out_ref, out_sem):
    count = mine_ref.shape[1]
    border = border_ref[0]
    held = border_ref[1] == 1
    masks = [(lane_index() + t * LANES >= border) == held for t in range(count)]
    for f in range(FIELDS):
        tiles = [jnp.where(masks[t], mine_ref[f, t], other_ref[f, t]) for t in range(count)]
        value = jnp.concatenate(tiles, axis=1)[:, :cells]
        for z in range(PLANES):
            out_ref[f, z] = value[z * rows : (z + 1) * rows]
        pltpu.make_async_copy(out_ref.at[f], out_hbm.at[f], out_sem.at[f]).start()
    for f in range(FIELDS):
        pltpu.make_async_copy(out_ref.at[f], out_hbm.at[f], out_sem.at[f]).wait()


def solution(mesh):
    places, peers = (mesh.shape["gx"], mesh.shape["gy"])
    smem = pl.BlockSpec(memory_space=pltpu.SMEM)
    vmem = pl.BlockSpec(memory_space=pltpu.VMEM)
    hbm = pl.BlockSpec(memory_space=pltpu.HBM)
    params = pltpu.CompilerParams(vmem_limit_bytes=8 * 2**20)
    axes = ("gx", "gy")

    def array(*shape):
        return jax.ShapeDtypeStruct(shape + (SUBLANES, LANES), jnp.float32)

    def scratch(*shape):
        return pltpu.VMEM(shape + (SUBLANES, LANES), jnp.float32)

    def device(x, y):
        return x % places * peers + y % peers

    devices = [(x, y) for x in range(places) for y in range(peers)]

    def ghosts(up_hop, down_hop, up, down):
        rise = [(device(x, y), device(x + 1, y + up_hop * (x == places - 1))) for x, y in devices]
        fall = [(device(x, y), device(x - 1, y - down_hop * (x == 0))) for x, y in devices]
        up = lax.ppermute(up, axes, rise)
        return up, lax.ppermute(down, axes, fall)

    def shards(state, shear_offset, remap_shift, frac_index):
        rows, cells = state.shape[2:]
        single = tiles_for(cells)
        double = tiles_for(2 * cells)
        window = tiles_for(BELOW + cells + ABOVE)
        below = lax.ppermute(state, "gy", [(i, (i + 1) % peers) for i in range(peers)])
        numbers = lambda *shape: jax.ShapeDtypeStruct(shape + (SUBLANES, LANES), jnp.int32)
        upper, weight, pick, border = pl.pallas_call(
            lambda *refs: lay_kernel(cells, peers, *refs),
            out_shape=[array(FIELDS, single), array(), numbers(2, 2), numbers(2)],
            in_specs=[smem] * 3 + [vmem],
            out_specs=[vmem] * 4,
            compiler_params=params,
            name="lay",
        )(shear_offset, remap_shift, frac_index, state)
        edge = FIELDS // 2 * single + 2
        joined, up, down = pl.pallas_call(
            lambda *refs: pair_kernel(cells, peers, rows, *refs),
            out_shape=[array(FIELDS, double), array(edge), array(edge)],
            in_specs=[smem, vmem, vmem],
            out_specs=[vmem] * 3,
            compiler_params=params,
            name="pair",
        )(shear_offset, upper, below)
        _, _, _, up_hop, down_hop = plan(shear_offset[0], cells, peers)
        branches = [
            lambda u, d, i=i: ghosts(i // 2 + i % 2, i // 2, u, d) for i in range(2 * peers)
        ]
        which = (down_hop + up_hop) & (2 * peers - 1)
        up, down = lax.switch(which, branches, up, down)
        block = pl.pallas_call(
            lambda *refs: step_kernel(cells, peers, rows, *refs),
            out_shape=array(FIELDS, single),
            in_specs=[smem] + [vmem] * 2 + [hbm] * 2,
            out_specs=vmem,
            scratch_shapes=[scratch(window, FIELDS, PLANES)] * 2
            + [scratch(edge), scratch(edge)]
            + [pltpu.SemaphoreType.DMA] * 2,
            compiler_params=params,
            name="step",
        )(shear_offset, weight, joined, up, down)

        def exchange(value, bits):
            return lax.ppermute(value, "gy", [(i, i ^ bits) for i in range(peers)])

        def across(offset):
            offsets = (offset, partner_order(offset, peers // 2))
            return lax.ppermute(block, "gy", [(i, i ^ (2 * offsets[i % 2])) for i in range(peers)])

        blocks = [block] + [across(offset) for offset in range(1, peers // 2)]

        def picked(target, name):
            return pl.pallas_call(
                lambda *refs: pick_kernel(target, *refs),
                out_shape=array(FIELDS, single),
                in_specs=[vmem] * (1 + peers // 2),
                out_specs=vmem,
                compiler_params=params,
                name=name,
            )(pick, *blocks)

        other = exchange(picked(0, "gather"), 1)
        mine = picked(1, "keep")
        return pl.pallas_call(
            lambda *refs: merge_kernel(cells, rows, *refs),
            out_shape=jax.ShapeDtypeStruct(state.shape, jnp.float32),
            in_specs=[vmem] * 3,
            out_specs=hbm,
            scratch_shapes=[
                pltpu.VMEM(state.shape, jnp.float32),
                pltpu.SemaphoreType.DMA((FIELDS,)),
            ],
            compiler_params=params,
            name="merge",
        )(border, mine, other)

    placed = (P(None, None, "gx", "gy"), P(), P("gx"), P("gx"))
    return jax.shard_map(
        shards, mesh=mesh, in_specs=placed, out_specs=P(None, None, "gx", "gy"), check_vma=False
    )
```
